128 devices in a mesh: section: 2 (over x_lo), dp: 4 (over z), expert: 16 (over x_hi, y, core).
Axes of the slice: x: 4 (x_hi: 2, x_lo: 2; x = x_hi * 2 + x_lo), y: 4, z: 4, core: 2. Of those that a mesh axis runs over, the one named last changes fastest.
Arguments:
- states: bfloat16 [2, 8192, 2048], P('section', ('dp', 'expert')), may hold values from -6 to 6
- routes: int32 [2, 8192, 2], P('section', ('dp', 'expert')), may hold values from 0 to 15, all different within a row; in each aligned block of 128 rows (0 to 127, 128 to 255, ..., all dimensions but the last counted through in order) at most 20 rows name the same one
- lengths: int32 [2, 64], P(None, ('dp', 'expert')), may hold values from 32 to 128
- router: bfloat16 [2, 2048, 16], P('section'), may hold values from -0.125 to 0.125
- w_in: bfloat16 [2, 16, 2048, 4096], P('section', 'expert', None, 'dp'), may hold values from -0.125 to 0.125
- w_out: bfloat16 [2, 16, 4096, 2048], P('section', 'expert', 'dp'), may hold values from -0.09375 to 0.09375
- w_query: bfloat16 [2048, 1024], P(('dp', 'expert')), may hold values from -4 to 4
- w_key: bfloat16 [2048, 1024], P(('dp', 'expert')), may hold values from -0.125 to 0.125
- w_value: bfloat16 [2048, 1024], P(('dp', 'expert')), may hold values from -0.125 to 0.125
- w_output: bfloat16 [1024, 2048], P(('dp', 'expert')), may hold values from -0.1875 to 0.1875
- cotangent: bfloat16 [2, 8192, 2048], P('section', ('dp', 'expert')), may hold values from -6 to 6
Outputs:
- forward_out: bfloat16 [2, 8192, 2048], P('section', ('dp', 'expert'))
- grads: float32 [2, 8192, 2048], P('section', ('dp', 'expert'))
The draws below stay inside these ranges and needn't reach their ends.
Inputs may be any that keep to these rules, and one draw needn't show every extreme that they name: In the rows of one device no expert is named by more than 20 tokens, and in every draw some device names some expert exactly 20 times; the two routes of a token differ.
All inputs are finite; a program needn't handle non-finite values.
Results may differ from the reference program's by a relative error of at most 0.02.
The reference program's roundings to bfloat16 on the way count: a program that leaves them out, or rounds other values in their place, can miss the bound.
Values may be sent and summed in bfloat16 or wider, within the bound.
No kernel may reach another device: no remote copies, remote signals or barrier semaphores. Data moves between devices by JAX's collectives and lax.ppermute only.
A program may use at most 192 MiB of HBM per device.

```python
import math
from functools import partial
import jax
import jax.numpy as jnp
import numpy as np
from jax import lax

D = 2048
FF = 4096
HEADS = 8
HEAD = 128
TOP = 2
LEN = 128
TOK_DEV = 128
EXPERTS = 16
CAP = 20
SEQS = 64
TOKENS = 8192
N_DP = 4
N_EXPERT = 16


def draw_w_query(key, part):
    key = jax.random.fold_in(key, 7)
    values_drawn = jax.random.normal(key, (D, HEADS * HEAD), jnp.float32) * D ** (-0.5)
    return jnp.clip(values_drawn, -4.0, 4.0).astype(jnp.bfloat16)


def touch_ends(values, stream_key, low, top_value):
    extent = values.shape
    place = [jax.random.randint(jax.random.fold_in(stream_key, axis), (), 0, extent[axis]) for axis in range(len(extent))]
    values = values.at[tuple(place)].set(low)
    longest = extent.index(max(extent))
    place[longest] = (place[longest] + 1) % extent[longest]
    return values.at[tuple(place)].set(top_value)


def level_of(key, dims, cuts, smallest, top_value):
    factor_of, own = 1.0, jax.random.fold_in(key, 6)
    for dim, shards_of in cuts:
        draws = jnp.exp(jax.random.uniform(jax.random.fold_in(own, dim), (shards_of,), jnp.float32, smallest / len(cuts), top_value / len(cuts)))
        factor_of = factor_of * jnp.repeat(draws, dims[dim] // shards_of).reshape([-1 if axis == dim else 1 for axis in range(len(dims))])
    return factor_of


def deal_out(rng, own, number, rows, count, top, most, lean):
    order = jax.random.permutation(rng, count)
    packed, common = shares(count, rows * top, most, lean, True), shares(count, rows * top, most, lean, False)
    places = jnp.arange(count)

    def named(tallies, rotation):
        used = int((tallies > 0).sum())
        fixed = max(1, used // 4)
        shifted = fixed + (places - fixed + rotation * (used - fixed)) % max(1, count - fixed)
        return jnp.zeros((count,), jnp.int32).at[order[jnp.where(places < fixed, places, shifted)]].set(jnp.asarray(tallies, jnp.int32))

    tallies = jnp.where(number % 4 == 0, named(packed, number // 4), named(common, number - number // 4 - 1))
    mixed = jax.random.permutation(jax.random.fold_in(own, 3), count)
    giver, receiver = mixed[0:count // 2 * 2:2], mixed[1:count // 2 * 2:2]
    margin = jnp.minimum(tallies[giver] - 1, most - tallies[receiver]) // 2
    margin = jnp.where((giver == order[0]) | (receiver == order[0]) | (tallies[receiver] == 0), 0, jnp.maximum(margin, 0))
    shifted = jax.random.randint(jax.random.fold_in(own, 4), (count // 2,), 0, 1 << 20) % (margin + 1)
    tallies = tallies.at[giver].add(-shifted).at[receiver].add(shifted)
    items = jnp.searchsorted(jnp.cumsum(tallies), jnp.arange(rows * top), side="right").astype(jnp.int32)
    grid = items.reshape(top, rows).T
    grid = grid[jax.random.permutation(jax.random.fold_in(own, 1), rows)]
    rotation = jax.random.randint(jax.random.fold_in(own, 2), (rows, 1), 0, top)
    return jnp.take_along_axis(grid, (jnp.arange(top)[None, :] + rotation) % top, axis=1)


def shares(count, total, most, slope, full):
    portions = [(1 << 20) // math.isqrt(rank ** slope) + 1 for rank in range(1, count + 1)]
    largest = most if full else min(most, max(-(-total // count), total * portions[0] // sum(portions)))
    least = 1 if total - largest >= count - 1 else 0
    counts, surplus = [largest] + [least] * (count - 1), total - largest - least * (count - 1)
    while surplus > 0:
        candidates = [i for i in range(1, count) if counts[i] < largest] or [i for i in range(1, count) if counts[i] < most]
        whole, budget = sum([portions[i] for i in candidates]), surplus
        for i in candidates:
            more = min(most - counts[i], max(1, budget * portions[i] // whole), surplus)
            counts[i] = counts[i] + more
            surplus = surplus - more
    return np.array(counts)


def scatter_about(rng, dims, spread, most, split=(), held_as=jnp.bfloat16):
    values = jax.random.normal(rng, dims, jnp.float32) * spread
    if len(split) > 0:
        values = level_of(rng, dims, split, -0.22, 0.18) * values
    return jnp.clip(values, min=-most, max=most).astype(held_as)


def setup_inputs(seed: int = 0) -> dict:
    seeds = jax.random.split(jax.random.key(seed), 12)
    states = scatter_about(seeds[0], (2, TOKENS, D), 1.0, 6.0, ((0, 2), (1, 64)))
    routes_keys = jax.random.split(jax.random.fold_in(seeds[1], 1), 2 * TOKENS // TOK_DEV)
    routes_turns = jax.random.permutation(jax.random.fold_in(seeds[1], 3), 2 * TOKENS // TOK_DEV)
    routes = jax.vmap(lambda own, number: deal_out(jax.random.fold_in(seeds[1], 2), own, number, TOK_DEV, EXPERTS, TOP, CAP, 2))(routes_keys, routes_turns).reshape((2, TOKENS, TOP))
    lengths = touch_ends(jax.random.randint(seeds[2], (2, SEQS), LEN // 4, LEN + 1), jax.random.fold_in(seeds[2], 1), LEN // 4, LEN).astype(jnp.int32)
    router = scatter_about(seeds[3], (2, D, EXPERTS), D ** -0.5, 0.125, ((0, 2),))
    w_in = scatter_about(seeds[4], (2, EXPERTS, D, FF), D ** -0.5, 0.125, ((0, 2), (1, 16), (3, 4)))
    w_out = scatter_about(seeds[5], (2, EXPERTS, FF, D), FF ** -0.5, 0.09375, ((0, 2), (1, 16), (2, 4)))
    w_query = draw_w_query(jax.random.fold_in(seeds[11], 71), 0)
    w_key = scatter_about(seeds[7], (D, HEADS * HEAD), D ** -0.5, 0.125, ((0, 64),))
    w_value = scatter_about(seeds[8], (D, HEADS * HEAD), D ** -0.5, 0.125, ((0, 64),))
    w_output = scatter_about(seeds[9], (HEADS * HEAD, D), (HEADS * HEAD) ** -0.5, 0.1875, ((0, 64),))
    cotangent = scatter_about(seeds[10], (2, TOKENS, D), 1.0, 6.0, ((0, 2), (1, 64)))
    return dict(states=states, routes=routes, lengths=lengths, router=router, w_in=w_in, w_out=w_out, w_query=w_query, w_key=w_key, w_value=w_value, w_output=w_output, cotangent=cotangent)


EPS = 1e-05
NEG_FILL = -1e+30

def layer_norm(values):
    centred = values - lax.optimization_barrier(jnp.mean(values, axis=-1, keepdims=True))
    variance = lax.optimization_barrier(jnp.mean(centred * centred, axis=-1, keepdims=True))
    return centred * lax.rsqrt(variance + EPS)

def norm_back(values, upstream):
    centred = values - lax.optimization_barrier(jnp.mean(values, axis=-1, keepdims=True))
    variance = lax.optimization_barrier(jnp.mean(centred * centred, axis=-1, keepdims=True))
    inverse = lax.rsqrt(variance + EPS)
    normed = centred * inverse
    return inverse * (upstream - lax.optimization_barrier(jnp.mean(upstream, axis=-1, keepdims=True)) - normed * lax.optimization_barrier(jnp.mean(upstream * normed, axis=-1, keepdims=True)))

def slot_tables(routes, experts, capacity):
    assigned = routes.reshape(-1)
    number = assigned.shape[0]
    onehot = (assigned[:, None] == jnp.arange(experts, dtype=jnp.int32)[None, :]).astype(jnp.int32)
    ranking = jnp.cumsum(onehot, axis=0) - 1
    position = lax.optimization_barrier(jnp.sum(onehot * ranking, axis=1))
    target = assigned * capacity + position
    matches = (target[:, None] == jnp.arange(experts * capacity, dtype=jnp.int32)[None, :]).astype(jnp.int32)
    source = lax.optimization_barrier(jnp.sum(matches * jnp.arange(number, dtype=jnp.int32)[:, None], axis=0))
    filled = lax.optimization_barrier(jnp.sum(matches, axis=0))
    return (target, source, filled)

def gate_values(normed, routes, router):
    logits = jnp.dot(normed, router, preferred_element_type=jnp.float32)
    expert_ids = jnp.arange(router.shape[1], dtype=jnp.int32)
    first_hot = (routes[:, 0:1] == expert_ids[None, :]).astype(jnp.float32)
    second_hot = (routes[:, 1:2] == expert_ids[None, :]).astype(jnp.float32)
    sign_hot = first_hot - second_hot
    spread_logit = lax.optimization_barrier(jnp.sum(logits * sign_hot, axis=1))
    return (jax.nn.sigmoid(spread_logit), sign_hot)

def pick_rows(rows_dev, indices, filled):
    return jnp.where(filled[:, None] > 0, jnp.take(rows_dev, indices, axis=0), jnp.zeros((), rows_dev.dtype))

def take_rows(table_rows, indices):
    return jnp.take(table_rows, indices, axis=0)

def to_expert_major(outgoing):
    groups = outgoing.shape[0]
    return outgoing.reshape(groups, EXPERTS, CAP, D).transpose(1, 0, 2, 3).reshape(EXPERTS, groups * CAP, D)

def to_device_major(per_expert):
    groups = per_expert.shape[1] // CAP
    return per_expert.reshape(EXPERTS, groups, CAP, D).transpose(1, 0, 2, 3).reshape(groups, EXPERTS * CAP, D)

def expert_forward_item(operands):
    rows_in, w_first, w_second = operands
    pre_active = jnp.dot(rows_in, w_first, preferred_element_type=jnp.float32)
    active = jnp.maximum(pre_active, 0.0).astype(jnp.bfloat16)
    return jnp.dot(active, w_second, preferred_element_type=jnp.float32).astype(jnp.bfloat16)

def expert_backward_item(operands):
    rows_in, grad_rows, w_first, w_second = operands
    pre_active = jnp.dot(rows_in, w_first, preferred_element_type=jnp.float32)
    hidden_grad = jnp.dot(grad_rows, w_second.T, preferred_element_type=jnp.float32)
    hidden_grad = jnp.where(pre_active > 0, hidden_grad, 0.0).astype(jnp.bfloat16)
    return jnp.dot(hidden_grad, w_first.T, preferred_element_type=jnp.float32).astype(jnp.bfloat16)

def moe_forward(states, routes, router, w_in, w_out):
    groups = N_DP * N_EXPERT
    normed = layer_norm(states.astype(jnp.float32)).astype(jnp.bfloat16)
    gate_first, sign_hot = gate_values(normed, routes, router)
    target, source, filled = jax.vmap(partial(slot_tables, experts=EXPERTS, capacity=CAP))(routes.reshape(groups, TOK_DEV, TOP))
    outgoing = jax.vmap(pick_rows)(normed.reshape(groups, TOK_DEV, D), source // TOP, filled)
    expert_rows = to_expert_major(outgoing)
    outputs = lax.map(expert_forward_item, (expert_rows, w_in, w_out))
    returned = to_device_major(outputs)
    picked = jax.vmap(take_rows)(returned, target).reshape(groups * TOK_DEV, TOP, D).astype(jnp.float32)
    mixing = jnp.stack([gate_first, 1.0 - gate_first], axis=1)
    hidden_state = states.astype(jnp.float32) + (mixing[:, 0:1] * picked[:, 0] + mixing[:, 1:2] * picked[:, 1])
    return (hidden_state, (gate_first, sign_hot, target, source, filled, expert_rows, picked))

def moe_backward(states, upstream, router, w_in, w_out, saved):
    gate_first, sign_hot, target, source, filled, expert_rows, picked = saved
    groups = N_DP * N_EXPERT
    mixing = jnp.stack([gate_first, 1.0 - gate_first], axis=1)
    slot_grad = (mixing[:, :, None] * upstream[:, None, :]).astype(jnp.bfloat16).reshape(groups, TOK_DEV * TOP, D)
    outgoing = jax.vmap(pick_rows)(slot_grad, source, filled)
    grad_rows = to_expert_major(outgoing)
    backward_rows = lax.map(expert_backward_item, (expert_rows, grad_rows, w_in, w_out))
    returned = to_device_major(backward_rows)
    back_picked = jax.vmap(take_rows)(returned, target).reshape(groups * TOK_DEV, TOP, D).astype(jnp.float32)
    gate_grad = lax.optimization_barrier(jnp.sum(upstream * (picked[:, 0] - picked[:, 1]), axis=1))
    logit_grad = gate_grad * gate_first * (1.0 - gate_first)
    router_term = jnp.dot(logit_grad[:, None] * sign_hot, router.astype(jnp.float32).T, precision=lax.Precision.HIGHEST)
    normed_grad = back_picked[:, 0] + back_picked[:, 1] + router_term
    return upstream + norm_back(states.astype(jnp.float32), normed_grad)

def cross_forward(normed_rows, memory_rows, key_mask, w_query, w_key, w_value, w_output):
    sequences = key_mask.shape[0]
    score_scale = HEAD ** (-0.5)

    def project(row_block, weight):
        return jnp.dot(row_block, weight, preferred_element_type=jnp.float32).astype(jnp.bfloat16).reshape(sequences, LEN, HEADS, HEAD)
    queries = project(normed_rows, w_query)
    key_rows = project(memory_rows, w_key)
    value_rows = project(memory_rows, w_value)
    scores = jnp.einsum('sqhd,skhd->shqk', queries.astype(jnp.float32), key_rows.astype(jnp.float32)) * score_scale
    scores = jnp.where(key_mask[:, None, None, :], scores, NEG_FILL)
    row_top = lax.optimization_barrier(jnp.max(scores, axis=-1, keepdims=True))
    exponent = jnp.exp(scores - row_top)
    attention = exponent / lax.optimization_barrier(jnp.sum(exponent, axis=-1, keepdims=True))
    attention_low = attention.astype(jnp.bfloat16)
    context = jnp.einsum('shqk,skhd->sqhd', attention_low.astype(jnp.float32), value_rows.astype(jnp.float32)).astype(jnp.bfloat16)
    context = context.reshape(sequences * LEN, HEADS * HEAD)
    attended = jnp.dot(context, w_output, preferred_element_type=jnp.float32)
    return (attended, (queries, key_rows, value_rows, attention, attention_low))

def cross_backward(out_grad, saved, w_query, w_key, w_value, w_output):
    queries, key_rows, value_rows, attention, attention_low = saved
    sequences = queries.shape[0]
    score_scale = HEAD ** (-0.5)
    out_low = out_grad.astype(jnp.bfloat16)
    context_grad = jnp.dot(out_low, w_output.T, preferred_element_type=jnp.float32).astype(jnp.bfloat16)
    context_grad = context_grad.reshape(sequences, LEN, HEADS, HEAD).astype(jnp.float32)
    weight_grad = jnp.einsum('sqhd,skhd->shqk', context_grad, value_rows.astype(jnp.float32))
    value_grad = jnp.einsum('shqk,sqhd->skhd', attention_low.astype(jnp.float32), context_grad).astype(jnp.bfloat16)
    score_grad = (attention * (weight_grad - lax.optimization_barrier(jnp.sum(attention * weight_grad, axis=-1, keepdims=True))) * score_scale).astype(jnp.bfloat16)
    score_grad = score_grad.astype(jnp.float32)
    query_grad = jnp.einsum('shqk,skhd->sqhd', score_grad, key_rows.astype(jnp.float32)).astype(jnp.bfloat16)
    key_grad = jnp.einsum('shqk,sqhd->skhd', score_grad, queries.astype(jnp.float32)).astype(jnp.bfloat16)
    width_all = HEADS * HEAD
    normed_grad = jnp.dot(query_grad.reshape(-1, width_all), w_query.T, preferred_element_type=jnp.float32)
    memory_grad = jnp.dot(key_grad.reshape(-1, width_all), w_key.T, preferred_element_type=jnp.float32)
    memory_grad = memory_grad + jnp.dot(value_grad.reshape(-1, width_all), w_value.T, preferred_element_type=jnp.float32)
    return (normed_grad, memory_grad)

def reference(states, routes, lengths, router, w_in, w_out, w_query, w_key, w_value, w_output, cotangent):
    encoder_hidden, encoder_saved = moe_forward(states[0], routes[0], router[0], w_in[0], w_out[0])
    decoder_hidden, decoder_saved = moe_forward(states[1], routes[1], router[1], w_in[1], w_out[1])
    memory = layer_norm(encoder_hidden).astype(jnp.bfloat16)
    decoder_normed = layer_norm(decoder_hidden).astype(jnp.bfloat16)
    positions = jnp.arange(LEN, dtype=jnp.int32)
    source_mask = positions[None, :] < lengths[0][:, None]
    target_mask = positions[None, :] < lengths[1][:, None]
    attended, attend_saved = cross_forward(decoder_normed, memory, source_mask, w_query, w_key, w_value, w_output)
    decoder_out = (decoder_hidden + attended).astype(jnp.bfloat16)
    source_live = source_mask.reshape(-1)[:, None].astype(jnp.float32)
    target_live = target_mask.reshape(-1)[:, None].astype(jnp.float32)
    out_grad = cotangent[1].astype(jnp.float32) * target_live
    query_side, memory_grad = cross_backward(out_grad, attend_saved, w_query, w_key, w_value, w_output)
    decoder_upstream = out_grad + norm_back(decoder_hidden, query_side)
    encoder_upstream = norm_back(encoder_hidden, cotangent[0].astype(jnp.float32) * source_live + memory_grad)
    encoder_grads = moe_backward(states[0], encoder_upstream, router[0], w_in[0], w_out[0], encoder_saved)
    decoder_grads = moe_backward(states[1], decoder_upstream, router[1], w_in[1], w_out[1], decoder_saved)
    return (jnp.stack([memory, decoder_out]), jnp.stack([encoder_grads, decoder_grads]))
```

```python
import functools

import jax
import jax.numpy as jnp
from jax import lax
from jax.experimental import pallas as pl
from jax.experimental.pallas import tpu as pltpu
from jax.sharding import PartitionSpec as P

HEADS = 8
HEAD = 128
TOP = 2
LEN = 128
STRIDE = 32


EPS = 1e-05
NEG_FILL = -1e30
LOW = jnp.bfloat16
WIDE = jnp.float32
VMEM = pl.BlockSpec(memory_space=pltpu.VMEM)
SMEM = pl.BlockSpec(memory_space=pltpu.SMEM)
PARAMS = pltpu.CompilerParams(vmem_limit_bytes=48 * 1024 * 1024)


def dot(a, b):
    return jnp.dot(a, b, preferred_element_type=WIDE)


def dot_nt(a, b):
    return lax.dot_general(a, b, (((1,), (1,)), ((), ())), preferred_element_type=WIDE)


def dot_tn(a, b):
    return lax.dot_general(a, b, (((0,), (0,)), ((), ())), preferred_element_type=WIDE)


def normalised(values):
    centred = values - jnp.mean(values, axis=-1, keepdims=True)
    variance = jnp.mean(centred * centred, axis=-1, keepdims=True)
    inverse = lax.rsqrt(variance + EPS)
    return centred * inverse, inverse


def norm_back(values, upstream):
    normed, inverse = normalised(values)
    return inverse * (
        upstream
        - jnp.mean(upstream, axis=-1, keepdims=True)
        - normed * jnp.mean(upstream * normed, axis=-1, keepdims=True)
    )


def route_hots(routes, experts):
    ids = lax.broadcasted_iota(jnp.int32, (routes.shape[0], experts), 1)
    return routes[:, 0:1] == ids, routes[:, 1:2] == ids


def spread_rows(rows, first_ref, second_ref):
    experts, capacity, columns = first_ref.shape
    for e in range(experts):
        block = rows[e * STRIDE : e * STRIDE + capacity]
        first_ref[e] = block[:, :columns].astype(LOW)
        second_ref[e] = block[:, columns:].astype(LOW)


def pack_rows(first_ref, second_ref, packed):
    experts, capacity, columns = first_ref.shape
    packed[...] = jnp.zeros_like(packed)
    for e in range(experts):
        packed[pl.ds(e * STRIDE, capacity), pl.ds(0, columns)] = first_ref[e]
        packed[pl.ds(e * STRIDE, capacity), pl.ds(columns, columns)] = second_ref[e]


def dispatch_kernel(states_ref, routes_ref, router_ref, first_ref, second_ref, pick_one_ref, pick_two_ref, gate_ref):
    experts = first_ref.shape[0]
    tokens = states_ref.shape[0]
    normed = normalised(states_ref[...].astype(WIDE))[0].astype(LOW)
    logits = dot(normed, router_ref[...])
    routes = routes_ref[...]
    hot_one, hot_two = route_hots(routes, experts)
    spread = jnp.sum(
        jnp.where(hot_one, logits, 0.0) - jnp.where(hot_two, logits, 0.0), axis=1, keepdims=True
    )
    gate_ref[...] = jax.nn.sigmoid(spread)
    named = jnp.where(hot_one | hot_two, 1.0, 0.0).astype(LOW)
    row = lax.broadcasted_iota(jnp.int32, (tokens, tokens), 0)
    column = lax.broadcasted_iota(jnp.int32, (tokens, tokens), 1)
    earlier = jnp.where(column < row, 1.0, 0.0).astype(LOW)
    rank = dot(earlier, named)
    slots = lax.broadcasted_iota(jnp.int32, (tokens, experts * STRIDE), 1)

    def picks(hot, route):
        place = jnp.sum(jnp.where(hot, rank, 0.0), axis=1, keepdims=True).astype(jnp.int32)
        return jnp.where(slots == route * STRIDE + place, 1.0, 0.0)

    one, two = picks(hot_one, routes[:, 0:1]), picks(hot_two, routes[:, 1:2])
    pick_one_ref[...] = one.astype(LOW)
    pick_two_ref[...] = two.astype(LOW)
    spread_rows(dot_tn((one + two).astype(LOW), normed), first_ref, second_ref)


def combine_kernel(first_ref, second_ref, states_ref, pick_one_ref, pick_two_ref, gate_ref, hidden_ref, normed_ref, packed):
    pack_rows(first_ref, second_ref, packed)
    rows = packed[...]
    gate = gate_ref[...]
    hidden = states_ref[...].astype(WIDE) + (
        gate * dot(pick_one_ref[...], rows) + (1.0 - gate) * dot(pick_two_ref[...], rows)
    )
    hidden_ref[...] = hidden
    normed_ref[...] = normalised(hidden)[0].astype(LOW)


def attend_kernel(length_ref, q_ref, k_ref, v_ref, grad_ref, context_ref, q_grad_ref, k_grad_ref, v_grad_ref):
    scale = HEAD ** (-0.5)
    live = lax.broadcasted_iota(jnp.int32, (LEN, LEN), 1) < length_ref[0, 0]
    for head in range(HEADS):
        at = slice(head * HEAD, (head + 1) * HEAD)
        q, k, v, grad = q_ref[:, at], k_ref[:, at], v_ref[:, at], grad_ref[:, at]
        scores = jnp.where(live, dot_nt(q, k) * scale, NEG_FILL)
        exponent = jnp.exp(scores - jnp.max(scores, axis=-1, keepdims=True))
        attention = exponent / jnp.sum(exponent, axis=-1, keepdims=True)
        attention_low = attention.astype(LOW)
        context_ref[:, at] = dot(attention_low, v).astype(LOW)
        weight_grad = dot_nt(grad, v)
        v_grad_ref[:, at] = dot_tn(attention_low, grad).astype(LOW)
        score_grad = (
            attention
            * (weight_grad - jnp.sum(attention * weight_grad, axis=-1, keepdims=True))
            * scale
        ).astype(LOW)
        q_grad_ref[:, at] = dot(score_grad, k).astype(LOW)
        k_grad_ref[:, at] = dot_tn(score_grad, q).astype(LOW)


def upstream_kernel(flags_ref, hidden_ref, back_ref, cotangent_ref, pick_one_ref, pick_two_ref, gate_ref, upstream_ref, first_ref, second_ref):
    live = lax.broadcasted_iota(jnp.int32, (LEN, 1), 0) < flags_ref[0, 0]
    encoder = flags_ref[0, 1] == 1
    masked = jnp.where(live, cotangent_ref[...].astype(WIDE), 0.0)
    out_grad = jnp.where(encoder, 0.0, masked)
    normed_grad = back_ref[...] + jnp.where(encoder, masked, 0.0)
    upstream = out_grad + norm_back(hidden_ref[...], normed_grad)
    upstream_ref[...] = upstream
    gate = gate_ref[...]
    rows = dot_tn(pick_one_ref[...], (gate * upstream).astype(LOW)) + dot_tn(
        pick_two_ref[...], ((1.0 - gate) * upstream).astype(LOW)
    )
    spread_rows(rows, first_ref, second_ref)


def router_kernel(first_ref, second_ref, upstream_ref, routes_ref, pick_one_ref, pick_two_ref, gate_ref, sign_ref, packed):
    pack_rows(first_ref, second_ref, packed)
    rows = packed[...]
    gate = gate_ref[...]
    apart = dot(pick_one_ref[...], rows) - dot(pick_two_ref[...], rows)
    gate_grad = jnp.sum(upstream_ref[...] * apart, axis=1, keepdims=True)
    logit_grad = gate_grad * gate * (1.0 - gate)
    hot_one, hot_two = route_hots(routes_ref[...], first_ref.shape[0])
    sign_ref[...] = jnp.where(hot_one, logit_grad, 0.0) - jnp.where(hot_two, logit_grad, 0.0)


def finish_kernel(first_ref, second_ref, states_ref, upstream_ref, sign_ref, router_ref, pick_one_ref, pick_two_ref, grads_ref, packed):
    pack_rows(first_ref, second_ref, packed)
    picks = pick_one_ref[...] + pick_two_ref[...]
    router_term = lax.dot_general(
        sign_ref[...],
        router_ref[...].astype(WIDE),
        (((1,), (1,)), ((), ())),
        precision=lax.Precision.HIGHEST,
        preferred_element_type=WIDE,
    )
    input_total = dot(picks, packed[...]) + router_term
    grads_ref[...] = upstream_ref[...] + norm_back(states_ref[...].astype(WIDE), input_total)


def local(kernel, out_shape, *operands, scalars=0, scratch=()):
    single = not isinstance(out_shape, tuple)
    shapes = (out_shape,) if single else out_shape
    cost = sum(x.size * x.dtype.itemsize for x in operands) + sum(
        x.size * x.dtype.itemsize for x in shapes
    )
    result = pl.pallas_call(
        kernel,
        out_shape=shapes,
        in_specs=[SMEM] * scalars + [VMEM] * (len(operands) - scalars),
        out_specs=tuple([VMEM] * len(shapes)),
        scratch_shapes=list(scratch),
        compiler_params=PARAMS,
        cost_estimate=pl.CostEstimate(flops=10**9, bytes_accessed=4 * cost, transcendentals=0),
    )(*operands)
    return result[0] if single else result


def shaped(shape, dtype):
    return jax.ShapeDtypeStruct(shape, dtype)


def shift(block, distance):
    count = lax.axis_size("dp")
    return lax.ppermute(block, "dp", [(i, (i + distance) % count) for i in range(count)])


def to_experts(block):
    return lax.all_to_all(block, "expert", split_axis=0, concat_axis=0, tiled=True)


def gather_ring(first, second):
    behind_one, ahead_one = shift(first, 1), shift(first, -1)
    behind_two, ahead_two = shift(second, 1), shift(second, -1)
    far_one, far_two = shift(behind_one, 1), shift(ahead_two, -1)
    return ((first, second), (behind_one, behind_two), (ahead_one, ahead_two), (far_one, far_two))


def reduce_ring(own, behind, ahead, far):
    step_one = shift(far[0].astype(LOW), 1)
    side_one = shift(behind[0].astype(LOW), -1)
    last_one = shift((ahead[0] + step_one.astype(WIDE)).astype(LOW), 1)
    first = (own[0] + side_one.astype(WIDE) + last_one.astype(WIDE)).astype(LOW)
    step_two = shift(far[1].astype(LOW), -1)
    side_two = shift(ahead[1].astype(LOW), 1)
    last_two = shift((behind[1] + step_two.astype(WIDE)).astype(LOW), -1)
    second = (own[1] + side_two.astype(WIDE) + last_two.astype(WIDE)).astype(LOW)
    return first, second


def per_device(
    states, routes, lengths, router, w_in, w_out, w_query, w_key, w_value, w_output, cotangent
):
    section = lax.axis_index("section")
    encoder_side = section == 0
    tokens_here = states[0]
    routes_here = routes[0]
    router_here = router[0]
    first_weight = w_in[0, 0]
    second_weight = w_out[0, 0]
    cotangent_here = cotangent[0]
    tokens, columns = tokens_here.shape
    experts = router_here.shape[1]
    capacity = max(2, 5 * TOP * tokens // (4 * experts))
    half = columns // 2
    width = HEADS * HEAD
    slot_count = experts * STRIDE
    block = shaped((experts, capacity, half), LOW)
    packed = pltpu.VMEM((slot_count, columns), LOW)

    rows_value = w_value.shape[0] // 2
    value_wide = jnp.concatenate([w_value[:rows_value], w_value[rows_value:]], axis=1)
    own_a = jnp.where(encoder_side, w_key, w_query)
    own_b = jnp.where(encoder_side, value_wide, w_output)
    full_a = lax.all_gather(own_a, ("dp", "expert"), axis=0, tiled=True)
    full_b = lax.all_gather(own_b, ("dp", "expert"), axis=0, tiled=True)
    full_value = (
        full_b.reshape(-1, rows_value, 2, width).transpose(0, 2, 1, 3).reshape(columns, width)
    )

    first, second, pick_one, pick_two, gate = local(
        dispatch_kernel,
        (block, block, shaped((tokens, slot_count), LOW), shaped((tokens, slot_count), LOW), shaped((tokens, 1), WIDE)),
        tokens_here,
        routes_here,
        router_here,
    )

    def to_holders(one, two):
        one = to_experts(one).reshape(-1, half)
        two = to_experts(two).reshape(-1, half)
        return gather_ring(one, two)

    def to_tokens(terms):
        one, two = reduce_ring(*terms)
        return (
            to_experts(one.reshape(experts, capacity, half)),
            to_experts(two.reshape(experts, capacity, half)),
        )

    actives, terms = [], []
    for one, two in to_holders(first, second):
        pre = dot(one, first_weight[:half]) + dot(two, first_weight[half:])
        active = jnp.maximum(pre, 0.0).astype(LOW)
        actives.append(active)
        terms.append((dot(active, second_weight[:, :half]), dot(active, second_weight[:, half:])))
    back_one, back_two = to_tokens(terms)

    hidden_state, normed_out = local(
        combine_kernel,
        (shaped((tokens, columns), WIDE), shaped((tokens, columns), LOW)),
        back_one,
        back_two,
        tokens_here,
        pick_one,
        pick_two,
        gate,
        scratch=(packed,),
    )
    own_length = jnp.where(encoder_side, lengths[0, 0], lengths[1, 0])
    live = jnp.arange(LEN, dtype=jnp.int32)[:, None] < own_length
    out_low = jnp.where(live & ~encoder_side, cotangent_here, jnp.zeros((), LOW))
    context_grad = dot_nt(out_low, full_b).astype(LOW)

    own_rows = dot(normed_out, full_a).astype(LOW)
    own_values = dot(normed_out, full_value).astype(LOW)
    key_rows = lax.ppermute(own_rows, "section", [(0, 1)])
    value_rows = lax.ppermute(own_values, "section", [(0, 1)])
    low_rows = shaped((tokens, width), LOW)
    context, query_grad, key_grad, value_grad = local(
        attend_kernel,
        (low_rows,) * 4,
        lengths[0].reshape(1, 1),
        own_rows,
        key_rows,
        value_rows,
        context_grad,
        scalars=1,
    )
    decoder_out = (hidden_state + dot(context, full_b)).astype(LOW)
    forward_out = jnp.where(encoder_side, normed_out, decoder_out)
    value_back = lax.ppermute(value_grad, "section", [(1, 0)])
    key_back = lax.ppermute(key_grad, "section", [(1, 0)])
    projection_back = dot_nt(jnp.where(encoder_side, key_back, query_grad), full_a) + dot_nt(
        value_back, full_value
    )
    flags = jnp.stack([own_length, encoder_side.astype(jnp.int32)])[None]
    upstream, first, second = local(
        upstream_kernel,
        (shaped((tokens, columns), WIDE), block, block),
        flags,
        hidden_state,
        projection_back,
        cotangent_here,
        pick_one,
        pick_two,
        gate,
        scalars=1,
    )
    sign_grad = local(
        router_kernel,
        shaped((tokens, experts), WIDE),
        back_one,
        back_two,
        upstream,
        routes_here,
        pick_one,
        pick_two,
        gate,
        scratch=(packed,),
    )
    terms = []
    for active, (one, two) in zip(actives, to_holders(first, second)):
        slope = dot_nt(one, second_weight[:, :half]) + dot_nt(two, second_weight[:, half:])
        slope = jnp.where(active > 0, slope, 0.0).astype(LOW)
        terms.append((dot_nt(slope, first_weight[:half]), dot_nt(slope, first_weight[half:])))
    back_one, back_two = to_tokens(terms)
    grads = local(
        finish_kernel,
        shaped((tokens, columns), WIDE),
        back_one,
        back_two,
        tokens_here,
        upstream,
        sign_grad,
        router_here,
        pick_one,
        pick_two,
        scratch=(packed,),
    )
    return (forward_out[None], grads[None])


def solution(mesh):
    in_specs = (
        P("section", ("dp", "expert"), None),
        P("section", ("dp", "expert"), None),
        P(None, ("dp", "expert")),
        P("section", None, None),
        P("section", "expert", None, "dp"),
        P("section", "expert", "dp", None),
        P(("dp", "expert"), None),
        P(("dp", "expert"), None),
        P(("dp", "expert"), None),
        P(("dp", "expert"), None),
        P("section", ("dp", "expert"), None),
    )
    out_specs = (P("section", ("dp", "expert"), None), P("section", ("dp", "expert"), None))
    return jax.shard_map(
        per_device, mesh=mesh, in_specs=in_specs, out_specs=out_specs, check_vma=False
    )
```

```python
import functools

import jax
import jax.numpy as jnp
from jax import lax
from jax.experimental import pallas as pl
from jax.experimental.pallas import tpu as pltpu
from jax.sharding import PartitionSpec as P

HEADS = 8
HEAD = 128
TOP = 2
LEN = 128
STRIDE = 32


EPS = 1e-05
NEG_FILL = -1e30
LOW = jnp.bfloat16
WIDE = jnp.float32
VMEM = pl.BlockSpec(memory_space=pltpu.VMEM)
SMEM = pl.BlockSpec(memory_space=pltpu.SMEM)
PARAMS = pltpu.CompilerParams(vmem_limit_bytes=48 * 1024 * 1024)


def dot(a, b):
    return jnp.dot(a, b, preferred_element_type=WIDE)


def dot_nt(a, b):
    return lax.dot_general(a, b, (((1,), (1,)), ((), ())), preferred_element_type=WIDE)


def dot_tn(a, b):
    return lax.dot_general(a, b, (((0,), (0,)), ((), ())), preferred_element_type=WIDE)


def normalised(values):
    centred = values - jnp.mean(values, axis=-1, keepdims=True)
    variance = jnp.mean(centred * centred, axis=-1, keepdims=True)
    inverse = lax.rsqrt(variance + EPS)
    return centred * inverse, inverse


def norm_back(values, upstream):
    normed, inverse = normalised(values)
    return inverse * (
        upstream
        - jnp.mean(upstream, axis=-1, keepdims=True)
        - normed * jnp.mean(upstream * normed, axis=-1, keepdims=True)
    )


def route_hots(routes, experts):
    ids = lax.broadcasted_iota(jnp.int32, (routes.shape[0], experts), 1)
    return routes[:, 0:1] == ids, routes[:, 1:2] == ids


def spread_rows(rows, slots_ref):
    experts, capacity, _ = slots_ref.shape
    for e in range(experts):
        slots_ref[e] = rows[e * STRIDE : e * STRIDE + capacity].astype(LOW)


def pack_rows(slots_ref, packed):
    experts, capacity, _ = slots_ref.shape
    packed[...] = jnp.zeros_like(packed)
    for e in range(experts):
        packed[pl.ds(e * STRIDE, capacity), :] = slots_ref[e]


def dispatch_kernel(states_ref, routes_ref, router_ref, slots_ref, pick_one_ref, pick_two_ref, gate_ref):
    experts = slots_ref.shape[0]
    tokens = states_ref.shape[0]
    normed = normalised(states_ref[...].astype(WIDE))[0].astype(LOW)
    logits = dot(normed, router_ref[...])
    routes = routes_ref[...]
    hot_one, hot_two = route_hots(routes, experts)
    spread = jnp.sum(
        jnp.where(hot_one, logits, 0.0) - jnp.where(hot_two, logits, 0.0), axis=1, keepdims=True
    )
    gate_ref[...] = jax.nn.sigmoid(spread)
    named = jnp.where(hot_one | hot_two, 1.0, 0.0).astype(LOW)
    row = lax.broadcasted_iota(jnp.int32, (tokens, tokens), 0)
    column = lax.broadcasted_iota(jnp.int32, (tokens, tokens), 1)
    earlier = jnp.where(column < row, 1.0, 0.0).astype(LOW)
    rank = dot(earlier, named)
    slots = lax.broadcasted_iota(jnp.int32, (tokens, experts * STRIDE), 1)

    def picks(hot, route):
        place = jnp.sum(jnp.where(hot, rank, 0.0), axis=1, keepdims=True).astype(jnp.int32)
        return jnp.where(slots == route * STRIDE + place, 1.0, 0.0)

    one, two = picks(hot_one, routes[:, 0:1]), picks(hot_two, routes[:, 1:2])
    pick_one_ref[...] = one.astype(LOW)
    pick_two_ref[...] = two.astype(LOW)
    spread_rows(dot_tn((one + two).astype(LOW), normed), slots_ref)


def combine_kernel(slots_ref, states_ref, pick_one_ref, pick_two_ref, gate_ref, hidden_ref, normed_ref, packed):
    pack_rows(slots_ref, packed)
    rows = packed[...]
    gate = gate_ref[...]
    hidden = states_ref[...].astype(WIDE) + (
        gate * dot(pick_one_ref[...], rows) + (1.0 - gate) * dot(pick_two_ref[...], rows)
    )
    hidden_ref[...] = hidden
    normed_ref[...] = normalised(hidden)[0].astype(LOW)


def attend_kernel(length_ref, q_ref, k_ref, v_ref, grad_ref, context_ref, q_grad_ref, k_grad_ref, v_grad_ref):
    scale = HEAD ** (-0.5)
    live = lax.broadcasted_iota(jnp.int32, (LEN, LEN), 1) < length_ref[0, 0]
    for head in range(HEADS):
        at = slice(head * HEAD, (head + 1) * HEAD)
        q, k, v, grad = q_ref[:, at], k_ref[:, at], v_ref[:, at], grad_ref[:, at]
        scores = jnp.where(live, dot_nt(q, k) * scale, NEG_FILL)
        exponent = jnp.exp(scores - jnp.max(scores, axis=-1, keepdims=True))
        attention = exponent / jnp.sum(exponent, axis=-1, keepdims=True)
        attention_low = attention.astype(LOW)
        context_ref[:, at] = dot(attention_low, v).astype(LOW)
        weight_grad = dot_nt(grad, v)
        v_grad_ref[:, at] = dot_tn(attention_low, grad).astype(LOW)
        score_grad = (
            attention
            * (weight_grad - jnp.sum(attention * weight_grad, axis=-1, keepdims=True))
            * scale
        ).astype(LOW)
        q_grad_ref[:, at] = dot(score_grad, k).astype(LOW)
        k_grad_ref[:, at] = dot_tn(score_grad, q).astype(LOW)


def upstream_kernel(flags_ref, hidden_ref, back_ref, cotangent_ref, pick_one_ref, pick_two_ref, gate_ref, upstream_ref, slots_ref):
    live = lax.broadcasted_iota(jnp.int32, (LEN, 1), 0) < flags_ref[0, 0]
    encoder = flags_ref[0, 1] == 1
    masked = jnp.where(live, cotangent_ref[...].astype(WIDE), 0.0)
    out_grad = jnp.where(encoder, 0.0, masked)
    normed_grad = back_ref[...] + jnp.where(encoder, masked, 0.0)
    upstream = out_grad + norm_back(hidden_ref[...], normed_grad)
    upstream_ref[...] = upstream
    gate = gate_ref[...]
    rows = dot_tn(pick_one_ref[...], (gate * upstream).astype(LOW)) + dot_tn(
        pick_two_ref[...], ((1.0 - gate) * upstream).astype(LOW)
    )
    spread_rows(rows, slots_ref)


def router_kernel(slots_ref, upstream_ref, routes_ref, pick_one_ref, pick_two_ref, gate_ref, sign_ref, packed):
    pack_rows(slots_ref, packed)
    rows = packed[...]
    gate = gate_ref[...]
    apart = dot(pick_one_ref[...], rows) - dot(pick_two_ref[...], rows)
    gate_grad = jnp.sum(upstream_ref[...] * apart, axis=1, keepdims=True)
    logit_grad = gate_grad * gate * (1.0 - gate)
    hot_one, hot_two = route_hots(routes_ref[...], slots_ref.shape[0])
    sign_ref[...] = jnp.where(hot_one, logit_grad, 0.0) - jnp.where(hot_two, logit_grad, 0.0)


def finish_kernel(slots_ref, states_ref, upstream_ref, sign_ref, router_ref, pick_one_ref, pick_two_ref, grads_ref, packed):
    pack_rows(slots_ref, packed)
    picks = pick_one_ref[...] + pick_two_ref[...]
    router_term = lax.dot_general(
        sign_ref[...],
        router_ref[...].astype(WIDE),
        (((1,), (1,)), ((), ())),
        precision=lax.Precision.HIGHEST,
        preferred_element_type=WIDE,
    )
    input_total = dot(picks, packed[...]) + router_term
    grads_ref[...] = upstream_ref[...] + norm_back(states_ref[...].astype(WIDE), input_total)


def local(kernel, out_shape, *operands, scalars=0, scratch=()):
    single = not isinstance(out_shape, tuple)
    shapes = (out_shape,) if single else out_shape
    cost = sum(x.size * x.dtype.itemsize for x in operands) + sum(
        x.size * x.dtype.itemsize for x in shapes
    )
    result = pl.pallas_call(
        kernel,
        out_shape=shapes,
        in_specs=[SMEM] * scalars + [VMEM] * (len(operands) - scalars),
        out_specs=tuple([VMEM] * len(shapes)),
        scratch_shapes=list(scratch),
        compiler_params=PARAMS,
        cost_estimate=pl.CostEstimate(flops=10**9, bytes_accessed=4 * cost, transcendentals=0),
    )(*operands)
    return result[0] if single else result


def shaped(shape, dtype):
    return jax.ShapeDtypeStruct(shape, dtype)


def shift(block, distance):
    count = lax.axis_size("dp")
    return lax.ppermute(block, "dp", [(i, (i + distance) % count) for i in range(count)])


def to_experts(block):
    return lax.all_to_all(block, "expert", split_axis=0, concat_axis=0, tiled=True)


def gather_ring(first, second):
    behind_one, ahead_one = shift(first, 1), shift(first, -1)
    behind_two, ahead_two = shift(second, 1), shift(second, -1)
    far_one, far_two = shift(behind_one, 1), shift(ahead_two, -1)
    return ((first, second), (behind_one, behind_two), (ahead_one, ahead_two), (far_one, far_two))


def reduce_ring(own, behind, ahead, far, sides):
    step_one = shift(far[0].astype(LOW), 1)
    side_one = shift(sides[0], -1)
    last_one = shift((ahead[0] + step_one.astype(WIDE)).astype(LOW), 1)
    first = (own[0] + side_one.astype(WIDE) + last_one.astype(WIDE)).astype(LOW)
    step_two = shift(far[1].astype(LOW), -1)
    side_two = shift(sides[1], 1)
    last_two = shift((behind[1] + step_two.astype(WIDE)).astype(LOW), -1)
    second = (own[1] + side_two.astype(WIDE) + last_two.astype(WIDE)).astype(LOW)
    return first, second


def expert_terms(blocks, term):
    terms = [term(block, place) for place, block in enumerate(blocks[:3])]
    sides = (terms[1][0].astype(LOW), terms[2][1].astype(LOW))
    far, sides = lax.optimization_barrier((blocks[3], sides))
    return terms + [term(far, 3), sides]


def per_device(
    states, routes, lengths, router, w_in, w_out, w_query, w_key, w_value, w_output, cotangent
):
    section = lax.axis_index("section")
    encoder_side = section == 0
    tokens_here = states[0]
    routes_here = routes[0]
    router_here = router[0]
    first_weight = w_in[0, 0]
    second_weight = w_out[0, 0]
    cotangent_here = cotangent[0]
    tokens, columns = tokens_here.shape
    experts = router_here.shape[1]
    capacity = max(2, 5 * TOP * tokens // (4 * experts))
    half = columns // 2
    width = HEADS * HEAD
    slot_count = experts * STRIDE
    block = shaped((experts, capacity, columns), LOW)
    packed = pltpu.VMEM((slot_count, columns), LOW)

    slots, pick_one, pick_two, gate = local(
        dispatch_kernel,
        (block, shaped((tokens, slot_count), LOW), shaped((tokens, slot_count), LOW), shaped((tokens, 1), WIDE)),
        tokens_here,
        routes_here,
        router_here,
    )

    def to_holders(slots):
        arrived = to_experts(slots)
        return gather_ring(
            arrived[:, :, :half].reshape(-1, half), arrived[:, :, half:].reshape(-1, half)
        )

    def to_tokens(terms):
        sums = [part.reshape(experts, capacity, half) for part in reduce_ring(*terms)]
        return to_experts(jnp.concatenate(sums, axis=2))

    actives = []

    def forward_term(rows, place):
        pre = dot(rows[0], first_weight[:half]) + dot(rows[1], first_weight[half:])
        active = jnp.maximum(pre, 0.0).astype(LOW)
        actives.append(active)
        return dot(active, second_weight[:, :half]), dot(active, second_weight[:, half:])

    terms = expert_terms(to_holders(slots), forward_term)
    own_a = jnp.where(encoder_side, w_key, w_query)
    output_wide = jnp.concatenate([w_output[:, :width], w_output[:, width:]], axis=0)
    own_b = jnp.where(encoder_side, w_value, output_wide)
    dense = lax.all_gather(
        jnp.concatenate([own_a, own_b], axis=0), ("dp", "expert"), axis=0, tiled=True
    )
    dense, terms[3] = lax.optimization_barrier((dense, terms[3]))
    dense = dense.reshape(-1, 2, own_a.shape[0], width)
    full_a = dense[:, 0].reshape(-1, width)
    full_value = dense[:, 1].reshape(-1, width)
    dense = dense[:, 1].reshape(-1, 2, w_output.shape[0], width)
    full_left, full_right = dense[:, 0].reshape(-1, width), dense[:, 1].reshape(-1, width)
    back = to_tokens(terms)

    hidden_state, normed_out = local(
        combine_kernel,
        (shaped((tokens, columns), WIDE), shaped((tokens, columns), LOW)),
        back,
        tokens_here,
        pick_one,
        pick_two,
        gate,
        scratch=(packed,),
    )
    own_length = jnp.where(encoder_side, lengths[0, 0], lengths[1, 0])
    live = jnp.arange(LEN, dtype=jnp.int32)[:, None] < own_length
    out_low = jnp.where(live & ~encoder_side, cotangent_here, jnp.zeros((), LOW))
    context_grad = (
        dot_nt(out_low[:, :half], full_left) + dot_nt(out_low[:, half:], full_right)
    ).astype(LOW)

    own_rows = dot(normed_out, full_a).astype(LOW)
    own_values = dot(normed_out, full_value).astype(LOW)
    key_rows = lax.ppermute(own_rows, "section", [(0, 1)])
    value_rows = lax.ppermute(own_values, "section", [(0, 1)])
    low_rows = shaped((tokens, width), LOW)
    context, query_grad, key_grad, value_grad = local(
        attend_kernel,
        (low_rows,) * 4,
        lengths[0].reshape(1, 1),
        own_rows,
        key_rows,
        value_rows,
        context_grad,
        scalars=1,
    )
    attended = jnp.concatenate([dot(context, full_left), dot(context, full_right)], axis=1)
    decoder_out = (hidden_state + attended).astype(LOW)
    forward_out = jnp.where(encoder_side, normed_out, decoder_out)
    value_back = lax.ppermute(value_grad, "section", [(1, 0)])
    key_back = lax.ppermute(key_grad, "section", [(1, 0)])
    projection_back = dot_nt(jnp.where(encoder_side, key_back, query_grad), full_a) + dot_nt(
        value_back, full_value
    )
    flags = jnp.stack([own_length, encoder_side.astype(jnp.int32)])[None]
    upstream, slots = local(
        upstream_kernel,
        (shaped((tokens, columns), WIDE), block),
        flags,
        hidden_state,
        projection_back,
        cotangent_here,
        pick_one,
        pick_two,
        gate,
        scalars=1,
    )
    sign_grad = local(
        router_kernel,
        shaped((tokens, experts), WIDE),
        back,
        upstream,
        routes_here,
        pick_one,
        pick_two,
        gate,
        scratch=(packed,),
    )

    def backward_term(rows, place):
        slope = dot_nt(rows[0], second_weight[:, :half]) + dot_nt(rows[1], second_weight[:, half:])
        slope = jnp.where(actives[place] > 0, slope, 0.0).astype(LOW)
        return dot_nt(slope, first_weight[:half]), dot_nt(slope, first_weight[half:])

    terms = expert_terms(to_holders(slots), backward_term)
    back = to_tokens(terms)
    grads = local(
        finish_kernel,
        shaped((tokens, columns), WIDE),
        back,
        tokens_here,
        upstream,
        sign_grad,
        router_here,
        pick_one,
        pick_two,
        scratch=(packed,),
    )
    return (forward_out[None], grads[None])


def solution(mesh):
    in_specs = (
        P("section", ("dp", "expert"), None),
        P("section", ("dp", "expert"), None),
        P(None, ("dp", "expert")),
        P("section", None, None),
        P("section", "expert", None, "dp"),
        P("section", "expert", "dp", None),
        P(("dp", "expert"), None),
        P(("dp", "expert"), None),
        P(("dp", "expert"), None),
        P(("dp", "expert"), None),
        P("section", ("dp", "expert"), None),
    )
    out_specs = (P("section", ("dp", "expert"), None), P("section", ("dp", "expert"), None))
    return jax.shard_map(
        per_device, mesh=mesh, in_specs=in_specs, out_specs=out_specs, check_vma=False
    )
```

```python
import functools

import jax
import jax.numpy as jnp
from jax import lax
from jax.experimental import pallas as pl
from jax.experimental.pallas import tpu as pltpu
from jax.sharding import PartitionSpec as P

HEADS = 8
HEAD = 128
TOP = 2
LEN = 128
STRIDE = 32
LANES = 128
PLANES = 4


EPS = 1e-05
NEG_FILL = -1e30
LOW = jnp.bfloat16
WIDE = jnp.float32
VMEM = pl.BlockSpec(memory_space=pltpu.VMEM)
SMEM = pl.BlockSpec(memory_space=pltpu.SMEM)
PARAMS = pltpu.CompilerParams(vmem_limit_bytes=48 * 1024 * 1024)


def dot(a, b):
    return jnp.dot(a, b, preferred_element_type=WIDE)


def dot_nt(a, b):
    return lax.dot_general(a, b, (((1,), (1,)), ((), ())), preferred_element_type=WIDE)


def dot_tn(a, b):
    return lax.dot_general(a, b, (((0,), (0,)), ((), ())), preferred_element_type=WIDE)


def normalised(values):
    centred = values - jnp.mean(values, axis=-1, keepdims=True)
    variance = jnp.mean(centred * centred, axis=-1, keepdims=True)
    inverse = lax.rsqrt(variance + EPS)
    return centred * inverse, inverse


def norm_back(values, upstream):
    normed, inverse = normalised(values)
    return inverse * (
        upstream
        - jnp.mean(upstream, axis=-1, keepdims=True)
        - normed * jnp.mean(upstream * normed, axis=-1, keepdims=True)
    )


def route_hots(routes, experts):
    ids = lax.broadcasted_iota(jnp.int32, (routes.shape[0], experts), 1)
    return routes[:, 0:1] == ids, routes[:, 1:2] == ids


def spread_rows(rows, slots_ref):
    experts, capacity, _ = slots_ref.shape
    for e in range(experts):
        slots_ref[e] = rows[e * STRIDE : e * STRIDE + capacity].astype(LOW)


def pack_rows(slots_ref, packed):
    experts, capacity, _ = slots_ref.shape
    packed[...] = jnp.zeros_like(packed)
    for e in range(experts):
        packed[pl.ds(e * STRIDE, capacity), :] = slots_ref[e]


def laned(columns):
    lane = lax.broadcasted_iota(jnp.int32, (columns[0].shape[0], LANES), 1)
    return sum(jnp.where(lane == place, column, 0.0) for place, column in enumerate(columns))


def split_low(column, parts):
    pieces = []
    for _ in range(parts):
        piece = column.astype(LOW).astype(WIDE)
        pieces.append(piece)
        column = column - piece
    return pieces


def plane_facts(block_refs):
    width = block_refs[0].shape[1]
    return jnp.concatenate([ref[:, width - LANES :] for ref in block_refs], axis=0).astype(WIDE)


def plane_hots(facts, slots, capacity):
    tokens = facts.shape[0]
    plane = lax.broadcasted_iota(jnp.int32, (tokens, 1), 0) // (tokens // PLANES)
    place = lax.broadcasted_iota(jnp.int32, (tokens, slots), 1)

    def hot(route, rank):
        wanted = (route * (PLANES * capacity) + rank).astype(jnp.int32) + plane * capacity
        return jnp.where(place == wanted, 1.0, 0.0)

    return hot(facts[:, 0:1], facts[:, 1:2]), hot(facts[:, 2:3], facts[:, 3:4])


def plane_gates(facts):
    return facts[:, 4:5] + facts[:, 5:6] + facts[:, 6:7]


def stacked(refs, width):
    return jnp.concatenate([ref[:, :width] for ref in refs], axis=0)


def dispatch_kernel(states_ref, routes_ref, router_ref, slots_ref, block_ref, pick_one_ref, pick_two_ref, gate_ref):
    experts, _, near = slots_ref.shape
    tokens, columns = states_ref.shape
    normed = normalised(states_ref[...].astype(WIDE))[0].astype(LOW)
    logits = dot(normed, router_ref[...])
    routes = routes_ref[...]
    hot_one, hot_two = route_hots(routes, experts)
    spread = jnp.sum(
        jnp.where(hot_one, logits, 0.0) - jnp.where(hot_two, logits, 0.0), axis=1, keepdims=True
    )
    gate = jax.nn.sigmoid(spread)
    gate_ref[...] = gate
    named = jnp.where(hot_one | hot_two, 1.0, 0.0).astype(LOW)
    row = lax.broadcasted_iota(jnp.int32, (tokens, tokens), 0)
    column = lax.broadcasted_iota(jnp.int32, (tokens, tokens), 1)
    earlier = jnp.where(column < row, 1.0, 0.0).astype(LOW)
    rank = dot(earlier, named)
    rank_one = jnp.sum(jnp.where(hot_one, rank, 0.0), axis=1, keepdims=True)
    rank_two = jnp.sum(jnp.where(hot_two, rank, 0.0), axis=1, keepdims=True)
    slots = lax.broadcasted_iota(jnp.int32, (tokens, experts * STRIDE), 1)
    one = jnp.where(slots == routes[:, 0:1] * STRIDE + rank_one.astype(jnp.int32), 1.0, 0.0)
    two = jnp.where(slots == routes[:, 1:2] * STRIDE + rank_two.astype(jnp.int32), 1.0, 0.0)
    pick_one_ref[...] = one.astype(LOW)
    pick_two_ref[...] = two.astype(LOW)
    block_ref[:, : columns - near] = normed[:, near:]
    facts = [routes[:, 0:1].astype(WIDE), rank_one, routes[:, 1:2].astype(WIDE), rank_two]
    block_ref[:, columns - near :] = laned(facts + split_low(gate, 3)).astype(LOW)
    spread_rows(dot_tn((one + two).astype(LOW), normed[:, :near]), slots_ref)


def plane_dispatch_kernel(own_ref, behind_ref, ahead_ref, far_ref, slots_ref):
    experts, rows, width = slots_ref.shape
    refs = (own_ref, behind_ref, ahead_ref, far_ref)
    one, two = plane_hots(plane_facts(refs), experts * rows, rows // PLANES)
    spread = dot_tn((one + two).astype(LOW), stacked(refs, width))
    slots_ref[...] = spread.astype(LOW).reshape(slots_ref.shape)


def plane_combine_kernel(slots_ref, own_ref, behind_ref, ahead_ref, far_ref, sum_ref, to_behind_ref, to_ahead_ref, to_far_ref, apart_ref):
    experts, rows, width = slots_ref.shape
    facts = plane_facts((own_ref, behind_ref, ahead_ref, far_ref))
    one, two = plane_hots(facts, experts * rows, rows // PLANES)
    table = slots_ref[...].reshape(experts * rows, width)
    first, second = dot(one.astype(LOW), table), dot(two.astype(LOW), table)
    gate = plane_gates(facts)
    apart_ref[...] = first - second
    mixed = gate * first + (1.0 - gate) * second
    tokens = sum_ref.shape[0]
    sum_ref[...] = mixed[:tokens]
    for place, ref in enumerate((to_behind_ref, to_ahead_ref, to_far_ref)):
        ref[...] = mixed[(place + 1) * tokens : (place + 2) * tokens].astype(LOW)


def plane_slope_kernel(own_ref, behind_ref, ahead_ref, far_ref, up_own_ref, up_behind_ref, up_ahead_ref, up_far_ref, slots_ref):
    experts, rows, width = slots_ref.shape
    facts = plane_facts((own_ref, behind_ref, ahead_ref, far_ref))
    one, two = plane_hots(facts, experts * rows, rows // PLANES)
    gate = plane_gates(facts)
    up = stacked((up_own_ref, up_behind_ref, up_ahead_ref, up_far_ref), width).astype(WIDE)
    spread = dot_tn(one.astype(LOW), (gate * up).astype(LOW)) + dot_tn(
        two.astype(LOW), ((1.0 - gate) * up).astype(LOW)
    )
    slots_ref[...] = spread.astype(LOW).reshape(slots_ref.shape)


def plane_back_kernel(slots_ref, own_ref, behind_ref, ahead_ref, far_ref, up_own_ref, up_behind_ref, up_ahead_ref, up_far_ref, apart_ref, sum_ref, to_behind_ref, to_ahead_ref, to_far_ref):
    experts, rows, width = slots_ref.shape
    facts = plane_facts((own_ref, behind_ref, ahead_ref, far_ref))
    one, two = plane_hots(facts, experts * rows, rows // PLANES)
    table = slots_ref[...].reshape(experts * rows, width)
    back = dot((one + two).astype(LOW), table)
    up = stacked((up_own_ref, up_behind_ref, up_ahead_ref, up_far_ref), width).astype(WIDE)
    gate_grad = jnp.sum(up * apart_ref[...], axis=1, keepdims=True)
    extra = laned(split_low(gate_grad, 2))
    tokens = sum_ref.shape[0]
    for place, ref in enumerate((sum_ref, to_behind_ref, to_ahead_ref, to_far_ref)):
        at = slice(place * tokens, (place + 1) * tokens)
        ref[:, :width] = back[at].astype(ref.dtype)
        ref[:, width:] = extra[at].astype(ref.dtype)


def unpack_kernel(slots_ref, *plane_refs):
    experts, rows, _ = slots_ref.shape
    capacity = rows // PLANES
    for e in range(experts):
        for place, ref in enumerate(plane_refs):
            ref[pl.ds(e * capacity, capacity), :] = slots_ref[e, pl.ds(place * capacity, capacity), :]


def pack_kernel(*refs):
    plane_refs, slots_ref = refs[:-1], refs[-1]
    experts, rows, _ = slots_ref.shape
    capacity = rows // PLANES
    for e in range(experts):
        for place, ref in enumerate(plane_refs):
            slots_ref[e, pl.ds(place * capacity, capacity), :] = ref[pl.ds(e * capacity, capacity), :]


def combine_kernel(slots_ref, states_ref, pick_one_ref, pick_two_ref, gate_ref, own_ref, behind_ref, ahead_ref, far_ref, hidden_ref, normed_ref, packed):
    pack_rows(slots_ref, packed)
    rows = packed[...]
    near = rows.shape[1]
    gate = gate_ref[...]
    mixed = gate * dot(pick_one_ref[...], rows) + (1.0 - gate) * dot(pick_two_ref[...], rows)
    others = own_ref[...] + behind_ref[...].astype(WIDE)
    others = others + ahead_ref[...].astype(WIDE) + far_ref[...].astype(WIDE)
    hidden_ref[:, :near] = states_ref[:, :near].astype(WIDE) + mixed
    hidden_ref[:, near:] = states_ref[:, near:].astype(WIDE) + others
    normed_ref[...] = normalised(hidden_ref[...])[0].astype(LOW)


def attend_kernel(length_ref, q_ref, k_ref, v_ref, grad_ref, context_ref, q_grad_ref, k_grad_ref, v_grad_ref):
    scale = HEAD ** (-0.5)
    live = lax.broadcasted_iota(jnp.int32, (LEN, LEN), 1) < length_ref[0, 0]
    for head in range(HEADS):
        at = slice(head * HEAD, (head + 1) * HEAD)
        q, k, v, grad = q_ref[:, at], k_ref[:, at], v_ref[:, at], grad_ref[:, at]
        scores = jnp.where(live, dot_nt(q, k) * scale, NEG_FILL)
        exponent = jnp.exp(scores - jnp.max(scores, axis=-1, keepdims=True))
        attention = exponent / jnp.sum(exponent, axis=-1, keepdims=True)
        attention_low = attention.astype(LOW)
        context_ref[:, at] = dot(attention_low, v).astype(LOW)
        weight_grad = dot_nt(grad, v)
        v_grad_ref[:, at] = dot_tn(attention_low, grad).astype(LOW)
        score_grad = (
            attention
            * (weight_grad - jnp.sum(attention * weight_grad, axis=-1, keepdims=True))
            * scale
        ).astype(LOW)
        q_grad_ref[:, at] = dot(score_grad, k).astype(LOW)
        k_grad_ref[:, at] = dot_tn(score_grad, q).astype(LOW)


def upstream_kernel(flags_ref, hidden_ref, back_ref, cotangent_ref, pick_one_ref, pick_two_ref, gate_ref, upstream_ref, slots_ref, block_ref):
    near = slots_ref.shape[2]
    live = lax.broadcasted_iota(jnp.int32, (LEN, 1), 0) < flags_ref[0, 0]
    encoder = flags_ref[0, 1] == 1
    masked = jnp.where(live, cotangent_ref[...].astype(WIDE), 0.0)
    out_grad = jnp.where(encoder, 0.0, masked)
    normed_grad = back_ref[...] + jnp.where(encoder, masked, 0.0)
    upstream = out_grad + norm_back(hidden_ref[...], normed_grad)
    upstream_ref[...] = upstream
    block_ref[...] = upstream[:, near:].astype(LOW)
    gate = gate_ref[...]
    rows = dot_tn(pick_one_ref[...], (gate * upstream[:, :near]).astype(LOW)) + dot_tn(
        pick_two_ref[...], ((1.0 - gate) * upstream[:, :near]).astype(LOW)
    )
    spread_rows(rows, slots_ref)


def gate_kernel(slots_ref, upstream_ref, pick_one_ref, pick_two_ref, gate_grad_ref, packed):
    pack_rows(slots_ref, packed)
    rows = packed[...]
    apart = dot(pick_one_ref[...], rows) - dot(pick_two_ref[...], rows)
    gate_grad_ref[...] = jnp.sum(
        upstream_ref[:, : rows.shape[1]] * apart, axis=1, keepdims=True
    )


def finish_kernel(slots_ref, states_ref, upstream_ref, gate_grad_ref, gate_ref, routes_ref, router_ref, pick_one_ref, pick_two_ref, own_ref, behind_ref, ahead_ref, far_ref, grads_ref, packed, total):
    pack_rows(slots_ref, packed)
    rows = packed[...]
    near = rows.shape[1]
    far = total.shape[1] - near
    others = own_ref[...] + behind_ref[...].astype(WIDE)
    others = others + ahead_ref[...].astype(WIDE) + far_ref[...].astype(WIDE)
    gate = gate_ref[...]
    gate_grad = gate_grad_ref[...] + others[:, far : far + 1] + others[:, far + 1 : far + 2]
    logit_grad = gate_grad * gate * (1.0 - gate)
    hot_one, hot_two = route_hots(routes_ref[...], slots_ref.shape[0])
    sign_grad = jnp.where(hot_one, logit_grad, 0.0) - jnp.where(hot_two, logit_grad, 0.0)
    router_term = lax.dot_general(
        sign_grad,
        router_ref[...].astype(WIDE),
        (((1,), (1,)), ((), ())),
        precision=lax.Precision.HIGHEST,
        preferred_element_type=WIDE,
    )
    picks = pick_one_ref[...] + pick_two_ref[...]
    total[:, :near] = dot(picks, rows) + router_term[:, :near]
    total[:, near:] = others[:, :far] + router_term[:, near:]
    grads_ref[...] = upstream_ref[...] + norm_back(states_ref[...].astype(WIDE), total[...])


def local(kernel, out_shape, *operands, scalars=0, scratch=()):
    single = not isinstance(out_shape, tuple)
    shapes = (out_shape,) if single else out_shape
    cost = sum(x.size * x.dtype.itemsize for x in operands) + sum(
        x.size * x.dtype.itemsize for x in shapes
    )
    result = pl.pallas_call(
        kernel,
        out_shape=shapes,
        in_specs=[SMEM] * scalars + [VMEM] * (len(operands) - scalars),
        out_specs=tuple([VMEM] * len(shapes)),
        scratch_shapes=list(scratch),
        compiler_params=PARAMS,
        cost_estimate=pl.CostEstimate(flops=10**9, bytes_accessed=4 * cost, transcendentals=0),
    )(*operands)
    return result[0] if single else result


def shaped(shape, dtype):
    return jax.ShapeDtypeStruct(shape, dtype)


def shift(block, distance):
    count = lax.axis_size("dp")
    return lax.ppermute(block, "dp", [(i, (i + distance) % count) for i in range(count)])


def to_experts(block):
    return lax.all_to_all(block, "expert", split_axis=0, concat_axis=0, tiled=True)


def from_planes(block):
    return block, shift(block, 1), shift(block, -1), shift(block, 2)


def to_planes(own, behind, ahead, far):
    return own, shift(behind, -1), shift(ahead, 1), shift(far, 2)


def per_device(
    states, routes, lengths, router, w_in, w_out, w_query, w_key, w_value, w_output, cotangent
):
    section = lax.axis_index("section")
    encoder_side = section == 0
    tokens_here = states[0]
    routes_here = routes[0]
    router_here = router[0]
    first_weight = w_in[0, 0]
    second_weight = w_out[0, 0]
    cotangent_here = cotangent[0]
    tokens, columns = tokens_here.shape
    experts = router_here.shape[1]
    capacity = max(2, 5 * TOP * tokens // (4 * experts))
    width = HEADS * HEAD
    half = columns // 2
    far = columns * 3 // 8
    near = columns - far
    slot_count = experts * STRIDE
    near_slots = shaped((experts, capacity, near), LOW)
    far_slots = shaped((experts, PLANES * capacity, far), LOW)
    packed = pltpu.VMEM((slot_count, near), LOW)
    pick = shaped((tokens, slot_count), LOW)
    wide_rows = shaped((tokens, columns), WIDE)
    column = shaped((tokens, 1), WIDE)

    slots, block, pick_one, pick_two, gate = local(
        dispatch_kernel,
        (near_slots, shaped((tokens, far + LANES), LOW), pick, pick, column),
        tokens_here,
        routes_here,
        router_here,
    )

    def to_holders(slots, far_slots_here):
        near_rows = from_planes(to_experts(slots).reshape(-1, near))
        far_rows = local(
            unpack_kernel,
            (shaped((experts * capacity, far), LOW),) * PLANES,
            to_experts(far_slots_here),
        )
        return tuple(zip(near_rows, far_rows))

    def to_tokens(terms):
        far_sums = to_experts(local(pack_kernel, far_slots, *[term[1].astype(LOW) for term in terms]))
        own = terms[0][0]
        others = to_planes(own, *[term[0].astype(LOW) for term in terms[1:]])[1:]
        total = own + others[0].astype(WIDE) + others[1].astype(WIDE) + others[2].astype(WIDE)
        return to_experts(total.astype(LOW).reshape(experts, capacity, near)), far_sums

    blocks = from_planes(block)
    actives, terms = [], []
    arrived = to_holders(slots, local(plane_dispatch_kernel, far_slots, *blocks))
    for rows in arrived:
        pre = dot(rows[0], first_weight[:near]) + dot(rows[1], first_weight[near:])
        active = jnp.maximum(pre, 0.0).astype(LOW)
        actives.append(active)
        terms.append((dot(active, second_weight[:, :near]), dot(active, second_weight[:, near:])))

    own_a = jnp.where(encoder_side, w_key, w_query)
    output_wide = jnp.concatenate([w_output[:, :width], w_output[:, width:]], axis=0)
    own_b = jnp.where(encoder_side, w_value, output_wide)
    dense = lax.all_gather(
        jnp.concatenate([own_a, own_b], axis=0), ("dp", "expert"), axis=0, tiled=True
    )
    dense, terms[3] = lax.optimization_barrier((dense, terms[3]))
    dense = dense.reshape(-1, 2, own_a.shape[0], width)
    full_a = dense[:, 0].reshape(-1, width)
    full_value = dense[:, 1].reshape(-1, width)
    dense = dense[:, 1].reshape(-1, 2, w_output.shape[0], width)
    full_left, full_right = dense[:, 0].reshape(-1, width), dense[:, 1].reshape(-1, width)
    back, far_back = to_tokens(terms)
    far_low = shaped((tokens, far), LOW)
    *far_sums, apart = local(
        plane_combine_kernel,
        (shaped((tokens, far), WIDE), far_low, far_low, far_low, shaped((PLANES * tokens, far), WIDE)),
        far_back,
        *blocks,
    )

    hidden_state, normed_out = local(
        combine_kernel,
        (wide_rows, shaped((tokens, columns), LOW)),
        back,
        tokens_here,
        pick_one,
        pick_two,
        gate,
        *to_planes(*far_sums),
        scratch=(packed,),
    )
    own_length = jnp.where(encoder_side, lengths[0, 0], lengths[1, 0])
    live = jnp.arange(LEN, dtype=jnp.int32)[:, None] < own_length
    out_low = jnp.where(live & ~encoder_side, cotangent_here, jnp.zeros((), LOW))
    context_grad = (
        dot_nt(out_low[:, :half], full_left) + dot_nt(out_low[:, half:], full_right)
    ).astype(LOW)

    own_rows = dot(normed_out, full_a).astype(LOW)
    own_values = dot(normed_out, full_value).astype(LOW)
    key_rows = lax.ppermute(own_rows, "section", [(0, 1)])
    value_rows = lax.ppermute(own_values, "section", [(0, 1)])
    low_rows = shaped((tokens, width), LOW)
    context, query_grad, key_grad, value_grad = local(
        attend_kernel,
        (low_rows,) * 4,
        lengths[0].reshape(1, 1),
        own_rows,
        key_rows,
        value_rows,
        context_grad,
        scalars=1,
    )
    attended = jnp.concatenate([dot(context, full_left), dot(context, full_right)], axis=1)
    decoder_out = (hidden_state + attended).astype(LOW)
    forward_out = jnp.where(encoder_side, normed_out, decoder_out)
    value_back = lax.ppermute(value_grad, "section", [(1, 0)])
    key_back = lax.ppermute(key_grad, "section", [(1, 0)])
    projection_back = dot_nt(jnp.where(encoder_side, key_back, query_grad), full_a) + dot_nt(
        value_back, full_value
    )
    flags = jnp.stack([own_length, encoder_side.astype(jnp.int32)])[None]
    upstream, slots, block = local(
        upstream_kernel,
        (wide_rows, near_slots, far_low),
        flags,
        hidden_state,
        projection_back,
        cotangent_here,
        pick_one,
        pick_two,
        gate,
        scalars=1,
    )
    gate_grad = local(
        gate_kernel, column, back, upstream, pick_one, pick_two, scratch=(packed,)
    )
    up_blocks = from_planes(block)
    terms = []
    arrived = to_holders(slots, local(plane_slope_kernel, far_slots, *blocks, *up_blocks))
    for active, rows in zip(actives, arrived):
        slope = dot_nt(rows[0], second_weight[:, :near]) + dot_nt(rows[1], second_weight[:, near:])
        slope = jnp.where(active > 0, slope, 0.0).astype(LOW)
        terms.append((dot_nt(slope, first_weight[:near]), dot_nt(slope, first_weight[near:])))
    back, far_back = to_tokens(terms)
    far_low = shaped((tokens, far + LANES), LOW)
    far_sums = local(
        plane_back_kernel,
        (shaped((tokens, far + LANES), WIDE), far_low, far_low, far_low),
        far_back,
        *blocks,
        *up_blocks,
        apart,
    )
    grads = local(
        finish_kernel,
        wide_rows,
        back,
        tokens_here,
        upstream,
        gate_grad,
        gate,
        routes_here,
        router_here,
        pick_one,
        pick_two,
        *to_planes(*far_sums),
        scratch=(packed, pltpu.VMEM((tokens, columns), WIDE)),
    )
    return (forward_out[None], grads[None])


def solution(mesh):
    in_specs = (
        P("section", ("dp", "expert"), None),
        P("section", ("dp", "expert"), None),
        P(None, ("dp", "expert")),
        P("section", None, None),
        P("section", "expert", None, "dp"),
        P("section", "expert", "dp", None),
        P(("dp", "expert"), None),
        P(("dp", "expert"), None),
        P(("dp", "expert"), None),
        P(("dp", "expert"), None),
        P("section", ("dp", "expert"), None),
    )
    out_specs = (P("section", ("dp", "expert"), None), P("section", ("dp", "expert"), None))
    return jax.shard_map(
        per_device, mesh=mesh, in_specs=in_specs, out_specs=out_specs, check_vma=False
    )
```

```python
import functools

import jax
import jax.numpy as jnp
from jax import lax
from jax.experimental import pallas as pl
from jax.experimental.pallas import tpu as pltpu
from jax.sharding import PartitionSpec as P

HEADS = 8
HEAD = 128
TOP = 2
LEN = 128
STRIDE = 32


EPS = 1e-05
NEG_FILL = -1e30
LOW = jnp.bfloat16
WIDE = jnp.float32
VMEM = pl.BlockSpec(memory_space=pltpu.VMEM)
SMEM = pl.BlockSpec(memory_space=pltpu.SMEM)
PARAMS = pltpu.CompilerParams(vmem_limit_bytes=48 * 1024 * 1024)


def dot(a, b):
    return jnp.dot(a, b, preferred_element_type=WIDE)


def dot_nt(a, b):
    return lax.dot_general(a, b, (((1,), (1,)), ((), ())), preferred_element_type=WIDE)


def dot_tn(a, b):
    return lax.dot_general(a, b, (((0,), (0,)), ((), ())), preferred_element_type=WIDE)


def normalised(values):
    centred = values - jnp.mean(values, axis=-1, keepdims=True)
    variance = jnp.mean(centred * centred, axis=-1, keepdims=True)
    inverse = lax.rsqrt(variance + EPS)
    return centred * inverse, inverse


def norm_back(values, upstream):
    normed, inverse = normalised(values)
    return inverse * (
        upstream
        - jnp.mean(upstream, axis=-1, keepdims=True)
        - normed * jnp.mean(upstream * normed, axis=-1, keepdims=True)
    )


def route_hots(routes, experts):
    ids = lax.broadcasted_iota(jnp.int32, (routes.shape[0], experts), 1)
    return routes[:, 0:1] == ids, routes[:, 1:2] == ids


def spread_rows(rows, *half_refs):
    experts, double, columns = half_refs[0].shape
    capacity = double // 2
    for e in range(experts):
        block = rows[e * STRIDE : e * STRIDE + capacity].astype(LOW)
        for place in range(2 * len(half_refs)):
            part = block[:, place * columns : (place + 1) * columns]
            half_refs[place // 2][e, pl.ds(place % 2 * capacity, capacity), :] = part


def pack_rows(packed, *half_refs):
    experts, double, columns = half_refs[0].shape
    capacity = double // 2
    packed[...] = jnp.zeros_like(packed)
    for e in range(experts):
        for place in range(2 * len(half_refs)):
            packed[pl.ds(e * STRIDE, capacity), pl.ds(place * columns, columns)] = half_refs[
                place // 2
            ][e, pl.ds(place % 2 * capacity, capacity), :]


def unfold_kernel(half_ref, rows_ref):
    experts, double, columns = half_ref.shape
    capacity = double // 2
    for e in range(experts):
        for place in range(2):
            rows_ref[pl.ds(e * capacity, capacity), pl.ds(place * columns, columns)] = half_ref[
                e, pl.ds(place * capacity, capacity), :
            ]


def fold_kernel(own_ref, side_ref, last_ref, half_ref):
    experts, double, columns = half_ref.shape
    capacity = double // 2
    total = (own_ref[...] + side_ref[...].astype(WIDE) + last_ref[...].astype(WIDE)).astype(LOW)
    for e in range(experts):
        for place in range(2):
            half_ref[e, pl.ds(place * capacity, capacity), :] = total[
                e * capacity : (e + 1) * capacity, place * columns : (place + 1) * columns
            ]


def planes_kernel(place_ref, own_ref, behind_ref, ahead_ref, far_ref, planes_ref):
    count = planes_ref.shape[0]
    for distance, ref in ((0, own_ref), (count - 1, behind_ref), (1, ahead_ref), (2, far_ref)):
        planes_ref[lax.rem(place_ref[0, 0] + distance, count)] = ref[...]


def dense_kernel(dense_ref, first_ref, second_ref, left_ref, right_ref):
    experts, _, double, width = dense_ref.shape
    rows = double // 2
    first_ref[...] = dense_ref[:, 0, :rows].reshape(experts * rows, width)
    second = dense_ref[:, 0, rows:]
    second_ref[...] = second.reshape(experts * rows, width)
    left_ref[...] = second[:, : rows // 2].reshape(experts * rows // 2, width)
    right_ref[...] = second[:, rows // 2 :].reshape(experts * rows // 2, width)


def dispatch_kernel(states_ref, routes_ref, router_ref, first_ref, second_ref, pick_one_ref, pick_two_ref, gate_ref):
    experts = first_ref.shape[0]
    tokens = states_ref.shape[0]
    normed = normalised(states_ref[...].astype(WIDE))[0].astype(LOW)
    logits = dot(normed, router_ref[...])
    routes = routes_ref[...]
    hot_one, hot_two = route_hots(routes, experts)
    spread = jnp.sum(
        jnp.where(hot_one, logits, 0.0) - jnp.where(hot_two, logits, 0.0), axis=1, keepdims=True
    )
    gate_ref[...] = jax.nn.sigmoid(spread)
    named = jnp.where(hot_one | hot_two, 1.0, 0.0).astype(LOW)
    row = lax.broadcasted_iota(jnp.int32, (tokens, tokens), 0)
    column = lax.broadcasted_iota(jnp.int32, (tokens, tokens), 1)
    earlier = jnp.where(column < row, 1.0, 0.0).astype(LOW)
    rank = dot(earlier, named)
    slots = lax.broadcasted_iota(jnp.int32, (tokens, experts * STRIDE), 1)

    def picks(hot, route):
        place = jnp.sum(jnp.where(hot, rank, 0.0), axis=1, keepdims=True).astype(jnp.int32)
        return jnp.where(slots == route * STRIDE + place, 1.0, 0.0)

    one, two = picks(hot_one, routes[:, 0:1]), picks(hot_two, routes[:, 1:2])
    pick_one_ref[...] = one.astype(LOW)
    pick_two_ref[...] = two.astype(LOW)
    spread_rows(dot_tn((one + two).astype(LOW), normed), first_ref, second_ref)


def combine_kernel(first_ref, second_ref, states_ref, pick_one_ref, pick_two_ref, gate_ref, hidden_ref, normed_ref, packed):
    pack_rows(packed, first_ref, second_ref)
    rows = packed[...]
    gate = gate_ref[...]
    hidden = states_ref[...].astype(WIDE) + (
        gate * dot(pick_one_ref[...], rows) + (1.0 - gate) * dot(pick_two_ref[...], rows)
    )
    hidden_ref[...] = hidden
    normed_ref[...] = normalised(hidden)[0].astype(LOW)


def attend_kernel(length_ref, q_ref, k_ref, grad_ref, attention_ref, v_grad_ref):
    scale = HEAD ** (-0.5)
    live = lax.broadcasted_iota(jnp.int32, (LEN, LEN), 1) < length_ref[0, 0]
    for head in range(HEADS):
        at = slice(head * HEAD, (head + 1) * HEAD)
        scores = jnp.where(live, dot_nt(q_ref[:, at], k_ref[:, at]) * scale, NEG_FILL)
        exponent = jnp.exp(scores - jnp.max(scores, axis=-1, keepdims=True))
        attention = exponent / jnp.sum(exponent, axis=-1, keepdims=True)
        attention_ref[head] = attention
        v_grad_ref[:, at] = dot_tn(attention.astype(LOW), grad_ref[:, at]).astype(LOW)


def attend_back_kernel(attention_ref, q_ref, k_ref, v_ref, grad_ref, q_grad_ref, k_grad_ref, context_ref):
    scale = HEAD ** (-0.5)
    for head in range(HEADS):
        at = slice(head * HEAD, (head + 1) * HEAD)
        attention, v = attention_ref[head], v_ref[:, at]
        weight_grad = dot_nt(grad_ref[:, at], v)
        score_grad = (
            attention
            * (weight_grad - jnp.sum(attention * weight_grad, axis=-1, keepdims=True))
            * scale
        ).astype(LOW)
        k_grad_ref[:, at] = dot_tn(score_grad, q_ref[:, at]).astype(LOW)
        q_grad_ref[:, at] = dot(score_grad, k_ref[:, at]).astype(LOW)
        context_ref[:, at] = dot(attention.astype(LOW), v).astype(LOW)


def upstream_kernel(flags_ref, hidden_ref, back_ref, cotangent_ref, pick_one_ref, pick_two_ref, gate_ref, upstream_ref, first_ref, second_ref):
    live = lax.broadcasted_iota(jnp.int32, (LEN, 1), 0) < flags_ref[0, 0]
    encoder = flags_ref[0, 1] == 1
    masked = jnp.where(live, cotangent_ref[...].astype(WIDE), 0.0)
    out_grad = jnp.where(encoder, 0.0, masked)
    normed_grad = back_ref[...] + jnp.where(encoder, masked, 0.0)
    upstream = out_grad + norm_back(hidden_ref[...], normed_grad)
    upstream_ref[...] = upstream
    gate = gate_ref[...]
    rows = dot_tn(pick_one_ref[...], (gate * upstream).astype(LOW)) + dot_tn(
        pick_two_ref[...], ((1.0 - gate) * upstream).astype(LOW)
    )
    spread_rows(rows, first_ref, second_ref)


def router_kernel(first_ref, second_ref, upstream_ref, routes_ref, pick_one_ref, pick_two_ref, gate_ref, sign_ref, packed):
    pack_rows(packed, first_ref, second_ref)
    rows = packed[...]
    gate = gate_ref[...]
    apart = dot(pick_one_ref[...], rows) - dot(pick_two_ref[...], rows)
    gate_grad = jnp.sum(upstream_ref[...] * apart, axis=1, keepdims=True)
    logit_grad = gate_grad * gate * (1.0 - gate)
    hot_one, hot_two = route_hots(routes_ref[...], first_ref.shape[0])
    sign_ref[...] = jnp.where(hot_one, logit_grad, 0.0) - jnp.where(hot_two, logit_grad, 0.0)


def finish_kernel(first_ref, second_ref, states_ref, upstream_ref, sign_ref, router_ref, pick_one_ref, pick_two_ref, grads_ref, packed):
    pack_rows(packed, first_ref, second_ref)
    picks = pick_one_ref[...] + pick_two_ref[...]
    router_term = lax.dot_general(
        sign_ref[...],
        router_ref[...].astype(WIDE),
        (((1,), (1,)), ((), ())),
        precision=lax.Precision.HIGHEST,
        preferred_element_type=WIDE,
    )
    input_total = dot(picks, packed[...]) + router_term
    grads_ref[...] = upstream_ref[...] + norm_back(states_ref[...].astype(WIDE), input_total)


def local(kernel, out_shape, *operands, scalars=0, scratch=()):
    single = not isinstance(out_shape, tuple)
    shapes = (out_shape,) if single else out_shape
    cost = sum(x.size * x.dtype.itemsize for x in operands) + sum(
        x.size * x.dtype.itemsize for x in shapes
    )
    result = pl.pallas_call(
        kernel,
        out_shape=shapes,
        in_specs=[SMEM] * scalars + [VMEM] * (len(operands) - scalars),
        out_specs=tuple([VMEM] * len(shapes)),
        scratch_shapes=list(scratch),
        compiler_params=PARAMS,
        cost_estimate=pl.CostEstimate(flops=10**9, bytes_accessed=4 * cost, transcendentals=0),
    )(*operands)
    return result[0] if single else result


def shaped(shape, dtype):
    return jax.ShapeDtypeStruct(shape, dtype)


def shift(block, distance):
    count = lax.axis_size("dp")
    return lax.ppermute(block, "dp", [(i, (i + distance) % count) for i in range(count)])


def to_experts(block):
    return lax.all_to_all(block, "expert", split_axis=0, concat_axis=0, tiled=True)


def arrange(dense):
    experts, planes, double, width = dense.shape
    rows = experts * double // 2

    def blocks(count):
        return pl.BlockSpec((count, width), lambda plane: (plane, 0))

    whole, part = shaped((planes * rows, width), LOW), shaped((planes * rows // 2, width), LOW)
    return pl.pallas_call(
        dense_kernel,
        grid=(planes,),
        out_shape=(whole, whole, part, part),
        in_specs=[pl.BlockSpec((experts, 1, double, width), lambda plane: (0, plane, 0, 0))],
        out_specs=(blocks(rows), blocks(rows), blocks(rows // 2), blocks(rows // 2)),
        compiler_params=PARAMS,
        cost_estimate=pl.CostEstimate(flops=10**6, bytes_accessed=20 * 2**20, transcendentals=0),
    )(dense)


def to_holders(first, second):
    columns = 2 * first.shape[2]
    rows = shaped((first.shape[0] * first.shape[1] // 2, columns), LOW)
    first = to_experts(first)
    first, second = lax.optimization_barrier((first, second))
    second = to_experts(second)
    one = local(unfold_kernel, rows, first)
    behind_one, ahead_one = shift(one, 1), shift(one, -1)
    two = local(unfold_kernel, rows, second)
    behind_two, ahead_two = shift(two, 1), shift(two, -1)
    far_one, far_two = shift(behind_one, 1), shift(ahead_two, -1)
    return ((one, two), (behind_one, behind_two), (ahead_one, ahead_two), (far_one, far_two))


def expert_terms(blocks, term):
    terms = [term(block, place) for place, block in enumerate(blocks[:3])]
    side = terms[1][0].astype(LOW)
    far, side = lax.optimization_barrier((blocks[3], side))
    return terms + [term(far, 3), side]


def to_tokens(own, behind, ahead, far, side, block, extra):
    step_one = shift(far[0].astype(LOW), 1)
    side_one = shift(side, -1)
    step_two = shift(far[1].astype(LOW), -1)
    last_one = shift((ahead[0] + step_one.astype(WIDE)).astype(LOW), 1)
    third = (behind[1] + step_two.astype(WIDE)).astype(LOW)
    side = ahead[1].astype(LOW)
    last_one, third, side, extra = lax.optimization_barrier((last_one, third, side, extra))
    last_two, side_two = shift(third, -1), shift(side, 1)
    first = to_experts(local(fold_kernel, block, own[0], side_one, last_one))
    second = to_experts(local(fold_kernel, block, own[1], side_two, last_two))
    return first, second, extra


def per_device(
    states, routes, lengths, router, w_in, w_out, w_query, w_key, w_value, w_output, cotangent
):
    section = lax.axis_index("section")
    encoder_side = section == 0
    tokens_here = states[0]
    routes_here = routes[0]
    router_here = router[0]
    first_weight = w_in[0, 0]
    second_weight = w_out[0, 0]
    cotangent_here = cotangent[0]
    tokens, columns = tokens_here.shape
    experts = router_here.shape[1]
    capacity = max(2, 5 * TOP * tokens // (4 * experts))
    half = columns // 2
    width = HEADS * HEAD
    slot_count = experts * STRIDE
    block = shaped((experts, 2 * capacity, half // 2), LOW)
    packed = pltpu.VMEM((slot_count, columns), LOW)

    first, second, pick_one, pick_two, gate = local(
        dispatch_kernel,
        (block, block, shaped((tokens, slot_count), LOW), shaped((tokens, slot_count), LOW), shaped((tokens, 1), WIDE)),
        tokens_here,
        routes_here,
        router_here,
    )
    first, w_query, w_key, w_value, w_output = lax.optimization_barrier(
        (first, w_query, w_key, w_value, w_output)
    )
    own_a = jnp.where(encoder_side, w_key, w_query)
    output_wide = jnp.concatenate([w_output[:, :width], w_output[:, width:]], axis=0)
    own_b = jnp.where(encoder_side, w_value, output_wide)
    dense = jnp.concatenate([own_a, own_b], axis=0)
    dense = local(
        planes_kernel,
        shaped((lax.axis_size("dp"),) + dense.shape, LOW),
        lax.axis_index("dp").reshape(1, 1),
        dense,
        shift(dense, 1),
        shift(dense, -1),
        shift(dense, 2),
        scalars=1,
    )
    blocks = to_holders(first, second)
    dense, waited = lax.optimization_barrier((dense, blocks[0][0]))
    blocks = ((waited, blocks[0][1]),) + blocks[1:]
    dense = lax.all_gather(dense, "expert", axis=0, tiled=True)
    dense = dense.reshape(lax.axis_size("expert"), lax.axis_size("dp"), -1, width)

    actives = []

    def forward_term(rows, place):
        pre = dot(rows[0], first_weight[:half]) + dot(rows[1], first_weight[half:])
        active = jnp.maximum(pre, 0.0).astype(LOW)
        actives.append(active)
        return dot(active, second_weight[:, :half]), dot(active, second_weight[:, half:])

    terms = expert_terms(blocks, forward_term)
    back_one, back_two, dense = to_tokens(*terms, block, dense)
    full_a, full_value, full_left, full_right = arrange(dense)

    hidden_state, normed_out = local(
        combine_kernel,
        (shaped((tokens, columns), WIDE), shaped((tokens, columns), LOW)),
        back_one,
        back_two,
        tokens_here,
        pick_one,
        pick_two,
        gate,
        scratch=(packed,),
    )
    own_length = jnp.where(encoder_side, lengths[0, 0], lengths[1, 0])
    live = jnp.arange(LEN, dtype=jnp.int32)[:, None] < own_length
    out_low = jnp.where(live & ~encoder_side, cotangent_here, jnp.zeros((), LOW))
    context_grad = (
        dot_nt(out_low[:, :half], full_left) + dot_nt(out_low[:, half:], full_right)
    ).astype(LOW)

    own_rows = dot(normed_out, full_a).astype(LOW)
    own_rows, later = lax.optimization_barrier((own_rows, normed_out))
    own_values = dot(later, full_value).astype(LOW)
    key_rows = lax.ppermute(own_rows, "section", [(0, 1)])
    value_rows = lax.ppermute(own_values, "section", [(0, 1)])
    low_rows = shaped((tokens, width), LOW)
    attention, value_grad = local(
        attend_kernel,
        (shaped((HEADS, LEN, LEN), WIDE), low_rows),
        lengths[0].reshape(1, 1),
        own_rows,
        key_rows,
        context_grad,
        scalars=1,
    )
    value_back = lax.ppermute(value_grad, "section", [(1, 0)])
    query_grad, key_grad, context = local(
        attend_back_kernel,
        (low_rows,) * 3,
        attention,
        own_rows,
        key_rows,
        value_rows,
        context_grad,
    )
    key_back = lax.ppermute(key_grad, "section", [(1, 0)])
    attended = jnp.concatenate([dot(context, full_left), dot(context, full_right)], axis=1)
    decoder_out = (hidden_state + attended).astype(LOW)
    forward_out = jnp.where(encoder_side, normed_out, decoder_out)
    projection_back = dot_nt(jnp.where(encoder_side, key_back, query_grad), full_a) + dot_nt(
        value_back, full_value
    )
    flags = jnp.stack([own_length, encoder_side.astype(jnp.int32)])[None]
    upstream, first, second = local(
        upstream_kernel,
        (shaped((tokens, columns), WIDE), block, block),
        flags,
        hidden_state,
        projection_back,
        cotangent_here,
        pick_one,
        pick_two,
        gate,
        scalars=1,
    )
    sign_grad = local(
        router_kernel,
        shaped((tokens, experts), WIDE),
        back_one,
        back_two,
        upstream,
        routes_here,
        pick_one,
        pick_two,
        gate,
        scratch=(packed,),
    )

    def backward_term(rows, place):
        slope = dot_nt(rows[0], second_weight[:, :half]) + dot_nt(rows[1], second_weight[:, half:])
        slope = jnp.where(actives[place] > 0, slope, 0.0).astype(LOW)
        return dot_nt(slope, first_weight[:half]), dot_nt(slope, first_weight[half:])

    terms = expert_terms(to_holders(first, second), backward_term)
    back_one, back_two, _ = to_tokens(*terms, block, ())
    grads = local(
        finish_kernel,
        shaped((tokens, columns), WIDE),
        back_one,
        back_two,
        tokens_here,
        upstream,
        sign_grad,
        router_here,
        pick_one,
        pick_two,
        scratch=(packed,),
    )
    return (forward_out[None], grads[None])


def solution(mesh):
    in_specs = (
        P("section", ("dp", "expert"), None),
        P("section", ("dp", "expert"), None),
        P(None, ("dp", "expert")),
        P("section", None, None),
        P("section", "expert", None, "dp"),
        P("section", "expert", "dp", None),
        P(("dp", "expert"), None),
        P(("dp", "expert"), None),
        P(("dp", "expert"), None),
        P(("dp", "expert"), None),
        P("section", ("dp", "expert"), None),
    )
    out_specs = (P("section", ("dp", "expert"), None), P("section", ("dp", "expert"), None))
    return jax.shard_map(
        per_device, mesh=mesh, in_specs=in_specs, out_specs=out_specs, check_vma=False
    )
```

```python
import functools

import jax
import jax.numpy as jnp
from jax import lax
from jax.experimental import pallas as pl
from jax.experimental.pallas import tpu as pltpu
from jax.sharding import PartitionSpec as P

HEADS = 8
HEAD = 128
TOP = 2
LEN = 128
STRIDE = 32
FOLD = 4


EPS = 1e-05
NEG_FILL = -1e30
LOW = jnp.bfloat16
WIDE = jnp.float32
VMEM = pl.BlockSpec(memory_space=pltpu.VMEM)
SMEM = pl.BlockSpec(memory_space=pltpu.SMEM)
PARAMS = pltpu.CompilerParams(vmem_limit_bytes=20 * 1024 * 1024)


def dot(a, b):
    return jnp.dot(a, b, preferred_element_type=WIDE)


def dot_nt(a, b):
    return lax.dot_general(a, b, (((1,), (1,)), ((), ())), preferred_element_type=WIDE)


def dot_tn(a, b):
    return lax.dot_general(a, b, (((0,), (0,)), ((), ())), preferred_element_type=WIDE)


def normalised(values):
    centred = values - jnp.mean(values, axis=-1, keepdims=True)
    variance = jnp.mean(centred * centred, axis=-1, keepdims=True)
    inverse = lax.rsqrt(variance + EPS)
    return centred * inverse, inverse


def norm_back(values, upstream):
    normed, inverse = normalised(values)
    return inverse * (
        upstream
        - jnp.mean(upstream, axis=-1, keepdims=True)
        - normed * jnp.mean(upstream * normed, axis=-1, keepdims=True)
    )


def route_hots(routes, experts):
    ids = lax.broadcasted_iota(jnp.int32, (routes.shape[0], experts), 1)
    return routes[:, 0:1] == ids, routes[:, 1:2] == ids


def spread_rows(rows, folded_ref):
    experts, stack, columns = folded_ref.shape
    capacity = stack // FOLD
    for e in range(experts):
        block = rows[e * STRIDE : e * STRIDE + capacity].astype(LOW)
        for place in range(FOLD):
            folded_ref[e, pl.ds(place * capacity, capacity), :] = block[
                :, place * columns : (place + 1) * columns
            ]


def pack_rows(folded_ref, packed):
    experts, stack, columns = folded_ref.shape
    capacity = stack // FOLD
    packed[...] = jnp.zeros_like(packed)
    for e in range(experts):
        for place in range(FOLD):
            packed[pl.ds(e * STRIDE, capacity), pl.ds(place * columns, columns)] = folded_ref[
                e, pl.ds(place * capacity, capacity), :
            ]


def unfold_kernel(folded_ref, rows_ref, *, begin):
    experts, stack, columns = folded_ref.shape
    capacity = stack // FOLD
    for e in range(experts):
        for place in range(FOLD // 2):
            rows_ref[pl.ds(e * capacity, capacity), pl.ds(place * columns, columns)] = folded_ref[
                e, pl.ds((begin + place) * capacity, capacity), :
            ]


def fold_kernel(*refs):
    folded_ref = refs[-1]
    experts, stack, columns = folded_ref.shape
    capacity = stack // FOLD
    for begin in range(2):
        own_ref, side_ref, last_ref = refs[begin * 3 : begin * 3 + 3]
        total = own_ref[...] + side_ref[...].astype(WIDE) + last_ref[...].astype(WIDE)
        total = total.astype(LOW)
        for e in range(experts):
            for place in range(FOLD // 2):
                folded_ref[e, pl.ds((begin * FOLD // 2 + place) * capacity, capacity), :] = total[
                    e * capacity : (e + 1) * capacity, place * columns : (place + 1) * columns
                ]


def planes_kernel(place_ref, own_ref, behind_ref, ahead_ref, far_ref, planes_ref):
    count = planes_ref.shape[0]
    for distance, ref in ((0, own_ref), (count - 1, behind_ref), (1, ahead_ref), (2, far_ref)):
        planes_ref[lax.rem(place_ref[0, 0] + distance, count)] = ref[...]


def dense_kernel(dense_ref, first_ref, second_ref, left_ref, right_ref):
    experts, _, double, width = dense_ref.shape
    rows = double // 2
    first_ref[...] = dense_ref[:, 0, :rows].reshape(experts * rows, width)
    second = dense_ref[:, 0, rows:]
    second_ref[...] = second.reshape(experts * rows, width)
    left_ref[...] = second[:, : rows // 2].reshape(experts * rows // 2, width)
    right_ref[...] = second[:, rows // 2 :].reshape(experts * rows // 2, width)


def dispatch_kernel(states_ref, routes_ref, router_ref, folded_ref, pick_one_ref, pick_two_ref, gate_ref):
    experts = folded_ref.shape[0]
    tokens = states_ref.shape[0]
    normed = normalised(states_ref[...].astype(WIDE))[0].astype(LOW)
    logits = dot(normed, router_ref[...])
    routes = routes_ref[...]
    hot_one, hot_two = route_hots(routes, experts)
    spread = jnp.sum(
        jnp.where(hot_one, logits, 0.0) - jnp.where(hot_two, logits, 0.0), axis=1, keepdims=True
    )
    gate_ref[...] = jax.nn.sigmoid(spread)
    named = jnp.where(hot_one | hot_two, 1.0, 0.0).astype(LOW)
    row = lax.broadcasted_iota(jnp.int32, (tokens, tokens), 0)
    column = lax.broadcasted_iota(jnp.int32, (tokens, tokens), 1)
    earlier = jnp.where(column < row, 1.0, 0.0).astype(LOW)
    rank = dot(earlier, named)
    slots = lax.broadcasted_iota(jnp.int32, (tokens, experts * STRIDE), 1)

    def picks(hot, route):
        place = jnp.sum(jnp.where(hot, rank, 0.0), axis=1, keepdims=True).astype(jnp.int32)
        return jnp.where(slots == route * STRIDE + place, 1.0, 0.0)

    one, two = picks(hot_one, routes[:, 0:1]), picks(hot_two, routes[:, 1:2])
    pick_one_ref[...] = one.astype(LOW)
    pick_two_ref[...] = two.astype(LOW)
    spread_rows(dot_tn((one + two).astype(LOW), normed), folded_ref)


def combine_kernel(folded_ref, states_ref, pick_one_ref, pick_two_ref, gate_ref, hidden_ref, normed_ref, packed):
    pack_rows(folded_ref, packed)
    rows = packed[...]
    gate = gate_ref[...]
    hidden = states_ref[...].astype(WIDE) + (
        gate * dot(pick_one_ref[...], rows) + (1.0 - gate) * dot(pick_two_ref[...], rows)
    )
    hidden_ref[...] = hidden
    normed_ref[...] = normalised(hidden)[0].astype(LOW)


def attend_kernel(length_ref, q_ref, k_ref, grad_ref, attention_ref, v_grad_ref):
    scale = HEAD ** (-0.5)
    live = lax.broadcasted_iota(jnp.int32, (LEN, LEN), 1) < length_ref[0, 0]
    for head in range(HEADS):
        at = slice(head * HEAD, (head + 1) * HEAD)
        scores = jnp.where(live, dot_nt(q_ref[:, at], k_ref[:, at]) * scale, NEG_FILL)
        exponent = jnp.exp(scores - jnp.max(scores, axis=-1, keepdims=True))
        attention = exponent / jnp.sum(exponent, axis=-1, keepdims=True)
        attention_ref[head] = attention
        v_grad_ref[:, at] = dot_tn(attention.astype(LOW), grad_ref[:, at]).astype(LOW)


def attend_back_kernel(attention_ref, q_ref, k_ref, v_ref, grad_ref, q_grad_ref, k_grad_ref, context_ref):
    scale = HEAD ** (-0.5)
    for head in range(HEADS):
        at = slice(head * HEAD, (head + 1) * HEAD)
        attention, v = attention_ref[head], v_ref[:, at]
        weight_grad = dot_nt(grad_ref[:, at], v)
        score_grad = (
            attention
            * (weight_grad - jnp.sum(attention * weight_grad, axis=-1, keepdims=True))
            * scale
        ).astype(LOW)
        k_grad_ref[:, at] = dot_tn(score_grad, q_ref[:, at]).astype(LOW)
        q_grad_ref[:, at] = dot(score_grad, k_ref[:, at]).astype(LOW)
        context_ref[:, at] = dot(attention.astype(LOW), v).astype(LOW)


def upstream_kernel(flags_ref, hidden_ref, back_ref, cotangent_ref, pick_one_ref, pick_two_ref, gate_ref, upstream_ref, folded_ref):
    live = lax.broadcasted_iota(jnp.int32, (LEN, 1), 0) < flags_ref[0, 0]
    encoder = flags_ref[0, 1] == 1
    masked = jnp.where(live, cotangent_ref[...].astype(WIDE), 0.0)
    out_grad = jnp.where(encoder, 0.0, masked)
    normed_grad = back_ref[...] + jnp.where(encoder, masked, 0.0)
    upstream = out_grad + norm_back(hidden_ref[...], normed_grad)
    upstream_ref[...] = upstream
    gate = gate_ref[...]
    rows = dot_tn(pick_one_ref[...], (gate * upstream).astype(LOW)) + dot_tn(
        pick_two_ref[...], ((1.0 - gate) * upstream).astype(LOW)
    )
    spread_rows(rows, folded_ref)


def router_kernel(folded_ref, upstream_ref, routes_ref, pick_one_ref, pick_two_ref, gate_ref, sign_ref, packed):
    pack_rows(folded_ref, packed)
    rows = packed[...]
    gate = gate_ref[...]
    apart = dot(pick_one_ref[...], rows) - dot(pick_two_ref[...], rows)
    gate_grad = jnp.sum(upstream_ref[...] * apart, axis=1, keepdims=True)
    logit_grad = gate_grad * gate * (1.0 - gate)
    hot_one, hot_two = route_hots(routes_ref[...], folded_ref.shape[0])
    sign_ref[...] = jnp.where(hot_one, logit_grad, 0.0) - jnp.where(hot_two, logit_grad, 0.0)


def finish_kernel(folded_ref, states_ref, upstream_ref, sign_ref, router_ref, pick_one_ref, pick_two_ref, grads_ref, packed):
    pack_rows(folded_ref, packed)
    picks = pick_one_ref[...] + pick_two_ref[...]
    router_term = lax.dot_general(
        sign_ref[...],
        router_ref[...].astype(WIDE),
        (((1,), (1,)), ((), ())),
        precision=lax.Precision.HIGHEST,
        preferred_element_type=WIDE,
    )
    input_total = dot(picks, packed[...]) + router_term
    grads_ref[...] = upstream_ref[...] + norm_back(states_ref[...].astype(WIDE), input_total)


def local(kernel, out_shape, *operands, scalars=0, scratch=()):
    single = not isinstance(out_shape, tuple)
    shapes = (out_shape,) if single else out_shape
    cost = sum(x.size * x.dtype.itemsize for x in operands) + sum(
        x.size * x.dtype.itemsize for x in shapes
    )
    result = pl.pallas_call(
        kernel,
        out_shape=shapes,
        in_specs=[SMEM] * scalars + [VMEM] * (len(operands) - scalars),
        out_specs=tuple([VMEM] * len(shapes)),
        scratch_shapes=list(scratch),
        compiler_params=PARAMS,
        cost_estimate=pl.CostEstimate(flops=10**9, bytes_accessed=4 * cost, transcendentals=0),
    )(*operands)
    return result[0] if single else result


def shaped(shape, dtype):
    return jax.ShapeDtypeStruct(shape, dtype)


def shift(block, distance):
    count = lax.axis_size("dp")
    return lax.ppermute(block, "dp", [(i, (i + distance) % count) for i in range(count)])


def to_experts(block):
    return lax.all_to_all(block, "expert", split_axis=0, concat_axis=0, tiled=True)


def arrange(dense):
    experts, planes, double, width = dense.shape
    rows = experts * double // 2

    def blocks(count):
        return pl.BlockSpec((count, width), lambda plane: (plane, 0))

    whole, part = shaped((planes * rows, width), LOW), shaped((planes * rows // 2, width), LOW)
    return pl.pallas_call(
        dense_kernel,
        grid=(planes,),
        out_shape=(whole, whole, part, part),
        in_specs=[pl.BlockSpec((experts, 1, double, width), lambda plane: (0, plane, 0, 0))],
        out_specs=(blocks(rows), blocks(rows), blocks(rows // 2), blocks(rows // 2)),
        compiler_params=PARAMS,
        cost_estimate=pl.CostEstimate(flops=10**6, bytes_accessed=20 * 2**20, transcendentals=0),
    )(dense)


def to_holders(folded):
    experts, stack, columns = folded.shape
    rows = shaped((experts * stack // FOLD, columns * FOLD // 2), LOW)
    folded = to_experts(folded)
    one = local(functools.partial(unfold_kernel, begin=0), rows, folded)
    two = local(functools.partial(unfold_kernel, begin=FOLD // 2), rows, folded)
    behind_one, ahead_one = shift(one, 1), shift(one, -1)
    behind_two, ahead_two = shift(two, 1), shift(two, -1)
    far_one, far_two = shift(behind_one, 1), shift(ahead_two, -1)
    return ((one, two), (behind_one, behind_two), (ahead_one, ahead_two), (far_one, far_two))


def expert_terms(blocks, term):
    terms = [term(block, place) for place, block in enumerate(blocks[:3])]
    sides = (terms[1][0].astype(LOW), terms[2][1].astype(LOW))
    far, sides = lax.optimization_barrier((blocks[3], sides))
    return terms + [term(far, 3), sides]


def to_tokens(own, behind, ahead, far, sides, block, extra):
    step_one, step_two = shift(far[0].astype(LOW), 1), shift(far[1].astype(LOW), -1)
    side_one, side_two = shift(sides[0], -1), shift(sides[1], 1)
    last_one = shift((ahead[0] + step_one.astype(WIDE)).astype(LOW), 1)
    last_two = shift((behind[1] + step_two.astype(WIDE)).astype(LOW), -1)
    last_one, last_two, extra = lax.optimization_barrier((last_one, last_two, extra))
    folded = local(fold_kernel, block, own[0], side_one, last_one, own[1], side_two, last_two)
    return to_experts(folded), extra


def per_device(
    states, routes, lengths, router, w_in, w_out, w_query, w_key, w_value, w_output, cotangent
):
    section = lax.axis_index("section")
    encoder_side = section == 0
    tokens_here = states[0]
    routes_here = routes[0]
    router_here = router[0]
    first_weight = w_in[0, 0]
    second_weight = w_out[0, 0]
    cotangent_here = cotangent[0]
    tokens, columns = tokens_here.shape
    experts = router_here.shape[1]
    capacity = max(2, 5 * TOP * tokens // (4 * experts))
    half = columns // 2
    width = HEADS * HEAD
    slot_count = experts * STRIDE
    block = shaped((experts, FOLD * capacity, columns // FOLD), LOW)
    packed = pltpu.VMEM((slot_count, columns), LOW)

    folded, pick_one, pick_two, gate = local(
        dispatch_kernel,
        (block, shaped((tokens, slot_count), LOW), shaped((tokens, slot_count), LOW), shaped((tokens, 1), WIDE)),
        tokens_here,
        routes_here,
        router_here,
    )
    folded, w_query, w_key, w_value, w_output = lax.optimization_barrier(
        (folded, w_query, w_key, w_value, w_output)
    )
    own_a = jnp.where(encoder_side, w_key, w_query)
    output_wide = jnp.concatenate([w_output[:, :width], w_output[:, width:]], axis=0)
    own_b = jnp.where(encoder_side, w_value, output_wide)
    dense = jnp.concatenate([own_a, own_b], axis=0)
    dense = local(
        planes_kernel,
        shaped((lax.axis_size("dp"),) + dense.shape, LOW),
        lax.axis_index("dp").reshape(1, 1),
        dense,
        shift(dense, 1),
        shift(dense, -1),
        shift(dense, 2),
        scalars=1,
    )
    blocks = to_holders(folded)
    dense, waited = lax.optimization_barrier((dense, blocks[0][0]))
    blocks = ((waited, blocks[0][1]),) + blocks[1:]
    dense = lax.all_gather(dense, "expert", axis=0, tiled=True)
    dense = dense.reshape(lax.axis_size("expert"), lax.axis_size("dp"), -1, width)

    actives = []

    def forward_term(rows, place):
        pre = dot(rows[0], first_weight[:half]) + dot(rows[1], first_weight[half:])
        active = jnp.maximum(pre, 0.0).astype(LOW)
        actives.append(active)
        return dot(active, second_weight[:, :half]), dot(active, second_weight[:, half:])

    terms = expert_terms(blocks, forward_term)
    back, dense = to_tokens(*terms, block, dense)
    full_a, full_value, full_left, full_right = arrange(dense)

    hidden_state, normed_out = local(
        combine_kernel,
        (shaped((tokens, columns), WIDE), shaped((tokens, columns), LOW)),
        back,
        tokens_here,
        pick_one,
        pick_two,
        gate,
        scratch=(packed,),
    )
    own_length = jnp.where(encoder_side, lengths[0, 0], lengths[1, 0])
    live = jnp.arange(LEN, dtype=jnp.int32)[:, None] < own_length
    out_low = jnp.where(live & ~encoder_side, cotangent_here, jnp.zeros((), LOW))
    context_grad = (
        dot_nt(out_low[:, :half], full_left) + dot_nt(out_low[:, half:], full_right)
    ).astype(LOW)

    own_rows = dot(normed_out, full_a).astype(LOW)
    own_rows, later = lax.optimization_barrier((own_rows, normed_out))
    own_values = dot(later, full_value).astype(LOW)
    key_rows = lax.ppermute(own_rows, "section", [(0, 1)])
    value_rows = lax.ppermute(own_values, "section", [(0, 1)])
    low_rows = shaped((tokens, width), LOW)
    attention, value_grad = local(
        attend_kernel,
        (shaped((HEADS, LEN, LEN), WIDE), low_rows),
        lengths[0].reshape(1, 1),
        own_rows,
        key_rows,
        context_grad,
        scalars=1,
    )
    value_back = lax.ppermute(value_grad, "section", [(1, 0)])
    query_grad, key_grad, context = local(
        attend_back_kernel,
        (low_rows,) * 3,
        attention,
        own_rows,
        key_rows,
        value_rows,
        context_grad,
    )
    key_back = lax.ppermute(key_grad, "section", [(1, 0)])
    attended = jnp.concatenate([dot(context, full_left), dot(context, full_right)], axis=1)
    decoder_out = (hidden_state + attended).astype(LOW)
    forward_out = jnp.where(encoder_side, normed_out, decoder_out)
    projection_back = dot_nt(jnp.where(encoder_side, key_back, query_grad), full_a) + dot_nt(
        value_back, full_value
    )
    flags = jnp.stack([own_length, encoder_side.astype(jnp.int32)])[None]
    upstream, folded = local(
        upstream_kernel,
        (shaped((tokens, columns), WIDE), block),
        flags,
        hidden_state,
        projection_back,
        cotangent_here,
        pick_one,
        pick_two,
        gate,
        scalars=1,
    )
    sign_grad = local(
        router_kernel,
        shaped((tokens, experts), WIDE),
        back,
        upstream,
        routes_here,
        pick_one,
        pick_two,
        gate,
        scratch=(packed,),
    )

    def backward_term(rows, place):
        slope = dot_nt(rows[0], second_weight[:, :half]) + dot_nt(rows[1], second_weight[:, half:])
        slope = jnp.where(actives[place] > 0, slope, 0.0).astype(LOW)
        return dot_nt(slope, first_weight[:half]), dot_nt(slope, first_weight[half:])

    terms = expert_terms(to_holders(folded), backward_term)
    back, _ = to_tokens(*terms, block, ())
    grads = local(
        finish_kernel,
        shaped((tokens, columns), WIDE),
        back,
        tokens_here,
        upstream,
        sign_grad,
        router_here,
        pick_one,
        pick_two,
        scratch=(packed,),
    )
    return (forward_out[None], grads[None])


def solution(mesh):
    in_specs = (
        P("section", ("dp", "expert"), None),
        P("section", ("dp", "expert"), None),
        P(None, ("dp", "expert")),
        P("section", None, None),
        P("section", "expert", None, "dp"),
        P("section", "expert", "dp", None),
        P(("dp", "expert"), None),
        P(("dp", "expert"), None),
        P(("dp", "expert"), None),
        P(("dp", "expert"), None),
        P("section", ("dp", "expert"), None),
    )
    out_specs = (P("section", ("dp", "expert"), None), P("section", ("dp", "expert"), None))
    return jax.shard_map(
        per_device, mesh=mesh, in_specs=in_specs, out_specs=out_specs, check_vma=False
    )
```

```python
import functools

import jax
import jax.numpy as jnp
from jax import lax
from jax.experimental import pallas as pl
from jax.experimental.pallas import tpu as pltpu
from jax.sharding import PartitionSpec as P

HEADS = 8
HEAD = 128
TOP = 2
LEN = 128
STRIDE = 32
FOLD = 2
LANES = 128
PLANES = 4


EPS = 1e-05
NEG_FILL = -1e30
LOW = jnp.bfloat16
WIDE = jnp.float32
VMEM = pl.BlockSpec(memory_space=pltpu.VMEM)
SMEM = pl.BlockSpec(memory_space=pltpu.SMEM)
PARAMS = pltpu.CompilerParams(vmem_limit_bytes=20 * 1024 * 1024)


def dot(a, b):
    return jnp.dot(a, b, preferred_element_type=WIDE)


def dot_nt(a, b):
    return lax.dot_general(a, b, (((1,), (1,)), ((), ())), preferred_element_type=WIDE)


def dot_tn(a, b):
    return lax.dot_general(a, b, (((0,), (0,)), ((), ())), preferred_element_type=WIDE)


def normalised(values):
    centred = values - jnp.mean(values, axis=-1, keepdims=True)
    variance = jnp.mean(centred * centred, axis=-1, keepdims=True)
    inverse = lax.rsqrt(variance + EPS)
    return centred * inverse, inverse


def norm_back(values, upstream):
    normed, inverse = normalised(values)
    return inverse * (
        upstream
        - jnp.mean(upstream, axis=-1, keepdims=True)
        - normed * jnp.mean(upstream * normed, axis=-1, keepdims=True)
    )


def route_hots(routes, experts):
    ids = lax.broadcasted_iota(jnp.int32, (routes.shape[0], experts), 1)
    return routes[:, 0:1] == ids, routes[:, 1:2] == ids


def spread_rows(rows, folded_ref):
    experts, stack, columns = folded_ref.shape
    capacity = stack // FOLD
    for e in range(experts):
        block = rows[e * STRIDE : e * STRIDE + capacity].astype(LOW)
        for place in range(FOLD):
            folded_ref[e, pl.ds(place * capacity, capacity), :] = block[
                :, place * columns : (place + 1) * columns
            ]


def pack_rows(folded_ref, packed):
    experts, stack, columns = folded_ref.shape
    capacity = stack // FOLD
    packed[...] = jnp.zeros_like(packed)
    for e in range(experts):
        for place in range(FOLD):
            packed[pl.ds(e * STRIDE, capacity), pl.ds(place * columns, columns)] = folded_ref[
                e, pl.ds(place * capacity, capacity), :
            ]


def unfold_kernel(folded_ref, rows_ref, *, begin):
    experts, stack, columns = folded_ref.shape
    capacity = stack // FOLD
    for e in range(experts):
        for place in range(FOLD // 2):
            rows_ref[pl.ds(e * capacity, capacity), pl.ds(place * columns, columns)] = folded_ref[
                e, pl.ds((begin + place) * capacity, capacity), :
            ]


def fold_kernel(*refs):
    folded_ref = refs[-1]
    experts, stack, columns = folded_ref.shape
    capacity = stack // FOLD
    for begin in range(2):
        own_ref, side_ref, last_ref = refs[begin * 3 : begin * 3 + 3]
        total = own_ref[...] + side_ref[...].astype(WIDE) + last_ref[...].astype(WIDE)
        total = total.astype(LOW)
        for e in range(experts):
            for place in range(FOLD // 2):
                folded_ref[e, pl.ds((begin * FOLD // 2 + place) * capacity, capacity), :] = total[
                    e * capacity : (e + 1) * capacity, place * columns : (place + 1) * columns
                ]


def planes_kernel(place_ref, own_ref, behind_ref, ahead_ref, far_ref, planes_ref):
    count = planes_ref.shape[0]
    for distance, ref in ((0, own_ref), (count - 1, behind_ref), (1, ahead_ref), (2, far_ref)):
        planes_ref[lax.rem(place_ref[0, 0] + distance, count)] = ref[...]


def dense_kernel(dense_ref, first_ref, second_ref, left_ref, right_ref):
    experts, _, double, width = dense_ref.shape
    rows = double // 2
    first_ref[...] = dense_ref[:, 0, :rows].reshape(experts * rows, width)
    second = dense_ref[:, 0, rows:]
    second_ref[...] = second.reshape(experts * rows, width)
    left_ref[...] = second[:, : rows // 2].reshape(experts * rows // 2, width)
    right_ref[...] = second[:, rows // 2 :].reshape(experts * rows // 2, width)


def laned(columns):
    lane = lax.broadcasted_iota(jnp.int32, (columns[0].shape[0], LANES), 1)
    return sum(jnp.where(lane == place, column, 0.0) for place, column in enumerate(columns))


def split_low(column, parts):
    pieces = []
    for _ in range(parts):
        piece = column.astype(LOW).astype(WIDE)
        pieces.append(piece)
        column = column - piece
    return pieces


def plane_facts(block_refs):
    width = block_refs[0].shape[1]
    return jnp.concatenate([ref[:, width - LANES :] for ref in block_refs], axis=0).astype(WIDE)


def near_hots(facts, experts):
    place = lax.broadcasted_iota(jnp.int32, (facts.shape[0], experts * STRIDE), 1)
    return tuple(
        jnp.where(place == (facts[:, at : at + 1] * STRIDE + facts[:, at + 1 : at + 2]).astype(jnp.int32), 1.0, 0.0)
        for at in (0, 2)
    )


def route_signs(facts, experts):
    ids = lax.broadcasted_iota(jnp.int32, (facts.shape[0], experts), 1).astype(WIDE)
    return jnp.where(facts[:, 0:1] == ids, 1.0, 0.0) - jnp.where(facts[:, 2:3] == ids, 1.0, 0.0)


def plane_hots(facts, slots, capacity):
    tokens = facts.shape[0]
    plane = lax.broadcasted_iota(jnp.int32, (tokens, 1), 0) // (tokens // PLANES)
    place = lax.broadcasted_iota(jnp.int32, (tokens, slots), 1)

    def hot(route, rank):
        wanted = (route * (PLANES * capacity) + rank).astype(jnp.int32) + plane * capacity
        return jnp.where(place == wanted, 1.0, 0.0)

    return hot(facts[:, 0:1], facts[:, 1:2]), hot(facts[:, 2:3], facts[:, 3:4])


def plane_gates(facts):
    return facts[:, 4:5] + facts[:, 5:6] + facts[:, 6:7]


def stacked(refs, width):
    return jnp.concatenate([ref[:, :width] for ref in refs], axis=0)


def dispatch_kernel(states_ref, routes_ref, router_ref, folded_ref, block_ref):
    experts = folded_ref.shape[0]
    near = folded_ref.shape[2] * FOLD
    tokens, columns = states_ref.shape
    normed = normalised(states_ref[...].astype(WIDE))[0].astype(LOW)
    logits = dot(normed, router_ref[...])
    routes = routes_ref[...]
    hot_one, hot_two = route_hots(routes, experts)
    spread = jnp.sum(
        jnp.where(hot_one, logits, 0.0) - jnp.where(hot_two, logits, 0.0), axis=1, keepdims=True
    )
    gate = jax.nn.sigmoid(spread)
    named = jnp.where(hot_one | hot_two, 1.0, 0.0).astype(LOW)
    row = lax.broadcasted_iota(jnp.int32, (tokens, tokens), 0)
    column = lax.broadcasted_iota(jnp.int32, (tokens, tokens), 1)
    earlier = jnp.where(column < row, 1.0, 0.0).astype(LOW)
    rank = dot(earlier, named)
    rank_one = jnp.sum(jnp.where(hot_one, rank, 0.0), axis=1, keepdims=True)
    rank_two = jnp.sum(jnp.where(hot_two, rank, 0.0), axis=1, keepdims=True)
    facts = [routes[:, 0:1].astype(WIDE), rank_one, routes[:, 1:2].astype(WIDE), rank_two]
    facts = laned(facts + split_low(gate, 3))
    block_ref[:, : columns - near] = normed[:, near:]
    block_ref[:, columns - near :] = facts.astype(LOW)
    one, two = near_hots(facts, experts)
    spread_rows(dot_tn((one + two).astype(LOW), normed[:, :near]), folded_ref)


def plane_dispatch_kernel(own_ref, behind_ref, ahead_ref, far_ref, slots_ref):
    experts, rows, width = slots_ref.shape
    refs = (own_ref, behind_ref, ahead_ref, far_ref)
    one, two = plane_hots(plane_facts(refs), experts * rows, rows // PLANES)
    spread = dot_tn((one + two).astype(LOW), stacked(refs, width))
    slots_ref[...] = spread.astype(LOW).reshape(slots_ref.shape)


def plane_combine_kernel(slots_ref, own_ref, behind_ref, ahead_ref, far_ref, sum_ref, to_behind_ref, to_ahead_ref, to_far_ref, apart_ref):
    experts, rows, width = slots_ref.shape
    facts = plane_facts((own_ref, behind_ref, ahead_ref, far_ref))
    one, two = plane_hots(facts, experts * rows, rows // PLANES)
    table = slots_ref[...].reshape(experts * rows, width)
    first, second = dot(one.astype(LOW), table), dot(two.astype(LOW), table)
    gate = plane_gates(facts)
    apart_ref[...] = first - second
    mixed = gate * first + (1.0 - gate) * second
    tokens = sum_ref.shape[0]
    sum_ref[...] = mixed[:tokens]
    for place, ref in enumerate((to_behind_ref, to_ahead_ref, to_far_ref)):
        ref[...] = mixed[(place + 1) * tokens : (place + 2) * tokens].astype(LOW)


def plane_slope_kernel(own_ref, behind_ref, ahead_ref, far_ref, up_own_ref, up_behind_ref, up_ahead_ref, up_far_ref, slots_ref):
    experts, rows, width = slots_ref.shape
    facts = plane_facts((own_ref, behind_ref, ahead_ref, far_ref))
    one, two = plane_hots(facts, experts * rows, rows // PLANES)
    gate = plane_gates(facts)
    up = stacked((up_own_ref, up_behind_ref, up_ahead_ref, up_far_ref), width).astype(WIDE)
    spread = dot_tn(one.astype(LOW), (gate * up).astype(LOW)) + dot_tn(
        two.astype(LOW), ((1.0 - gate) * up).astype(LOW)
    )
    slots_ref[...] = spread.astype(LOW).reshape(slots_ref.shape)


def plane_back_kernel(slots_ref, own_ref, behind_ref, ahead_ref, far_ref, up_own_ref, up_behind_ref, up_ahead_ref, up_far_ref, apart_ref, sum_ref, to_behind_ref, to_ahead_ref, to_far_ref):
    experts, rows, width = slots_ref.shape
    facts = plane_facts((own_ref, behind_ref, ahead_ref, far_ref))
    one, two = plane_hots(facts, experts * rows, rows // PLANES)
    table = slots_ref[...].reshape(experts * rows, width)
    back = dot((one + two).astype(LOW), table)
    up = stacked((up_own_ref, up_behind_ref, up_ahead_ref, up_far_ref), width).astype(WIDE)
    gate_grad = jnp.sum(up * apart_ref[...], axis=1, keepdims=True)
    extra = laned(split_low(gate_grad, 2))
    tokens = sum_ref.shape[0]
    for place, ref in enumerate((sum_ref, to_behind_ref, to_ahead_ref, to_far_ref)):
        at = slice(place * tokens, (place + 1) * tokens)
        ref[:, :width] = back[at].astype(ref.dtype)
        ref[:, width:] = extra[at].astype(ref.dtype)


def unpack_kernel(slots_ref, *plane_refs):
    experts, rows, _ = slots_ref.shape
    capacity = rows // PLANES
    for e in range(experts):
        for place, ref in enumerate(plane_refs):
            ref[pl.ds(e * capacity, capacity), :] = slots_ref[e, pl.ds(place * capacity, capacity), :]


def pack_kernel(*refs):
    plane_refs, slots_ref = refs[:-1], refs[-1]
    experts, rows, _ = slots_ref.shape
    capacity = rows // PLANES
    for e in range(experts):
        for place, ref in enumerate(plane_refs):
            slots_ref[e, pl.ds(place * capacity, capacity), :] = ref[pl.ds(e * capacity, capacity), :]


def combine_kernel(folded_ref, states_ref, block_ref, own_ref, behind_ref, ahead_ref, far_ref, hidden_ref, normed_ref, packed):
    pack_rows(folded_ref, packed)
    rows = packed[...]
    near = rows.shape[1]
    facts = plane_facts((block_ref,))
    gate = plane_gates(facts)
    one, two = near_hots(facts, folded_ref.shape[0])
    mixed = gate * dot(one.astype(LOW), rows) + (1.0 - gate) * dot(two.astype(LOW), rows)
    others = own_ref[...] + behind_ref[...].astype(WIDE)
    others = others + ahead_ref[...].astype(WIDE) + far_ref[...].astype(WIDE)
    hidden_ref[:, :near] = states_ref[:, :near].astype(WIDE) + mixed
    hidden_ref[:, near:] = states_ref[:, near:].astype(WIDE) + others
    normed_ref[...] = normalised(hidden_ref[...])[0].astype(LOW)


def attend_kernel(length_ref, q_ref, k_ref, grad_ref, attention_ref, v_grad_ref):
    scale = HEAD ** (-0.5)
    live = lax.broadcasted_iota(jnp.int32, (LEN, LEN), 1) < length_ref[0, 0]
    for head in range(HEADS):
        at = slice(head * HEAD, (head + 1) * HEAD)
        scores = jnp.where(live, dot_nt(q_ref[:, at], k_ref[:, at]) * scale, NEG_FILL)
        exponent = jnp.exp(scores - jnp.max(scores, axis=-1, keepdims=True))
        attention = exponent / jnp.sum(exponent, axis=-1, keepdims=True)
        attention_ref[head] = attention
        v_grad_ref[:, at] = dot_tn(attention.astype(LOW), grad_ref[:, at]).astype(LOW)


def attend_back_kernel(attention_ref, q_ref, k_ref, v_ref, grad_ref, q_grad_ref, k_grad_ref, context_ref):
    scale = HEAD ** (-0.5)
    for head in range(HEADS):
        at = slice(head * HEAD, (head + 1) * HEAD)
        attention, v = attention_ref[head], v_ref[:, at]
        weight_grad = dot_nt(grad_ref[:, at], v)
        score_grad = (
            attention
            * (weight_grad - jnp.sum(attention * weight_grad, axis=-1, keepdims=True))
            * scale
        ).astype(LOW)
        k_grad_ref[:, at] = dot_tn(score_grad, q_ref[:, at]).astype(LOW)
        q_grad_ref[:, at] = dot(score_grad, k_ref[:, at]).astype(LOW)
        context_ref[:, at] = dot(attention.astype(LOW), v).astype(LOW)


def upstream_kernel(flags_ref, hidden_ref, back_ref, cotangent_ref, block_ref, upstream_ref, folded_ref, up_ref):
    near = folded_ref.shape[2] * FOLD
    live = lax.broadcasted_iota(jnp.int32, (LEN, 1), 0) < flags_ref[0, 0]
    encoder = flags_ref[0, 1] == 1
    masked = jnp.where(live, cotangent_ref[...].astype(WIDE), 0.0)
    out_grad = jnp.where(encoder, 0.0, masked)
    normed_grad = back_ref[...] + jnp.where(encoder, masked, 0.0)
    upstream = out_grad + norm_back(hidden_ref[...], normed_grad)
    upstream_ref[...] = upstream
    up_ref[...] = upstream[:, near:].astype(LOW)
    facts = plane_facts((block_ref,))
    gate = plane_gates(facts)
    one, two = near_hots(facts, folded_ref.shape[0])
    rows = dot_tn(one.astype(LOW), (gate * upstream[:, :near]).astype(LOW)) + dot_tn(
        two.astype(LOW), ((1.0 - gate) * upstream[:, :near]).astype(LOW)
    )
    spread_rows(rows, folded_ref)


def gate_kernel(folded_ref, upstream_ref, block_ref, gate_grad_ref, packed):
    pack_rows(folded_ref, packed)
    rows = packed[...]
    one, two = near_hots(plane_facts((block_ref,)), folded_ref.shape[0])
    apart = dot(one.astype(LOW), rows) - dot(two.astype(LOW), rows)
    gate_grad_ref[...] = jnp.sum(
        upstream_ref[:, : rows.shape[1]] * apart, axis=1, keepdims=True
    )


def finish_kernel(folded_ref, states_ref, upstream_ref, gate_grad_ref, router_ref, block_ref, own_ref, behind_ref, ahead_ref, far_ref, grads_ref, packed, total):
    pack_rows(folded_ref, packed)
    rows = packed[...]
    near = rows.shape[1]
    far = total.shape[1] - near
    experts = folded_ref.shape[0]
    others = own_ref[...] + behind_ref[...].astype(WIDE)
    others = others + ahead_ref[...].astype(WIDE) + far_ref[...].astype(WIDE)
    facts = plane_facts((block_ref,))
    gate = plane_gates(facts)
    gate_grad = gate_grad_ref[...] + others[:, far : far + 1] + others[:, far + 1 : far + 2]
    logit_grad = gate_grad * gate * (1.0 - gate)
    router_term = lax.dot_general(
        logit_grad * route_signs(facts, experts),
        router_ref[...].astype(WIDE),
        (((1,), (1,)), ((), ())),
        precision=lax.Precision.HIGHEST,
        preferred_element_type=WIDE,
    )
    one, two = near_hots(facts, experts)
    total[:, :near] = dot((one + two).astype(LOW), rows) + router_term[:, :near]
    total[:, near:] = others[:, :far] + router_term[:, near:]
    grads_ref[...] = upstream_ref[...] + norm_back(states_ref[...].astype(WIDE), total[...])


def local(kernel, out_shape, *operands, scalars=0, scratch=()):
    single = not isinstance(out_shape, tuple)
    shapes = (out_shape,) if single else out_shape
    cost = sum(x.size * x.dtype.itemsize for x in operands) + sum(
        x.size * x.dtype.itemsize for x in shapes
    )
    result = pl.pallas_call(
        kernel,
        out_shape=shapes,
        in_specs=[SMEM] * scalars + [VMEM] * (len(operands) - scalars),
        out_specs=tuple([VMEM] * len(shapes)),
        scratch_shapes=list(scratch),
        compiler_params=PARAMS,
        cost_estimate=pl.CostEstimate(flops=10**9, bytes_accessed=4 * cost, transcendentals=0),
    )(*operands)
    return result[0] if single else result


def shaped(shape, dtype):
    return jax.ShapeDtypeStruct(shape, dtype)


def shift(block, distance):
    count = lax.axis_size("dp")
    return lax.ppermute(block, "dp", [(i, (i + distance) % count) for i in range(count)])


def to_experts(block):
    return lax.all_to_all(block, "expert", split_axis=0, concat_axis=0, tiled=True)


def arrange(dense):
    experts, planes, double, width = dense.shape
    rows = experts * double // 2

    def blocks(count):
        return pl.BlockSpec((count, width), lambda plane: (plane, 0))

    whole, part = shaped((planes * rows, width), LOW), shaped((planes * rows // 2, width), LOW)
    return pl.pallas_call(
        dense_kernel,
        grid=(planes,),
        out_shape=(whole, whole, part, part),
        in_specs=[pl.BlockSpec((experts, 1, double, width), lambda plane: (0, plane, 0, 0))],
        out_specs=(blocks(rows), blocks(rows), blocks(rows // 2), blocks(rows // 2)),
        compiler_params=PARAMS,
        cost_estimate=pl.CostEstimate(flops=10**6, bytes_accessed=20 * 2**20, transcendentals=0),
    )(dense)


def from_planes(block):
    return block, shift(block, 1), shift(block, -1), shift(block, 2)


def to_planes(own, behind, ahead, far):
    return own, shift(behind, -1), shift(ahead, 1), shift(far, 2)


def to_holders(folded, far_slots):
    experts, stack, columns = folded.shape
    rows = shaped((experts * stack // FOLD, columns * FOLD // 2), LOW)
    folded = to_experts(folded)
    one = local(functools.partial(unfold_kernel, begin=0), rows, folded)
    two = local(functools.partial(unfold_kernel, begin=FOLD // 2), rows, folded)
    one, two, far_slots = lax.optimization_barrier((one, two, far_slots))
    behind_one, ahead_one = shift(one, 1), shift(one, -1)
    behind_two, ahead_two = shift(two, 1), shift(two, -1)
    far_one, far_two = shift(behind_one, 1), shift(ahead_two, -1)
    tail = shaped((experts * stack // FOLD, far_slots.shape[2]), LOW)
    tails = local(unpack_kernel, (tail,) * PLANES, to_experts(far_slots))
    nears = ((one, two), (behind_one, behind_two), (ahead_one, ahead_two), (far_one, far_two))
    return [near + (tail,) for near, tail in zip(nears, tails)]


def expert_terms(blocks, term):
    terms = [term(block, place) for place, block in enumerate(blocks[:3])]
    sides = (terms[1][0].astype(LOW), terms[2][1].astype(LOW))
    far, sides = lax.optimization_barrier((blocks[3], sides))
    return terms + [term(far, 3), sides]


def to_tokens(own, behind, ahead, far, sides, block, far_block, extra):
    steps = (far[0].astype(LOW), far[1].astype(LOW))
    tails = tuple(term[2].astype(LOW) for term in (own, behind, ahead, far))
    steps, tails = lax.optimization_barrier((steps, tails))
    step_one, step_two = shift(steps[0], 1), shift(steps[1], -1)
    side_one, side_two = shift(sides[0], -1), shift(sides[1], 1)
    tails = to_experts(local(pack_kernel, far_block, *tails))
    last_one = shift((ahead[0] + step_one.astype(WIDE)).astype(LOW), 1)
    last_two = shift((behind[1] + step_two.astype(WIDE)).astype(LOW), -1)
    last_one, last_two, extra = lax.optimization_barrier((last_one, last_two, extra))
    folded = local(fold_kernel, block, own[0], side_one, last_one, own[1], side_two, last_two)
    return to_experts(folded), tails, extra


def per_device(
    states, routes, lengths, router, w_in, w_out, w_query, w_key, w_value, w_output, cotangent
):
    section = lax.axis_index("section")
    encoder_side = section == 0
    tokens_here = states[0]
    routes_here = routes[0]
    router_here = router[0]
    first_weight = w_in[0, 0]
    second_weight = w_out[0, 0]
    cotangent_here = cotangent[0]
    tokens, columns = tokens_here.shape
    experts = router_here.shape[1]
    capacity = max(2, 5 * TOP * tokens // (4 * experts))
    half = columns // 2
    width = HEADS * HEAD
    slot_count = experts * STRIDE
    far = columns // 4
    near = columns - far
    middle = near // 2
    near_slots = shaped((experts, FOLD * capacity, near // FOLD), LOW)
    far_slots = shaped((experts, PLANES * capacity, far), LOW)
    packed = pltpu.VMEM((slot_count, near), LOW)
    wide_rows = shaped((tokens, columns), WIDE)

    folded, block = local(
        dispatch_kernel,
        (near_slots, shaped((tokens, far + LANES), LOW)),
        tokens_here,
        routes_here,
        router_here,
    )
    blocks = from_planes(block)
    spread = local(plane_dispatch_kernel, far_slots, *blocks)
    folded, w_query, w_key, w_value, w_output = lax.optimization_barrier(
        (folded, w_query, w_key, w_value, w_output)
    )
    own_a = jnp.where(encoder_side, w_key, w_query)
    output_wide = jnp.concatenate([w_output[:, :width], w_output[:, width:]], axis=0)
    own_b = jnp.where(encoder_side, w_value, output_wide)
    dense = jnp.concatenate([own_a, own_b], axis=0)
    dense = local(
        planes_kernel,
        shaped((lax.axis_size("dp"),) + dense.shape, LOW),
        lax.axis_index("dp").reshape(1, 1),
        dense,
        shift(dense, 1),
        shift(dense, -1),
        shift(dense, 2),
        scalars=1,
    )
    rows = to_holders(folded, spread)
    dense, waited = lax.optimization_barrier((dense, rows[0][0]))
    rows[0] = (waited,) + rows[0][1:]
    dense = lax.all_gather(dense, "expert", axis=0, tiled=True)
    dense = dense.reshape(lax.axis_size("expert"), lax.axis_size("dp"), -1, width)

    actives = []

    edges = (slice(0, middle), slice(middle, near), slice(near, columns))

    def forward_term(rows, place):
        pre = sum(dot(part, first_weight[edge]) for part, edge in zip(rows, edges))
        active = jnp.maximum(pre, 0.0).astype(LOW)
        actives.append(active)
        return tuple(dot(active, second_weight[:, edge]) for edge in edges)

    terms = expert_terms(rows, forward_term)
    back, far_back, dense = to_tokens(*terms, near_slots, far_slots, dense)
    full_a, full_value, full_left, full_right = arrange(dense)
    far_low = shaped((tokens, far), LOW)
    *far_sums, apart = local(
        plane_combine_kernel,
        (shaped((tokens, far), WIDE), far_low, far_low, far_low, shaped((PLANES * tokens, far), WIDE)),
        far_back,
        *blocks,
    )
    hidden_state, normed_out = local(
        combine_kernel,
        (wide_rows, shaped((tokens, columns), LOW)),
        back,
        tokens_here,
        block,
        *to_planes(*far_sums),
        scratch=(packed,),
    )
    own_length = jnp.where(encoder_side, lengths[0, 0], lengths[1, 0])
    live = jnp.arange(LEN, dtype=jnp.int32)[:, None] < own_length
    out_low = jnp.where(live & ~encoder_side, cotangent_here, jnp.zeros((), LOW))
    context_grad = (
        dot_nt(out_low[:, :half], full_left) + dot_nt(out_low[:, half:], full_right)
    ).astype(LOW)

    own_rows = dot(normed_out, full_a).astype(LOW)
    own_rows, later = lax.optimization_barrier((own_rows, normed_out))
    own_values = dot(later, full_value).astype(LOW)
    key_rows = lax.ppermute(own_rows, "section", [(0, 1)])
    value_rows = lax.ppermute(own_values, "section", [(0, 1)])
    low_rows = shaped((tokens, width), LOW)
    attention, value_grad = local(
        attend_kernel,
        (shaped((HEADS, LEN, LEN), WIDE), low_rows),
        lengths[0].reshape(1, 1),
        own_rows,
        key_rows,
        context_grad,
        scalars=1,
    )
    value_back = lax.ppermute(value_grad, "section", [(1, 0)])
    query_grad, key_grad, context = local(
        attend_back_kernel,
        (low_rows,) * 3,
        attention,
        own_rows,
        key_rows,
        value_rows,
        context_grad,
    )
    key_back = lax.ppermute(key_grad, "section", [(1, 0)])
    attended = jnp.concatenate([dot(context, full_left), dot(context, full_right)], axis=1)
    decoder_out = (hidden_state + attended).astype(LOW)
    forward_out = jnp.where(encoder_side, normed_out, decoder_out)
    projection_back = dot_nt(jnp.where(encoder_side, key_back, query_grad), full_a) + dot_nt(
        value_back, full_value
    )
    flags = jnp.stack([own_length, encoder_side.astype(jnp.int32)])[None]
    upstream, folded, up = local(
        upstream_kernel,
        (wide_rows, near_slots, far_low),
        flags,
        hidden_state,
        projection_back,
        cotangent_here,
        block,
        scalars=1,
    )
    gate_grad = local(
        gate_kernel, shaped((tokens, 1), WIDE), back, upstream, block, scratch=(packed,)
    )
    ups = from_planes(up)
    rows = to_holders(folded, local(plane_slope_kernel, far_slots, *blocks, *ups))

    def backward_term(rows, place):
        slope = sum(dot_nt(part, second_weight[:, edge]) for part, edge in zip(rows, edges))
        slope = jnp.where(actives[place] > 0, slope, 0.0).astype(LOW)
        return tuple(dot_nt(slope, first_weight[edge]) for edge in edges)

    terms = expert_terms(rows, backward_term)
    back, far_back, _ = to_tokens(*terms, near_slots, far_slots, ())
    far_low = shaped((tokens, far + LANES), LOW)
    far_sums = local(
        plane_back_kernel,
        (shaped((tokens, far + LANES), WIDE), far_low, far_low, far_low),
        far_back,
        *blocks,
        *ups,
        apart,
    )
    grads = local(
        finish_kernel,
        wide_rows,
        back,
        tokens_here,
        upstream,
        gate_grad,
        router_here,
        block,
        *to_planes(*far_sums),
        scratch=(packed, pltpu.VMEM((tokens, columns), WIDE)),
    )
    return (forward_out[None], grads[None])


def solution(mesh):
    in_specs = (
        P("section", ("dp", "expert"), None),
        P("section", ("dp", "expert"), None),
        P(None, ("dp", "expert")),
        P("section", None, None),
        P("section", "expert", None, "dp"),
        P("section", "expert", "dp", None),
        P(("dp", "expert"), None),
        P(("dp", "expert"), None),
        P(("dp", "expert"), None),
        P(("dp", "expert"), None),
        P("section", ("dp", "expert"), None),
    )
    out_specs = (P("section", ("dp", "expert"), None), P("section", ("dp", "expert"), None))
    return jax.shard_map(
        per_device, mesh=mesh, in_specs=in_specs, out_specs=out_specs, check_vma=False
    )
```

```python
import functools

import jax
import jax.numpy as jnp
from jax import lax
from jax.experimental import pallas as pl
from jax.experimental.pallas import tpu as pltpu
from jax.sharding import PartitionSpec as P

HEADS = 8
HEAD = 128
TOP = 2
LEN = 128
STRIDE = 32
FOLD = 4
LANES = 128


EPS = 1e-05
NEG_FILL = -1e30
LOW = jnp.bfloat16
WIDE = jnp.float32
VMEM = pl.BlockSpec(memory_space=pltpu.VMEM)
SMEM = pl.BlockSpec(memory_space=pltpu.SMEM)
PARAMS = pltpu.CompilerParams(vmem_limit_bytes=20 * 1024 * 1024)


def dot(a, b):
    return jnp.dot(a, b, preferred_element_type=WIDE)


def dot_nt(a, b):
    return lax.dot_general(a, b, (((1,), (1,)), ((), ())), preferred_element_type=WIDE)


def dot_tn(a, b):
    return lax.dot_general(a, b, (((0,), (0,)), ((), ())), preferred_element_type=WIDE)


def normalised(values):
    centred = values - jnp.mean(values, axis=-1, keepdims=True)
    variance = jnp.mean(centred * centred, axis=-1, keepdims=True)
    inverse = lax.rsqrt(variance + EPS)
    return centred * inverse, inverse


def norm_back(values, upstream):
    normed, inverse = normalised(values)
    return inverse * (
        upstream
        - jnp.mean(upstream, axis=-1, keepdims=True)
        - normed * jnp.mean(upstream * normed, axis=-1, keepdims=True)
    )


class Late:
    def __init__(self, source, held, semaphore):
        self.copy = pltpu.make_async_copy(source, held, semaphore)
        self.held, self.shape, self.dtype, self.waiting = held, held.shape, held.dtype, True
        self.copy.start()

    def __getitem__(self, index):
        if self.waiting:
            self.copy.wait()
            self.waiting = False
        return self.held[index]


class Sent:
    def __init__(self, target, held, semaphore):
        self.copy = pltpu.make_async_copy(held, target, semaphore)
        self.held, self.shape, self.dtype = held, held.shape, held.dtype

    def __setitem__(self, index, value):
        self.held[index] = value

    def send(self):
        self.copy.start()


def laned(columns):
    lane = lax.broadcasted_iota(jnp.int32, (columns[0].shape[0], LANES), 1)
    return sum(jnp.where(lane == place, column, 0.0) for place, column in enumerate(columns))


def slot_hots(facts, experts):
    place = lax.broadcasted_iota(jnp.int32, (facts.shape[0], experts * STRIDE), 1)
    return tuple(
        jnp.where(place == (facts[:, at : at + 1] * STRIDE + facts[:, at + 1 : at + 2]).astype(jnp.int32), 1.0, 0.0)
        for at in (0, 2)
    )


def route_signs(facts, experts):
    ids = lax.broadcasted_iota(jnp.int32, (facts.shape[0], experts), 1).astype(WIDE)
    return jnp.where(facts[:, 0:1] == ids, 1.0, 0.0) - jnp.where(facts[:, 2:3] == ids, 1.0, 0.0)


def spread_rows(rows, folded_ref):
    experts, stack, columns = folded_ref.shape
    capacity = stack // FOLD
    for e in range(experts):
        block = rows[e * STRIDE : e * STRIDE + capacity].astype(LOW)
        for place in range(FOLD):
            folded_ref[e, pl.ds(place * capacity, capacity), :] = block[
                :, place * columns : (place + 1) * columns
            ]


def pack_rows(folded_ref, packed):
    experts, stack, columns = folded_ref.shape
    capacity = stack // FOLD
    packed[...] = jnp.zeros_like(packed)
    for e in range(experts):
        for place in range(FOLD):
            packed[pl.ds(e * STRIDE, capacity), pl.ds(place * columns, columns)] = folded_ref[
                e, pl.ds(place * capacity, capacity), :
            ]


def unfold_kernel(folded_ref, rows_ref, *, begin):
    experts, stack, columns = folded_ref.shape
    capacity = stack // FOLD
    for e in range(experts):
        for place in range(FOLD // 2):
            rows_ref[pl.ds(e * capacity, capacity), pl.ds(place * columns, columns)] = folded_ref[
                e, pl.ds((begin + place) * capacity, capacity), :
            ]


def fold_kernel(*refs):
    folded_ref = refs[-1]
    experts, stack, columns = folded_ref.shape
    capacity = stack // FOLD
    for begin in range(2):
        own_ref, side_ref, last_ref = refs[begin * 3 : begin * 3 + 3]
        total = own_ref[...] + side_ref[...].astype(WIDE) + last_ref[...].astype(WIDE)
        total = total.astype(LOW)
        for e in range(experts):
            for place in range(FOLD // 2):
                folded_ref[e, pl.ds((begin * FOLD // 2 + place) * capacity, capacity), :] = total[
                    e * capacity : (e + 1) * capacity, place * columns : (place + 1) * columns
                ]


def planes_kernel(place_ref, own_ref, behind_ref, ahead_ref, far_ref, planes_ref):
    count = planes_ref.shape[0]
    for distance, ref in ((0, own_ref), (count - 1, behind_ref), (1, ahead_ref), (2, far_ref)):
        planes_ref[lax.rem(place_ref[0, 0] + distance, count)] = ref[...]


def dense_kernel(dense_ref, first_ref, second_ref, left_ref, right_ref):
    experts, _, double, width = dense_ref.shape
    rows = double // 2
    first_ref[...] = dense_ref[:, 0, :rows].reshape(experts * rows, width)
    second = dense_ref[:, 0, rows:]
    second_ref[...] = second.reshape(experts * rows, width)
    left_ref[...] = second[:, : rows // 2].reshape(experts * rows // 2, width)
    right_ref[...] = second[:, rows // 2 :].reshape(experts * rows // 2, width)


def dispatch_kernel(states_ref, routes_ref, router_ref, folded_ref, facts_ref):
    experts = folded_ref.shape[0]
    tokens = states_ref.shape[0]
    ids = lax.broadcasted_iota(jnp.int32, (experts, tokens), 0)
    row = lax.broadcasted_iota(jnp.int32, (experts, experts), 0)
    column = lax.broadcasted_iota(jnp.int32, (experts, experts), 1)
    same = jnp.where(row == column, 1.0, 0.0).astype(LOW)
    hots = [
        dot_tn(jnp.where(routes_ref[k : k + 1, :] == ids, 1.0, 0.0).astype(LOW), same)
        for k in range(TOP)
    ]
    row = lax.broadcasted_iota(jnp.int32, (tokens, tokens), 0)
    column = lax.broadcasted_iota(jnp.int32, (tokens, tokens), 1)
    earlier = jnp.where(column < row, 1.0, 0.0).astype(LOW)
    rank = dot(earlier, (hots[0] + hots[1]).astype(LOW))
    number = lax.broadcasted_iota(jnp.int32, (tokens, experts), 1).astype(WIDE)
    facts = []
    for hot in hots:
        facts.append(jnp.sum(hot * number, axis=1, keepdims=True))
        facts.append(jnp.sum(hot * rank, axis=1, keepdims=True))
    normed = normalised(states_ref[...].astype(WIDE))[0].astype(LOW)
    logits = dot_nt(normed, router_ref[...])
    spread = jnp.sum(hots[0] * logits - hots[1] * logits, axis=1, keepdims=True)
    facts = laned(facts + [jax.nn.sigmoid(spread)])
    facts_ref[...] = facts
    one, two = slot_hots(facts, experts)
    spread_rows(dot_tn((one + two).astype(LOW), normed), folded_ref)


def combine_kernel(folded_ref, states_ref, facts_ref, hidden_ref, normed_ref, packed):
    pack_rows(folded_ref, packed)
    rows = packed[...]
    facts = facts_ref[...]
    gate = facts[:, 4:5]
    one, two = slot_hots(facts, folded_ref.shape[0])
    hidden = states_ref[...].astype(WIDE) + (
        gate * dot(one.astype(LOW), rows) + (1.0 - gate) * dot(two.astype(LOW), rows)
    )
    hidden_ref[...] = hidden
    hidden_ref.send()
    normed_ref[...] = normalised(hidden)[0].astype(LOW)


def attend_kernel(length_ref, q_ref, k_ref, grad_ref, attention_ref, v_grad_ref):
    scale = HEAD ** (-0.5)
    live = lax.broadcasted_iota(jnp.int32, (LEN, LEN), 1) < length_ref[0, 0]
    for head in range(HEADS):
        at = slice(head * HEAD, (head + 1) * HEAD)
        scores = jnp.where(live, dot_nt(q_ref[:, at], k_ref[:, at]) * scale, NEG_FILL)
        exponent = jnp.exp(scores - jnp.max(scores, axis=-1, keepdims=True))
        attention = exponent / jnp.sum(exponent, axis=-1, keepdims=True)
        attention_ref[head] = attention
        v_grad_ref[:, at] = dot_tn(attention.astype(LOW), grad_ref[:, at]).astype(LOW)
    attention_ref.send()


def attend_back_kernel(attention_ref, q_ref, k_ref, v_ref, grad_ref, q_grad_ref, k_grad_ref, context_ref):
    scale = HEAD ** (-0.5)
    for head in range(HEADS):
        at = slice(head * HEAD, (head + 1) * HEAD)
        attention, v = attention_ref[head], v_ref[:, at]
        weight_grad = dot_nt(grad_ref[:, at], v)
        score_grad = (
            attention
            * (weight_grad - jnp.sum(attention * weight_grad, axis=-1, keepdims=True))
            * scale
        ).astype(LOW)
        k_grad_ref[:, at] = dot_tn(score_grad, q_ref[:, at]).astype(LOW)
        q_grad_ref[:, at] = dot(score_grad, k_ref[:, at]).astype(LOW)
        context_ref[:, at] = dot(attention.astype(LOW), v).astype(LOW)


def upstream_kernel(flags_ref, hidden_ref, back_ref, cotangent_ref, facts_ref, upstream_ref, folded_ref):
    live = lax.broadcasted_iota(jnp.int32, (LEN, 1), 0) < flags_ref[0, 0]
    encoder = flags_ref[0, 1] == 1
    masked = jnp.where(live, cotangent_ref[...].astype(WIDE), 0.0)
    out_grad = jnp.where(encoder, 0.0, masked)
    normed_grad = back_ref[...] + jnp.where(encoder, masked, 0.0)
    upstream = out_grad + norm_back(hidden_ref[...], normed_grad)
    upstream_ref[...] = upstream
    upstream_ref.send()
    facts = facts_ref[...]
    gate = facts[:, 4:5]
    one, two = slot_hots(facts, folded_ref.shape[0])
    rows = dot_tn(one.astype(LOW), (gate * upstream).astype(LOW)) + dot_tn(
        two.astype(LOW), ((1.0 - gate) * upstream).astype(LOW)
    )
    spread_rows(rows, folded_ref)


def router_kernel(folded_ref, upstream_ref, facts_ref, sign_ref, packed):
    pack_rows(folded_ref, packed)
    rows = packed[...]
    facts = facts_ref[...]
    gate = facts[:, 4:5]
    one, two = slot_hots(facts, folded_ref.shape[0])
    apart = dot(one.astype(LOW), rows) - dot(two.astype(LOW), rows)
    gate_grad = jnp.sum(upstream_ref[...] * apart, axis=1, keepdims=True)
    logit_grad = gate_grad * gate * (1.0 - gate)
    sign_ref[...] = logit_grad * route_signs(facts, folded_ref.shape[0])


def finish_kernel(folded_ref, states_ref, upstream_ref, sign_ref, router_ref, facts_ref, grads_ref, packed):
    pack_rows(folded_ref, packed)
    one, two = slot_hots(facts_ref[...], folded_ref.shape[0])
    back = dot((one + two).astype(LOW), packed[...])
    router_term = jnp.dot(
        sign_ref[...],
        router_ref[...].astype(WIDE),
        precision=lax.Precision.HIGHEST,
        preferred_element_type=WIDE,
    )
    input_total = back + router_term
    grads_ref[...] = upstream_ref[...] + norm_back(states_ref[...].astype(WIDE), input_total)


def local(kernel, out_shape, *operands, scalars=0, scratch=(), late=(), sent=()):
    single = not isinstance(out_shape, tuple)
    shapes = (out_shape,) if single else out_shape
    count = len(operands)
    total = count + len(shapes)
    moved = [place for place in range(count) if place in late]
    moved += [count + place for place in range(len(shapes)) if place in sent]
    both = list(operands) + list(shapes)

    def body(*refs):
        refs, extra = list(refs[:total]), refs[total:]
        held, semaphores = extra[: len(moved)], extra[len(moved)] if moved else None
        for number, place in enumerate(moved):
            made = Late if place < count else Sent
            refs[place] = made(refs[place], held[number], semaphores.at[number])
        kernel(*refs, *extra[len(moved) + (1 if moved else 0) :])
        for place in moved:
            if place >= count:
                refs[place].copy.wait()

    scratches = [pltpu.VMEM(both[place].shape, both[place].dtype) for place in moved]
    if moved:
        scratches.append(pltpu.SemaphoreType.DMA((len(moved),)))
    specs = [SMEM] * scalars + [VMEM] * (total - scalars)
    for place in moved:
        specs[place] = pl.BlockSpec(memory_space=pl.ANY)
    cost = sum(x.size * x.dtype.itemsize for x in both)
    result = pl.pallas_call(
        body,
        out_shape=shapes,
        in_specs=specs[:count],
        out_specs=tuple(specs[count:]),
        scratch_shapes=scratches + list(scratch),
        compiler_params=PARAMS,
        cost_estimate=pl.CostEstimate(flops=10**9, bytes_accessed=4 * cost, transcendentals=0),
    )(*operands)
    return result[0] if single else result


def shaped(shape, dtype):
    return jax.ShapeDtypeStruct(shape, dtype)


def shift(block, distance):
    count = lax.axis_size("dp")
    return lax.ppermute(block, "dp", [(i, (i + distance) % count) for i in range(count)])


def to_experts(block):
    return lax.all_to_all(block, "expert", split_axis=0, concat_axis=0, tiled=True)


def arrange(dense):
    experts, planes, double, width = dense.shape
    rows = experts * double // 2

    def blocks(count):
        return pl.BlockSpec((count, width), lambda plane: (plane, 0))

    whole, part = shaped((planes * rows, width), LOW), shaped((planes * rows // 2, width), LOW)
    return pl.pallas_call(
        dense_kernel,
        grid=(planes,),
        out_shape=(whole, whole, part, part),
        in_specs=[pl.BlockSpec((experts, 1, double, width), lambda plane: (0, plane, 0, 0))],
        out_specs=(blocks(rows), blocks(rows), blocks(rows // 2), blocks(rows // 2)),
        compiler_params=PARAMS,
        cost_estimate=pl.CostEstimate(flops=10**6, bytes_accessed=20 * 2**20, transcendentals=0),
    )(dense)


def to_holders(folded):
    experts, stack, columns = folded.shape
    rows = shaped((experts * stack // FOLD, columns * FOLD // 2), LOW)
    folded = to_experts(folded)
    one = local(functools.partial(unfold_kernel, begin=0), rows, folded)
    two = local(functools.partial(unfold_kernel, begin=FOLD // 2), rows, folded)
    behind_one, ahead_one = shift(one, 1), shift(one, -1)
    behind_two, ahead_two = shift(two, 1), shift(two, -1)
    far_one, far_two = shift(behind_one, 1), shift(ahead_two, -1)
    return ((one, two), (behind_one, behind_two), (ahead_one, ahead_two), (far_one, far_two))


def expert_terms(blocks, term):
    terms = [term(block, place) for place, block in enumerate(blocks[:3])]
    sides = (terms[1][0].astype(LOW), terms[2][1].astype(LOW))
    far, sides = lax.optimization_barrier((blocks[3], sides))
    return terms + [term(far, 3), sides]


def to_tokens(own, behind, ahead, far, sides, block, extra):
    step_one, step_two = shift(far[0].astype(LOW), 1), shift(far[1].astype(LOW), -1)
    side_one, side_two = shift(sides[0], -1), shift(sides[1], 1)
    last_one = shift((ahead[0] + step_one.astype(WIDE)).astype(LOW), 1)
    last_two = shift((behind[1] + step_two.astype(WIDE)).astype(LOW), -1)
    _, extra = lax.optimization_barrier((last_one[:16, :LANES], extra))
    folded = local(fold_kernel, block, own[0], side_one, last_one, own[1], side_two, last_two)
    return to_experts(folded), extra


def per_device(
    states, routes, lengths, router, w_in, w_out, w_query, w_key, w_value, w_output, cotangent
):
    section = lax.axis_index("section")
    encoder_side = section == 0
    tokens_here = states[0]
    routes_here = routes[0]
    router_here = router[0].T
    routes_here = routes_here.T
    first_weight = w_in[0, 0]
    second_weight = w_out[0, 0]
    cotangent_here = cotangent[0]
    tokens, columns = tokens_here.shape
    experts = router_here.shape[0]
    capacity = max(2, 5 * TOP * tokens // (4 * experts))
    half = columns // 2
    width = HEADS * HEAD
    slot_count = experts * STRIDE
    block = shaped((experts, FOLD * capacity, columns // FOLD), LOW)
    packed = pltpu.VMEM((slot_count, columns), LOW)

    facts_shape, wide_rows = shaped((tokens, LANES), WIDE), shaped((tokens, columns), WIDE)
    folded, facts = local(
        dispatch_kernel,
        (block, facts_shape),
        tokens_here,
        routes_here,
        router_here,
        late=(0, 2),
    )
    facts, w_query, w_key, w_value, w_output = lax.optimization_barrier(
        (facts, w_query, w_key, w_value, w_output)
    )
    own_a = jnp.where(encoder_side, w_key, w_query)
    output_wide = jnp.concatenate([w_output[:, :width], w_output[:, width:]], axis=0)
    own_b = jnp.where(encoder_side, w_value, output_wide)
    dense = jnp.concatenate([own_a, own_b], axis=0)
    dense = local(
        planes_kernel,
        shaped((lax.axis_size("dp"),) + dense.shape, LOW),
        lax.axis_index("dp").reshape(1, 1),
        dense,
        shift(dense, 1),
        shift(dense, -1),
        shift(dense, 2),
        scalars=1,
    )
    blocks = to_holders(folded)
    dense, _ = lax.optimization_barrier((dense, blocks[0][0][:16, :LANES]))
    dense = lax.all_gather(dense, "expert", axis=0, tiled=True)
    dense = dense.reshape(lax.axis_size("expert"), lax.axis_size("dp"), -1, width)

    actives = []

    def forward_term(rows, place):
        pre = dot(rows[0], first_weight[:half]) + dot(rows[1], first_weight[half:])
        active = jnp.maximum(pre, 0.0).astype(LOW)
        actives.append(active)
        return dot(active, second_weight[:, :half]), dot(active, second_weight[:, half:])

    terms = expert_terms(blocks, forward_term)
    back, dense = to_tokens(*terms, block, dense)
    full_a, full_value, full_left, full_right = arrange(dense)

    hidden_state, normed_out = local(
        combine_kernel,
        (wide_rows, shaped((tokens, columns), LOW)),
        back,
        tokens_here,
        facts,
        scratch=(packed,),
        late=(1, 2),
        sent=(0,),
    )
    own_length = jnp.where(encoder_side, lengths[0, 0], lengths[1, 0])
    live = jnp.arange(LEN, dtype=jnp.int32)[:, None] < own_length
    out_low = jnp.where(live & ~encoder_side, cotangent_here, jnp.zeros((), LOW))
    context_grad = (
        dot_nt(out_low[:, :half], full_left) + dot_nt(out_low[:, half:], full_right)
    ).astype(LOW)

    own_rows = dot(normed_out, full_a).astype(LOW)
    own_values = dot(normed_out, full_value).astype(LOW)
    key_rows = lax.ppermute(own_rows, "section", [(0, 1)])
    value_rows = lax.ppermute(own_values, "section", [(0, 1)])
    low_rows = shaped((tokens, width), LOW)
    attention, value_grad = local(
        attend_kernel,
        (shaped((HEADS, LEN, LEN), WIDE), low_rows),
        lengths[0].reshape(1, 1),
        own_rows,
        key_rows,
        context_grad,
        scalars=1,
        late=(3,),
        sent=(0,),
    )
    value_back = lax.ppermute(value_grad, "section", [(1, 0)])
    query_grad, key_grad, context = local(
        attend_back_kernel,
        (low_rows,) * 3,
        attention,
        own_rows,
        key_rows,
        value_rows,
        context_grad,
        late=(0, 1, 2, 4),
    )
    key_back = lax.ppermute(key_grad, "section", [(1, 0)])
    attended = jnp.concatenate([dot(context, full_left), dot(context, full_right)], axis=1)
    decoder_out = (hidden_state + attended).astype(LOW)
    forward_out = jnp.where(encoder_side, normed_out, decoder_out)
    projection_back = dot_nt(jnp.where(encoder_side, key_back, query_grad), full_a) + dot_nt(
        value_back, full_value
    )
    flags = jnp.stack([own_length, encoder_side.astype(jnp.int32)])[None]
    upstream, folded = local(
        upstream_kernel,
        (wide_rows, block),
        flags,
        hidden_state,
        projection_back,
        cotangent_here,
        facts,
        scalars=1,
        late=(1, 3, 4),
        sent=(0,),
    )
    sign_grad = local(
        router_kernel,
        shaped((tokens, experts), WIDE),
        back,
        upstream,
        facts,
        scratch=(packed,),
        late=(1, 2),
    )

    def backward_term(rows, place):
        slope = dot_nt(rows[0], second_weight[:, :half]) + dot_nt(rows[1], second_weight[:, half:])
        slope = jnp.where(actives[place] > 0, slope, 0.0).astype(LOW)
        return dot_nt(slope, first_weight[:half]), dot_nt(slope, first_weight[half:])

    terms = expert_terms(to_holders(folded), backward_term)
    back, _ = to_tokens(*terms, block, ())
    grads = local(
        finish_kernel,
        wide_rows,
        back,
        tokens_here,
        upstream,
        sign_grad,
        router_here,
        facts,
        scratch=(packed,),
        late=(1, 2, 3, 4, 5),
    )
    return (forward_out[None], grads[None])


def solution(mesh):
    in_specs = (
        P("section", ("dp", "expert"), None),
        P("section", ("dp", "expert"), None),
        P(None, ("dp", "expert")),
        P("section", None, None),
        P("section", "expert", None, "dp"),
        P("section", "expert", "dp", None),
        P(("dp", "expert"), None),
        P(("dp", "expert"), None),
        P(("dp", "expert"), None),
        P(("dp", "expert"), None),
        P("section", ("dp", "expert"), None),
    )
    out_specs = (P("section", ("dp", "expert"), None), P("section", ("dp", "expert"), None))
    return jax.shard_map(
        per_device, mesh=mesh, in_specs=in_specs, out_specs=out_specs, check_vma=False
    )
```

```python
import functools

import jax
import jax.numpy as jnp
from jax import lax
from jax.experimental import pallas as pl
from jax.experimental.pallas import tpu as pltpu
from jax.sharding import PartitionSpec as P

HEADS = 8
HEAD = 128
TOP = 2
LEN = 128
STRIDE = 32
FOLD = 4
LANES = 128


EPS = 1e-05
NEG_FILL = -1e30
LOW = jnp.bfloat16
WIDE = jnp.float32
VMEM = pl.BlockSpec(memory_space=pltpu.VMEM)
SMEM = pl.BlockSpec(memory_space=pltpu.SMEM)
PARAMS = pltpu.CompilerParams(vmem_limit_bytes=20 * 1024 * 1024)


def dot(a, b):
    return jnp.dot(a, b, preferred_element_type=WIDE)


def dot_nt(a, b):
    return lax.dot_general(a, b, (((1,), (1,)), ((), ())), preferred_element_type=WIDE)


def dot_tn(a, b):
    return lax.dot_general(a, b, (((0,), (0,)), ((), ())), preferred_element_type=WIDE)


def normalised(values):
    centred = values - jnp.mean(values, axis=-1, keepdims=True)
    variance = jnp.mean(centred * centred, axis=-1, keepdims=True)
    inverse = lax.rsqrt(variance + EPS)
    return centred * inverse, inverse


def norm_back(values, upstream):
    normed, inverse = normalised(values)
    return inverse * (
        upstream
        - jnp.mean(upstream, axis=-1, keepdims=True)
        - normed * jnp.mean(upstream * normed, axis=-1, keepdims=True)
    )


class Late:
    def __init__(self, source, held, semaphore):
        self.copy = pltpu.make_async_copy(source, held, semaphore)
        self.held, self.shape, self.dtype, self.waiting = held, held.shape, held.dtype, True
        self.copy.start()

    def __getitem__(self, index):
        if self.waiting:
            self.copy.wait()
            self.waiting = False
        return self.held[index]


class Sent:
    def __init__(self, target, held, semaphore):
        self.copy = pltpu.make_async_copy(held, target, semaphore)
        self.held, self.shape, self.dtype = held, held.shape, held.dtype

    def __setitem__(self, index, value):
        self.held[index] = value

    def send(self):
        self.copy.start()


def laned(columns):
    lane = lax.broadcasted_iota(jnp.int32, (columns[0].shape[0], LANES), 1)
    return sum(jnp.where(lane == place, column, 0.0) for place, column in enumerate(columns))


def slot_hots(facts, experts):
    place = lax.broadcasted_iota(jnp.int32, (facts.shape[0], experts * STRIDE), 1)
    return tuple(
        jnp.where(place == (facts[:, at : at + 1] * STRIDE + facts[:, at + 1 : at + 2]).astype(jnp.int32), 1.0, 0.0)
        for at in (0, 2)
    )


def route_signs(facts, experts):
    ids = lax.broadcasted_iota(jnp.int32, (facts.shape[0], experts), 1).astype(WIDE)
    return jnp.where(facts[:, 0:1] == ids, 1.0, 0.0) - jnp.where(facts[:, 2:3] == ids, 1.0, 0.0)


def spread_rows(rows, folded_ref):
    experts, stack, columns = folded_ref.shape
    capacity = stack // FOLD
    for e in range(experts):
        block = rows[e * STRIDE : e * STRIDE + capacity].astype(LOW)
        for place in range(FOLD):
            folded_ref[e, pl.ds(place * capacity, capacity), :] = block[
                :, place * columns : (place + 1) * columns
            ]


def pack_rows(folded_ref, packed):
    experts, stack, columns = folded_ref.shape
    capacity = stack // FOLD
    packed[...] = jnp.zeros_like(packed)
    for e in range(experts):
        for place in range(FOLD):
            packed[pl.ds(e * STRIDE, capacity), pl.ds(place * columns, columns)] = folded_ref[
                e, pl.ds(place * capacity, capacity), :
            ]


def unfold_kernel(folded_ref, rows_ref, token_ref, *, begin):
    token_ref[...] = jnp.zeros_like(token_ref)
    experts, stack, columns = folded_ref.shape
    capacity = stack // FOLD
    for e in range(experts):
        for place in range(FOLD // 2):
            rows_ref[pl.ds(e * capacity, capacity), pl.ds(place * columns, columns)] = folded_ref[
                e, pl.ds((begin + place) * capacity, capacity), :
            ]


def fold_kernel(*refs):
    folded_ref = refs[-1]
    experts, stack, columns = folded_ref.shape
    capacity = stack // FOLD
    for begin in range(2):
        own_ref, side_ref, last_ref = refs[begin * 3 : begin * 3 + 3]
        total = own_ref[...] + side_ref[...].astype(WIDE) + last_ref[...].astype(WIDE)
        total = total.astype(LOW)
        for e in range(experts):
            for place in range(FOLD // 2):
                folded_ref[e, pl.ds((begin * FOLD // 2 + place) * capacity, capacity), :] = total[
                    e * capacity : (e + 1) * capacity, place * columns : (place + 1) * columns
                ]


def planes_kernel(place_ref, own_ref, behind_ref, ahead_ref, far_ref, token_ref, planes_ref):
    count = planes_ref.shape[0]
    for distance, ref in ((0, own_ref), (count - 1, behind_ref), (1, ahead_ref), (2, far_ref)):
        planes_ref[lax.rem(place_ref[0, 0] + distance, count)] = ref[...]


def dense_kernel(dense_ref, first_ref, second_ref, left_ref, right_ref):
    experts, _, double, width = dense_ref.shape
    rows = double // 2
    first_ref[...] = dense_ref[:, 0, :rows].reshape(experts * rows, width)
    second = dense_ref[:, 0, rows:]
    second_ref[...] = second.reshape(experts * rows, width)
    left_ref[...] = second[:, : rows // 2].reshape(experts * rows // 2, width)
    right_ref[...] = second[:, rows // 2 :].reshape(experts * rows // 2, width)


def dispatch_kernel(states_ref, routes_ref, router_ref, folded_ref, facts_ref):
    experts = folded_ref.shape[0]
    tokens = states_ref.shape[0]
    ids = lax.broadcasted_iota(jnp.int32, (experts, tokens), 0)
    row = lax.broadcasted_iota(jnp.int32, (experts, experts), 0)
    column = lax.broadcasted_iota(jnp.int32, (experts, experts), 1)
    same = jnp.where(row == column, 1.0, 0.0).astype(LOW)
    hots = [
        dot_tn(jnp.where(routes_ref[k : k + 1, :] == ids, 1.0, 0.0).astype(LOW), same)
        for k in range(TOP)
    ]
    row = lax.broadcasted_iota(jnp.int32, (tokens, tokens), 0)
    column = lax.broadcasted_iota(jnp.int32, (tokens, tokens), 1)
    earlier = jnp.where(column < row, 1.0, 0.0).astype(LOW)
    rank = dot(earlier, (hots[0] + hots[1]).astype(LOW))
    number = lax.broadcasted_iota(jnp.int32, (tokens, experts), 1).astype(WIDE)
    facts = []
    for hot in hots:
        facts.append(jnp.sum(hot * number, axis=1, keepdims=True))
        facts.append(jnp.sum(hot * rank, axis=1, keepdims=True))
    normed = normalised(states_ref[...].astype(WIDE))[0].astype(LOW)
    logits = dot_nt(normed, router_ref[...])
    spread = jnp.sum(hots[0] * logits - hots[1] * logits, axis=1, keepdims=True)
    facts = laned(facts + [jax.nn.sigmoid(spread)])
    facts_ref[...] = facts
    facts_ref.send()
    one, two = slot_hots(facts, experts)
    spread_rows(dot_tn((one + two).astype(LOW), normed), folded_ref)


def combine_kernel(folded_ref, states_ref, facts_ref, ready_ref, hidden_ref, normed_ref, packed):
    pack_rows(folded_ref, packed)
    rows = packed[...]
    facts = facts_ref[...]
    gate = facts[:, 4:5]
    one, two = slot_hots(facts, folded_ref.shape[0])
    hidden = states_ref[...].astype(WIDE) + (
        gate * dot(one.astype(LOW), rows) + (1.0 - gate) * dot(two.astype(LOW), rows)
    )
    hidden_ref[...] = hidden
    hidden_ref.send()
    normed_ref[...] = normalised(hidden)[0].astype(LOW)


def attend_kernel(length_ref, q_ref, k_ref, grad_ref, v_grad_ref, attention_ref, kept_ref):
    kept_ref[0], kept_ref[1], kept_ref[2] = q_ref[...], k_ref[...], grad_ref[...]
    kept_ref.send()
    scale = HEAD ** (-0.5)
    live = lax.broadcasted_iota(jnp.int32, (LEN, LEN), 1) < length_ref[0, 0]
    for head in range(HEADS):
        at = slice(head * HEAD, (head + 1) * HEAD)
        scores = jnp.where(live, dot_nt(q_ref[:, at], k_ref[:, at]) * scale, NEG_FILL)
        exponent = jnp.exp(scores - jnp.max(scores, axis=-1, keepdims=True))
        attention = exponent / jnp.sum(exponent, axis=-1, keepdims=True)
        attention_ref[head] = attention
        v_grad_ref[:, at] = dot_tn(attention.astype(LOW), grad_ref[:, at]).astype(LOW)
    attention_ref.send()


def attend_back_kernel(v_ref, attention_ref, kept_ref, q_grad_ref, k_grad_ref, context_ref):
    scale = HEAD ** (-0.5)
    for head in range(HEADS):
        at = slice(head * HEAD, (head + 1) * HEAD)
        attention, v = attention_ref[head], v_ref[:, at]
        q, k, grad = kept_ref[0, :, at], kept_ref[1, :, at], kept_ref[2, :, at]
        weight_grad = dot_nt(grad, v)
        score_grad = (
            attention
            * (weight_grad - jnp.sum(attention * weight_grad, axis=-1, keepdims=True))
            * scale
        ).astype(LOW)
        k_grad_ref[:, at] = dot_tn(score_grad, q).astype(LOW)
        q_grad_ref[:, at] = dot(score_grad, k).astype(LOW)
        context_ref[:, at] = dot(attention.astype(LOW), v).astype(LOW)


def upstream_kernel(flags_ref, hidden_ref, back_ref, cotangent_ref, facts_ref, upstream_ref, folded_ref):
    live = lax.broadcasted_iota(jnp.int32, (LEN, 1), 0) < flags_ref[0, 0]
    encoder = flags_ref[0, 1] == 1
    masked = jnp.where(live, cotangent_ref[...].astype(WIDE), 0.0)
    out_grad = jnp.where(encoder, 0.0, masked)
    normed_grad = back_ref[...] + jnp.where(encoder, masked, 0.0)
    upstream = out_grad + norm_back(hidden_ref[...], normed_grad)
    upstream_ref[...] = upstream
    upstream_ref.send()
    facts = facts_ref[...]
    gate = facts[:, 4:5]
    one, two = slot_hots(facts, folded_ref.shape[0])
    rows = dot_tn(one.astype(LOW), (gate * upstream).astype(LOW)) + dot_tn(
        two.astype(LOW), ((1.0 - gate) * upstream).astype(LOW)
    )
    spread_rows(rows, folded_ref)


def router_kernel(folded_ref, upstream_ref, facts_ref, sign_ref, packed):
    pack_rows(folded_ref, packed)
    rows = packed[...]
    facts = facts_ref[...]
    gate = facts[:, 4:5]
    one, two = slot_hots(facts, folded_ref.shape[0])
    apart = dot(one.astype(LOW), rows) - dot(two.astype(LOW), rows)
    gate_grad = jnp.sum(upstream_ref[...] * apart, axis=1, keepdims=True)
    logit_grad = gate_grad * gate * (1.0 - gate)
    sign_ref[...] = logit_grad * route_signs(facts, folded_ref.shape[0])


def finish_kernel(folded_ref, states_ref, upstream_ref, sign_ref, router_ref, facts_ref, grads_ref, packed):
    pack_rows(folded_ref, packed)
    one, two = slot_hots(facts_ref[...], folded_ref.shape[0])
    back = dot((one + two).astype(LOW), packed[...])
    router_term = jnp.dot(
        sign_ref[...],
        router_ref[...].astype(WIDE),
        precision=lax.Precision.HIGHEST,
        preferred_element_type=WIDE,
    )
    input_total = back + router_term
    grads_ref[...] = upstream_ref[...] + norm_back(states_ref[...].astype(WIDE), input_total)


def local(kernel, out_shape, *operands, scalars=0, scratch=(), late=(), sent=(), held=()):
    single = not isinstance(out_shape, tuple)
    shapes = (out_shape,) if single else out_shape
    count = len(operands)
    total = count + len(shapes)
    moved = [place for place in range(count) if place in late]
    moved += [count + place for place in range(len(shapes)) if place in sent]
    both = list(operands) + list(shapes)

    def body(*refs):
        refs, extra = list(refs[:total]), refs[total:]
        holds, semaphores = extra[: len(moved)], extra[len(moved)] if moved else None
        for number, place in enumerate(moved):
            made = Late if place < count else Sent
            refs[place] = made(refs[place], holds[number], semaphores.at[number])
        kernel(*refs, *extra[len(moved) + (1 if moved else 0) :])
        for place in moved:
            if place >= count:
                refs[place].copy.wait()

    scratches = [pltpu.VMEM(both[place].shape, both[place].dtype) for place in moved]
    if moved:
        scratches.append(pltpu.SemaphoreType.DMA((len(moved),)))
    specs = [SMEM] * scalars + [VMEM] * (total - scalars)
    for place in [*moved, *held]:
        specs[place] = pl.BlockSpec(memory_space=pltpu.HBM)
    cost = sum(x.size * x.dtype.itemsize for x in both)
    operands = [
        pltpu.with_memory_space_constraint(operand, pltpu.HBM) if place in [*late, *held] else operand
        for place, operand in enumerate(operands)
    ]
    shapes = tuple(
        pltpu.HBM(shape.shape, shape.dtype) if place in sent else shape
        for place, shape in enumerate(shapes)
    )
    result = pl.pallas_call(
        body,
        out_shape=shapes,
        in_specs=specs[:count],
        out_specs=tuple(specs[count:]),
        scratch_shapes=scratches + list(scratch),
        compiler_params=PARAMS,
        cost_estimate=pl.CostEstimate(flops=10**9, bytes_accessed=4 * cost, transcendentals=0),
    )(*operands)
    return result[0] if single else result


def shaped(shape, dtype):
    return jax.ShapeDtypeStruct(shape, dtype)


def shift(block, distance):
    count = lax.axis_size("dp")
    return lax.ppermute(block, "dp", [(i, (i + distance) % count) for i in range(count)])


def to_experts(block):
    return lax.all_to_all(block, "expert", split_axis=0, concat_axis=0, tiled=True)


def arrange(dense):
    experts, planes, double, width = dense.shape
    rows = experts * double // 2

    def blocks(count):
        return pl.BlockSpec((count, width), lambda plane: (plane, 0))

    whole, part = shaped((planes * rows, width), LOW), shaped((planes * rows // 2, width), LOW)
    return pl.pallas_call(
        dense_kernel,
        grid=(planes,),
        out_shape=(whole, whole, part, part),
        in_specs=[pl.BlockSpec((experts, 1, double, width), lambda plane: (0, plane, 0, 0))],
        out_specs=(blocks(rows), blocks(rows), blocks(rows // 2), blocks(rows // 2)),
        compiler_params=PARAMS,
        cost_estimate=pl.CostEstimate(flops=10**6, bytes_accessed=20 * 2**20, transcendentals=0),
    )(dense)


def to_holders(folded):
    experts, stack, columns = folded.shape
    rows = shaped((experts * stack // FOLD, columns * FOLD // 2), LOW)
    folded = to_experts(folded)
    token = shaped((8, LANES), WIDE)
    one, token = local(functools.partial(unfold_kernel, begin=0), (rows, token), folded)
    two, _ = local(functools.partial(unfold_kernel, begin=FOLD // 2), (rows, token), folded)
    behind_one, ahead_one = shift(one, 1), shift(one, -1)
    behind_two, ahead_two = shift(two, 1), shift(two, -1)
    far_one, far_two = shift(behind_one, 1), shift(ahead_two, -1)
    return ((one, two), (behind_one, behind_two), (ahead_one, ahead_two), (far_one, far_two)), token


def expert_terms(blocks, term):
    terms = [term(block, place) for place, block in enumerate(blocks[:3])]
    sides = (terms[1][0].astype(LOW), terms[2][1].astype(LOW))
    far, sides = lax.optimization_barrier((blocks[3], sides))
    return terms + [term(far, 3), sides]


def to_tokens(own, behind, ahead, far, sides, block):
    step_one, step_two = shift(far[0].astype(LOW), 1), shift(far[1].astype(LOW), -1)
    side_one, side_two = shift(sides[0], -1), shift(sides[1], 1)
    last_one = shift((ahead[0] + step_one.astype(WIDE)).astype(LOW), 1)
    last_two = shift((behind[1] + step_two.astype(WIDE)).astype(LOW), -1)
    folded = local(fold_kernel, block, own[0], side_one, last_one, own[1], side_two, last_two)
    return to_experts(folded)


def per_device(
    states, routes, lengths, router, w_in, w_out, w_query, w_key, w_value, w_output, cotangent
):
    section = lax.axis_index("section")
    encoder_side = section == 0
    tokens_here = states[0]
    routes_here = routes[0]
    router_here = router[0].T
    routes_here = routes_here.T
    first_weight = w_in[0, 0]
    second_weight = w_out[0, 0]
    cotangent_here = cotangent[0]
    tokens, columns = tokens_here.shape
    experts = router_here.shape[0]
    capacity = max(2, 5 * TOP * tokens // (4 * experts))
    half = columns // 2
    width = HEADS * HEAD
    slot_count = experts * STRIDE
    block = shaped((experts, FOLD * capacity, columns // FOLD), LOW)
    packed = pltpu.VMEM((slot_count, columns), LOW)

    facts_shape, wide_rows = shaped((tokens, LANES), WIDE), shaped((tokens, columns), WIDE)
    folded, facts = local(
        dispatch_kernel,
        (block, facts_shape),
        tokens_here,
        routes_here,
        router_here,
        late=(0, 2),
        sent=(1,),
    )
    folded, w_query, w_key, w_value, w_output = lax.optimization_barrier(
        (folded, w_query, w_key, w_value, w_output)
    )
    own_a = jnp.where(encoder_side, w_key, w_query)
    output_wide = jnp.concatenate([w_output[:, :width], w_output[:, width:]], axis=0)
    own_b = jnp.where(encoder_side, w_value, output_wide)
    dense = jnp.concatenate([own_a, own_b], axis=0)
    others = shift(dense, 1), shift(dense, -1), shift(dense, 2)
    blocks, token = to_holders(folded)
    dense = local(
        planes_kernel,
        shaped((lax.axis_size("dp"),) + dense.shape, LOW),
        lax.axis_index("dp").reshape(1, 1),
        dense,
        *others,
        token,
        scalars=1,
    )
    dense = lax.all_gather(dense, "expert", axis=0, tiled=True)
    dense = dense.reshape(lax.axis_size("expert"), lax.axis_size("dp"), -1, width)

    actives = []

    def forward_term(rows, place):
        pre = dot(rows[0], first_weight[:half]) + dot(rows[1], first_weight[half:])
        active = jnp.maximum(pre, 0.0).astype(LOW)
        actives.append(active)
        return dot(active, second_weight[:, :half]), dot(active, second_weight[:, half:])

    terms = expert_terms(blocks, forward_term)
    back = to_tokens(*terms, block)
    full_a, full_value, full_left, full_right = arrange(dense)

    hidden_state, normed_out = local(
        combine_kernel,
        (wide_rows, shaped((tokens, columns), LOW)),
        back,
        tokens_here,
        facts,
        full_a,
        scratch=(packed,),
        late=(1, 2),
        held=(3,),
        sent=(0,),
    )
    own_length = jnp.where(encoder_side, lengths[0, 0], lengths[1, 0])
    live = jnp.arange(LEN, dtype=jnp.int32)[:, None] < own_length
    out_low = jnp.where(live & ~encoder_side, cotangent_here, jnp.zeros((), LOW))
    context_grad = (
        dot_nt(out_low[:, :half], full_left) + dot_nt(out_low[:, half:], full_right)
    ).astype(LOW)

    own_rows = dot(normed_out, full_a).astype(LOW)
    own_values = dot(normed_out, full_value).astype(LOW)
    key_rows = lax.ppermute(own_rows, "section", [(0, 1)])
    value_rows = lax.ppermute(own_values, "section", [(0, 1)])
    low_rows = shaped((tokens, width), LOW)
    value_grad, attention, kept = local(
        attend_kernel,
        (low_rows, shaped((HEADS, LEN, LEN), WIDE), shaped((3, tokens, width), LOW)),
        lengths[0].reshape(1, 1),
        own_rows,
        key_rows,
        context_grad,
        scalars=1,
        sent=(1, 2),
    )
    value_back = lax.ppermute(value_grad, "section", [(1, 0)])
    query_grad, key_grad, context = local(
        attend_back_kernel,
        (low_rows,) * 3,
        value_rows,
        attention,
        kept,
        late=(1, 2),
    )
    key_back = lax.ppermute(key_grad, "section", [(1, 0)])
    attended = jnp.concatenate([dot(context, full_left), dot(context, full_right)], axis=1)
    decoder_out = (hidden_state + attended).astype(LOW)
    forward_out = jnp.where(encoder_side, normed_out, decoder_out)
    projection_back = dot_nt(jnp.where(encoder_side, key_back, query_grad), full_a) + dot_nt(
        value_back, full_value
    )
    flags = jnp.stack([own_length, encoder_side.astype(jnp.int32)])[None]
    upstream, folded = local(
        upstream_kernel,
        (wide_rows, block),
        flags,
        hidden_state,
        projection_back,
        cotangent_here,
        facts,
        scalars=1,
        late=(1, 3, 4),
        sent=(0,),
    )
    sign_grad = local(
        router_kernel,
        shaped((tokens, experts), WIDE),
        back,
        upstream,
        facts,
        scratch=(packed,),
        late=(1, 2),
    )

    def backward_term(rows, place):
        slope = dot_nt(rows[0], second_weight[:, :half]) + dot_nt(rows[1], second_weight[:, half:])
        slope = jnp.where(actives[place] > 0, slope, 0.0).astype(LOW)
        return dot_nt(slope, first_weight[:half]), dot_nt(slope, first_weight[half:])

    terms = expert_terms(to_holders(folded)[0], backward_term)
    back = to_tokens(*terms, block)
    grads = local(
        finish_kernel,
        wide_rows,
        back,
        tokens_here,
        upstream,
        sign_grad,
        router_here,
        facts,
        scratch=(packed,),
        late=(1, 2, 3, 4, 5),
    )
    return (forward_out[None], grads[None])


def solution(mesh):
    in_specs = (
        P("section", ("dp", "expert"), None),
        P("section", ("dp", "expert"), None),
        P(None, ("dp", "expert")),
        P("section", None, None),
        P("section", "expert", None, "dp"),
        P("section", "expert", "dp", None),
        P(("dp", "expert"), None),
        P(("dp", "expert"), None),
        P(("dp", "expert"), None),
        P(("dp", "expert"), None),
        P("section", ("dp", "expert"), None),
    )
    out_specs = (P("section", ("dp", "expert"), None), P("section", ("dp", "expert"), None))
    return jax.shard_map(
        per_device, mesh=mesh, in_specs=in_specs, out_specs=out_specs, check_vma=False
    )
```

```python
import functools

import jax
import jax.numpy as jnp
from jax import lax
from jax.experimental import pallas as pl
from jax.experimental.pallas import tpu as pltpu
from jax.sharding import PartitionSpec as P

HEADS = 8
HEAD = 128
TOP = 2
LEN = 128
STRIDE = 32
FOLD = 4
LANES = 128


EPS = 1e-05
NEG_FILL = -1e30
LOW = jnp.bfloat16
WIDE = jnp.float32
VMEM = pl.BlockSpec(memory_space=pltpu.VMEM)
SMEM = pl.BlockSpec(memory_space=pltpu.SMEM)
PARAMS = pltpu.CompilerParams(vmem_limit_bytes=20 * 1024 * 1024)


def dot(a, b):
    return jnp.dot(a, b, preferred_element_type=WIDE)


def dot_nt(a, b):
    return lax.dot_general(a, b, (((1,), (1,)), ((), ())), preferred_element_type=WIDE)


def dot_tn(a, b):
    return lax.dot_general(a, b, (((0,), (0,)), ((), ())), preferred_element_type=WIDE)


def normalised(values):
    centred = values - jnp.mean(values, axis=-1, keepdims=True)
    variance = jnp.mean(centred * centred, axis=-1, keepdims=True)
    inverse = lax.rsqrt(variance + EPS)
    return centred * inverse, inverse


def norm_back(values, upstream):
    normed, inverse = normalised(values)
    return inverse * (
        upstream
        - jnp.mean(upstream, axis=-1, keepdims=True)
        - normed * jnp.mean(upstream * normed, axis=-1, keepdims=True)
    )


class Late:
    def __init__(self, source, held, semaphore):
        self.copy = pltpu.make_async_copy(source, held, semaphore)
        self.held, self.shape, self.dtype, self.waiting = held, held.shape, held.dtype, True
        self.copy.start()

    def __getitem__(self, index):
        if self.waiting:
            self.copy.wait()
            self.waiting = False
        return self.held[index]


class Sent:
    def __init__(self, target, held, semaphore):
        self.copy = pltpu.make_async_copy(held, target, semaphore)
        self.held, self.shape, self.dtype = held, held.shape, held.dtype

    def __setitem__(self, index, value):
        self.held[index] = value

    def send(self):
        self.copy.start()


def laned(columns):
    lane = lax.broadcasted_iota(jnp.int32, (columns[0].shape[0], LANES), 1)
    return sum(jnp.where(lane == place, column, 0.0) for place, column in enumerate(columns))


def slot_hots(facts, experts):
    place = lax.broadcasted_iota(jnp.int32, (facts.shape[0], experts * STRIDE), 1)
    return tuple(
        jnp.where(place == (facts[:, at : at + 1] * STRIDE + facts[:, at + 1 : at + 2]).astype(jnp.int32), 1.0, 0.0)
        for at in (0, 2)
    )


def route_signs(facts, experts):
    ids = lax.broadcasted_iota(jnp.int32, (facts.shape[0], experts), 1).astype(WIDE)
    return jnp.where(facts[:, 0:1] == ids, 1.0, 0.0) - jnp.where(facts[:, 2:3] == ids, 1.0, 0.0)


def spread_rows(rows, folded_ref):
    experts, stack, columns = folded_ref.shape
    capacity = stack // FOLD
    for e in range(experts):
        block = rows[e * STRIDE : e * STRIDE + capacity].astype(LOW)
        for place in range(FOLD):
            folded_ref[e, pl.ds(place * capacity, capacity), :] = block[
                :, place * columns : (place + 1) * columns
            ]


def pack_rows(folded_ref, packed):
    experts, stack, columns = folded_ref.shape
    capacity = stack // FOLD
    packed[...] = jnp.zeros_like(packed)
    for e in range(experts):
        for place in range(FOLD):
            packed[pl.ds(e * STRIDE, capacity), pl.ds(place * columns, columns)] = folded_ref[
                e, pl.ds(place * capacity, capacity), :
            ]


def unfold_kernel(folded_ref, rows_ref, token_ref, *, begin):
    token_ref[...] = jnp.zeros_like(token_ref)
    experts, stack, columns = folded_ref.shape
    capacity = stack // FOLD
    for e in range(experts):
        for place in range(FOLD // 2):
            rows_ref[pl.ds(e * capacity, capacity), pl.ds(place * columns, columns)] = folded_ref[
                e, pl.ds((begin + place) * capacity, capacity), :
            ]


def fold_kernel(*refs):
    folded_ref = refs[-1]
    experts, stack, columns = folded_ref.shape
    capacity = stack // FOLD
    for begin in range(2):
        base_ref, last_ref = refs[begin * 2 : begin * 2 + 2]
        total = (base_ref[...] + last_ref[...].astype(WIDE)).astype(LOW)
        for e in range(experts):
            for place in range(FOLD // 2):
                folded_ref[e, pl.ds((begin * FOLD // 2 + place) * capacity, capacity), :] = total[
                    e * capacity : (e + 1) * capacity, place * columns : (place + 1) * columns
                ]


def planes_kernel(place_ref, own_ref, behind_ref, ahead_ref, far_ref, token_ref, planes_ref):
    count = planes_ref.shape[0]
    for distance, ref in ((0, own_ref), (count - 1, behind_ref), (1, ahead_ref), (2, far_ref)):
        planes_ref[lax.rem(place_ref[0, 0] + distance, count)] = ref[...]


def dense_kernel(dense_ref, first_ref, second_ref, left_ref, right_ref):
    experts, _, double, width = dense_ref.shape
    rows = double // 2
    first_ref[...] = dense_ref[:, 0, :rows].reshape(experts * rows, width)
    second = dense_ref[:, 0, rows:]
    second_ref[...] = second.reshape(experts * rows, width)
    left_ref[...] = second[:, : rows // 2].reshape(experts * rows // 2, width)
    right_ref[...] = second[:, rows // 2 :].reshape(experts * rows // 2, width)


def dispatch_kernel(states_ref, routes_ref, router_ref, folded_ref, facts_ref):
    experts = folded_ref.shape[0]
    tokens = states_ref.shape[0]
    ids = lax.broadcasted_iota(jnp.int32, (experts, tokens), 0)
    row = lax.broadcasted_iota(jnp.int32, (experts, experts), 0)
    column = lax.broadcasted_iota(jnp.int32, (experts, experts), 1)
    same = jnp.where(row == column, 1.0, 0.0).astype(LOW)
    hots = [
        dot_tn(jnp.where(routes_ref[k : k + 1, :] == ids, 1.0, 0.0).astype(LOW), same)
        for k in range(TOP)
    ]
    row = lax.broadcasted_iota(jnp.int32, (tokens, tokens), 0)
    column = lax.broadcasted_iota(jnp.int32, (tokens, tokens), 1)
    earlier = jnp.where(column < row, 1.0, 0.0).astype(LOW)
    rank = dot(earlier, (hots[0] + hots[1]).astype(LOW))
    number = lax.broadcasted_iota(jnp.int32, (tokens, experts), 1).astype(WIDE)
    facts = []
    for hot in hots:
        facts.append(jnp.sum(hot * number, axis=1, keepdims=True))
        facts.append(jnp.sum(hot * rank, axis=1, keepdims=True))
    normed = normalised(states_ref[...].astype(WIDE))[0].astype(LOW)
    logits = dot_nt(normed, router_ref[...])
    spread = jnp.sum(hots[0] * logits - hots[1] * logits, axis=1, keepdims=True)
    facts = laned(facts + [jax.nn.sigmoid(spread)])
    facts_ref[...] = facts
    facts_ref.send()
    one, two = slot_hots(facts, experts)
    spread_rows(dot_tn((one + two).astype(LOW), normed), folded_ref)


def combine_kernel(folded_ref, states_ref, facts_ref, ready_ref, hidden_ref, normed_ref, packed):
    pack_rows(folded_ref, packed)
    rows = packed[...]
    facts = facts_ref[...]
    gate = facts[:, 4:5]
    one, two = slot_hots(facts, folded_ref.shape[0])
    hidden = states_ref[...].astype(WIDE) + (
        gate * dot(one.astype(LOW), rows) + (1.0 - gate) * dot(two.astype(LOW), rows)
    )
    hidden_ref[...] = hidden
    hidden_ref.send()
    normed_ref[...] = normalised(hidden)[0].astype(LOW)


def attend_kernel(length_ref, q_ref, k_ref, grad_ref, v_grad_ref, attention_ref, kept_ref):
    kept_ref[0], kept_ref[1], kept_ref[2] = q_ref[...], k_ref[...], grad_ref[...]
    kept_ref.send()
    scale = HEAD ** (-0.5)
    live = lax.broadcasted_iota(jnp.int32, (LEN, LEN), 1) < length_ref[0, 0]
    for head in range(HEADS):
        at = slice(head * HEAD, (head + 1) * HEAD)
        scores = jnp.where(live, dot_nt(q_ref[:, at], k_ref[:, at]) * scale, NEG_FILL)
        exponent = jnp.exp(scores - jnp.max(scores, axis=-1, keepdims=True))
        attention = exponent / jnp.sum(exponent, axis=-1, keepdims=True)
        attention_ref[head] = attention
        v_grad_ref[:, at] = dot_tn(attention.astype(LOW), grad_ref[:, at]).astype(LOW)
    attention_ref.send()


def attend_back_kernel(v_ref, attention_ref, kept_ref, q_grad_ref, k_grad_ref, context_ref):
    scale = HEAD ** (-0.5)
    for head in range(HEADS):
        at = slice(head * HEAD, (head + 1) * HEAD)
        attention, v = attention_ref[head], v_ref[:, at]
        q, k, grad = kept_ref[0, :, at], kept_ref[1, :, at], kept_ref[2, :, at]
        weight_grad = dot_nt(grad, v)
        score_grad = (
            attention
            * (weight_grad - jnp.sum(attention * weight_grad, axis=-1, keepdims=True))
            * scale
        ).astype(LOW)
        k_grad_ref[:, at] = dot_tn(score_grad, q).astype(LOW)
        q_grad_ref[:, at] = dot(score_grad, k).astype(LOW)
        context_ref[:, at] = dot(attention.astype(LOW), v).astype(LOW)


def upstream_kernel(flags_ref, hidden_ref, back_ref, cotangent_ref, facts_ref, upstream_ref, folded_ref):
    live = lax.broadcasted_iota(jnp.int32, (LEN, 1), 0) < flags_ref[0, 0]
    encoder = flags_ref[0, 1] == 1
    masked = jnp.where(live, cotangent_ref[...].astype(WIDE), 0.0)
    out_grad = jnp.where(encoder, 0.0, masked)
    normed_grad = back_ref[...] + jnp.where(encoder, masked, 0.0)
    upstream = out_grad + norm_back(hidden_ref[...], normed_grad)
    upstream_ref[...] = upstream
    upstream_ref.send()
    facts = facts_ref[...]
    gate = facts[:, 4:5]
    one, two = slot_hots(facts, folded_ref.shape[0])
    rows = dot_tn(one.astype(LOW), (gate * upstream).astype(LOW)) + dot_tn(
        two.astype(LOW), ((1.0 - gate) * upstream).astype(LOW)
    )
    spread_rows(rows, folded_ref)


def router_kernel(folded_ref, upstream_ref, facts_ref, sign_ref, packed):
    pack_rows(folded_ref, packed)
    rows = packed[...]
    facts = facts_ref[...]
    gate = facts[:, 4:5]
    one, two = slot_hots(facts, folded_ref.shape[0])
    apart = dot(one.astype(LOW), rows) - dot(two.astype(LOW), rows)
    gate_grad = jnp.sum(upstream_ref[...] * apart, axis=1, keepdims=True)
    logit_grad = gate_grad * gate * (1.0 - gate)
    sign_ref[...] = logit_grad * route_signs(facts, folded_ref.shape[0])


def finish_kernel(folded_ref, states_ref, upstream_ref, sign_ref, router_ref, facts_ref, grads_ref, packed):
    pack_rows(folded_ref, packed)
    one, two = slot_hots(facts_ref[...], folded_ref.shape[0])
    back = dot((one + two).astype(LOW), packed[...])
    router_term = jnp.dot(
        sign_ref[...],
        router_ref[...].astype(WIDE),
        precision=lax.Precision.HIGHEST,
        preferred_element_type=WIDE,
    )
    input_total = back + router_term
    grads_ref[...] = upstream_ref[...] + norm_back(states_ref[...].astype(WIDE), input_total)


def local(kernel, out_shape, *operands, scalars=0, scratch=(), late=(), sent=(), held=()):
    single = not isinstance(out_shape, tuple)
    shapes = (out_shape,) if single else out_shape
    count = len(operands)
    total = count + len(shapes)
    moved = [place for place in range(count) if place in late]
    moved += [count + place for place in range(len(shapes)) if place in sent]
    both = list(operands) + list(shapes)

    def body(*refs):
        refs, extra = list(refs[:total]), refs[total:]
        holds, semaphores = extra[: len(moved)], extra[len(moved)] if moved else None
        for number, place in enumerate(moved):
            made = Late if place < count else Sent
            refs[place] = made(refs[place], holds[number], semaphores.at[number])
        kernel(*refs, *extra[len(moved) + (1 if moved else 0) :])
        for place in moved:
            if place >= count:
                refs[place].copy.wait()

    scratches = [pltpu.VMEM(both[place].shape, both[place].dtype) for place in moved]
    if moved:
        scratches.append(pltpu.SemaphoreType.DMA((len(moved),)))
    specs = [SMEM] * scalars + [VMEM] * (total - scalars)
    for place in [*moved, *held]:
        specs[place] = pl.BlockSpec(memory_space=pltpu.HBM)
    cost = sum(x.size * x.dtype.itemsize for x in both)
    operands = [
        pltpu.with_memory_space_constraint(operand, pltpu.HBM) if place in [*late, *held] else operand
        for place, operand in enumerate(operands)
    ]
    shapes = tuple(
        pltpu.HBM(shape.shape, shape.dtype) if place in sent else shape
        for place, shape in enumerate(shapes)
    )
    result = pl.pallas_call(
        body,
        out_shape=shapes,
        in_specs=specs[:count],
        out_specs=tuple(specs[count:]),
        scratch_shapes=scratches + list(scratch),
        compiler_params=PARAMS,
        cost_estimate=pl.CostEstimate(flops=10**9, bytes_accessed=4 * cost, transcendentals=0),
    )(*operands)
    return result[0] if single else result


def shaped(shape, dtype):
    return jax.ShapeDtypeStruct(shape, dtype)


def shift(block, distance):
    count = lax.axis_size("dp")
    return lax.ppermute(block, "dp", [(i, (i + distance) % count) for i in range(count)])


def to_experts(block):
    return lax.all_to_all(block, "expert", split_axis=0, concat_axis=0, tiled=True)


def arrange(dense):
    experts, planes, double, width = dense.shape
    rows = experts * double // 2

    def blocks(count):
        return pl.BlockSpec((count, width), lambda plane: (plane, 0))

    whole, part = shaped((planes * rows, width), LOW), shaped((planes * rows // 2, width), LOW)
    return pl.pallas_call(
        dense_kernel,
        grid=(planes,),
        out_shape=(whole, whole, part, part),
        in_specs=[pl.BlockSpec((experts, 1, double, width), lambda plane: (0, plane, 0, 0))],
        out_specs=(blocks(rows), blocks(rows), blocks(rows // 2), blocks(rows // 2)),
        compiler_params=PARAMS,
        cost_estimate=pl.CostEstimate(flops=10**6, bytes_accessed=20 * 2**20, transcendentals=0),
    )(dense)


def to_holders(folded):
    experts, stack, columns = folded.shape
    rows = shaped((experts * stack // FOLD, columns * FOLD // 2), LOW)
    folded = to_experts(folded)
    token = shaped((8, LANES), WIDE)
    one, token = local(functools.partial(unfold_kernel, begin=0), (rows, token), folded)
    two, _ = local(functools.partial(unfold_kernel, begin=FOLD // 2), (rows, token), folded)
    behind_one, ahead_one = shift(one, 1), shift(one, -1)
    behind_two, ahead_two = shift(two, 1), shift(two, -1)
    far_one, far_two = shift(behind_one, 1), shift(ahead_two, -1)
    return ((one, two), (behind_one, behind_two), (ahead_one, ahead_two), (far_one, far_two)), token


def expert_terms(blocks, term):
    terms = [term(block, place) for place, block in enumerate(blocks[:3])]
    sides = (terms[1][0].astype(LOW), terms[2][1].astype(LOW))
    far, sides = lax.optimization_barrier((blocks[3], sides))
    return terms + [term(far, 3), sides]


def to_tokens(own, behind, ahead, far, sides, block):
    step_one, step_two = shift(far[0].astype(LOW), 1), shift(far[1].astype(LOW), -1)
    side_one, side_two = shift(sides[0], -1), shift(sides[1], 1)
    last_one = (ahead[0] + step_one.astype(WIDE)).astype(LOW)
    last_two = (behind[1] + step_two.astype(WIDE)).astype(LOW)
    base_one, base_two = own[0] + side_one.astype(WIDE), own[1] + side_two.astype(WIDE)
    last_one, last_two, base_one, base_two = lax.optimization_barrier(
        (last_one, last_two, base_one, base_two)
    )
    last_one, last_two = shift(last_one, 1), shift(last_two, -1)
    return to_experts(local(fold_kernel, block, base_one, last_one, base_two, last_two))


def per_device(
    states, routes, lengths, router, w_in, w_out, w_query, w_key, w_value, w_output, cotangent
):
    section = lax.axis_index("section")
    encoder_side = section == 0
    tokens_here = states[0]
    routes_here = routes[0]
    router_here = router[0].T
    routes_here = routes_here.T
    first_weight = w_in[0, 0]
    second_weight = w_out[0, 0]
    cotangent_here = cotangent[0]
    tokens, columns = tokens_here.shape
    experts = router_here.shape[0]
    capacity = max(2, 5 * TOP * tokens // (4 * experts))
    half = columns // 2
    width = HEADS * HEAD
    slot_count = experts * STRIDE
    block = shaped((experts, FOLD * capacity, columns // FOLD), LOW)
    packed = pltpu.VMEM((slot_count, columns), LOW)

    facts_shape, wide_rows = shaped((tokens, LANES), WIDE), shaped((tokens, columns), WIDE)
    folded, facts = local(
        dispatch_kernel,
        (block, facts_shape),
        tokens_here,
        routes_here,
        router_here,
        late=(0, 2),
        sent=(1,),
    )
    folded, w_query, w_key, w_value, w_output = lax.optimization_barrier(
        (folded, w_query, w_key, w_value, w_output)
    )
    own_a = jnp.where(encoder_side, w_key, w_query)
    output_wide = jnp.concatenate([w_output[:, :width], w_output[:, width:]], axis=0)
    own_b = jnp.where(encoder_side, w_value, output_wide)
    dense = jnp.concatenate([own_a, own_b], axis=0)
    others = shift(dense, 1), shift(dense, -1), shift(dense, 2)
    blocks, token = to_holders(folded)
    dense = local(
        planes_kernel,
        shaped((lax.axis_size("dp"),) + dense.shape, LOW),
        lax.axis_index("dp").reshape(1, 1),
        dense,
        *others,
        token,
        scalars=1,
    )
    dense = lax.all_gather(dense, "expert", axis=0, tiled=True)
    dense = dense.reshape(lax.axis_size("expert"), lax.axis_size("dp"), -1, width)

    actives = []

    def forward_term(rows, place):
        pre = dot(rows[0], first_weight[:half]) + dot(rows[1], first_weight[half:])
        active = jnp.maximum(pre, 0.0).astype(LOW)
        actives.append(active)
        return dot(active, second_weight[:, :half]), dot(active, second_weight[:, half:])

    terms = expert_terms(blocks, forward_term)
    back = to_tokens(*terms, block)
    full_a, full_value, full_left, full_right = arrange(dense)

    hidden_state, normed_out = local(
        combine_kernel,
        (wide_rows, shaped((tokens, columns), LOW)),
        back,
        tokens_here,
        facts,
        full_a,
        scratch=(packed,),
        late=(1, 2),
        held=(3,),
        sent=(0,),
    )
    own_length = jnp.where(encoder_side, lengths[0, 0], lengths[1, 0])
    live = jnp.arange(LEN, dtype=jnp.int32)[:, None] < own_length
    out_low = jnp.where(live & ~encoder_side, cotangent_here, jnp.zeros((), LOW))
    context_grad = (
        dot_nt(out_low[:, :half], full_left) + dot_nt(out_low[:, half:], full_right)
    ).astype(LOW)

    own_rows = dot(normed_out, full_a).astype(LOW)
    own_values = dot(normed_out, full_value).astype(LOW)
    key_rows = lax.ppermute(own_rows, "section", [(0, 1)])
    value_rows = lax.ppermute(own_values, "section", [(0, 1)])
    low_rows = shaped((tokens, width), LOW)
    value_grad, attention, kept = local(
        attend_kernel,
        (low_rows, shaped((HEADS, LEN, LEN), WIDE), shaped((3, tokens, width), LOW)),
        lengths[0].reshape(1, 1),
        own_rows,
        key_rows,
        context_grad,
        scalars=1,
        sent=(1, 2),
    )
    value_back = lax.ppermute(value_grad, "section", [(1, 0)])
    query_grad, key_grad, context = local(
        attend_back_kernel,
        (low_rows,) * 3,
        value_rows,
        attention,
        kept,
        late=(1, 2),
    )
    key_back = lax.ppermute(key_grad, "section", [(1, 0)])
    attended = jnp.concatenate([dot(context, full_left), dot(context, full_right)], axis=1)
    decoder_out = (hidden_state + attended).astype(LOW)
    forward_out = jnp.where(encoder_side, normed_out, decoder_out)
    projection_back = dot_nt(jnp.where(encoder_side, key_back, query_grad), full_a) + dot_nt(
        value_back, full_value
    )
    flags = jnp.stack([own_length, encoder_side.astype(jnp.int32)])[None]
    upstream, folded = local(
        upstream_kernel,
        (wide_rows, block),
        flags,
        hidden_state,
        projection_back,
        cotangent_here,
        facts,
        scalars=1,
        sent=(0,),
    )
    sign_grad = local(
        router_kernel,
        shaped((tokens, experts), WIDE),
        back,
        upstream,
        facts,
        scratch=(packed,),
        late=(1, 2),
    )

    def backward_term(rows, place):
        slope = dot_nt(rows[0], second_weight[:, :half]) + dot_nt(rows[1], second_weight[:, half:])
        slope = jnp.where(actives[place] > 0, slope, 0.0).astype(LOW)
        return dot_nt(slope, first_weight[:half]), dot_nt(slope, first_weight[half:])

    terms = expert_terms(to_holders(folded)[0], backward_term)
    back = to_tokens(*terms, block)
    grads = local(
        finish_kernel,
        wide_rows,
        back,
        tokens_here,
        upstream,
        sign_grad,
        router_here,
        facts,
        scratch=(packed,),
        late=(1, 2, 3, 4, 5),
    )
    return (forward_out[None], grads[None])


def solution(mesh):
    in_specs = (
        P("section", ("dp", "expert"), None),
        P("section", ("dp", "expert"), None),
        P(None, ("dp", "expert")),
        P("section", None, None),
        P("section", "expert", None, "dp"),
        P("section", "expert", "dp", None),
        P(("dp", "expert"), None),
        P(("dp", "expert"), None),
        P(("dp", "expert"), None),
        P(("dp", "expert"), None),
        P("section", ("dp", "expert"), None),
    )
    out_specs = (P("section", ("dp", "expert"), None), P("section", ("dp", "expert"), None))
    return jax.shard_map(
        per_device, mesh=mesh, in_specs=in_specs, out_specs=out_specs, check_vma=False
    )
```

```python
import functools

import jax
import jax.numpy as jnp
from jax import lax
from jax.experimental import pallas as pl
from jax.experimental.pallas import tpu as pltpu
from jax.sharding import PartitionSpec as P

HEADS = 8
HEAD = 128
TOP = 2
LEN = 128
STRIDE = 32
FOLD = 2
LANES = 128
PLANES = 4


EPS = 1e-05
NEG_FILL = -1e30
LOW = jnp.bfloat16
WIDE = jnp.float32
VMEM = pl.BlockSpec(memory_space=pltpu.VMEM)
SMEM = pl.BlockSpec(memory_space=pltpu.SMEM)
PARAMS = pltpu.CompilerParams(vmem_limit_bytes=20 * 1024 * 1024)


def dot(a, b):
    return jnp.dot(a, b, preferred_element_type=WIDE)


def dot_nt(a, b):
    return lax.dot_general(a, b, (((1,), (1,)), ((), ())), preferred_element_type=WIDE)


def dot_tn(a, b):
    return lax.dot_general(a, b, (((0,), (0,)), ((), ())), preferred_element_type=WIDE)


def normalised(values):
    centred = values - jnp.mean(values, axis=-1, keepdims=True)
    variance = jnp.mean(centred * centred, axis=-1, keepdims=True)
    inverse = lax.rsqrt(variance + EPS)
    return centred * inverse, inverse


def norm_back(values, upstream):
    normed, inverse = normalised(values)
    return inverse * (
        upstream
        - jnp.mean(upstream, axis=-1, keepdims=True)
        - normed * jnp.mean(upstream * normed, axis=-1, keepdims=True)
    )


class Late:
    def __init__(self, source, held, semaphore):
        self.copy = pltpu.make_async_copy(source, held, semaphore)
        self.held, self.shape, self.dtype, self.waiting = held, held.shape, held.dtype, True
        self.copy.start()

    def __getitem__(self, index):
        if self.waiting:
            self.copy.wait()
            self.waiting = False
        return self.held[index]


class Sent:
    def __init__(self, target, held, semaphore):
        self.copy = pltpu.make_async_copy(held, target, semaphore)
        self.held, self.shape, self.dtype = held, held.shape, held.dtype

    def __setitem__(self, index, value):
        self.held[index] = value

    def send(self):
        self.copy.start()


def laned(columns):
    lane = lax.broadcasted_iota(jnp.int32, (columns[0].shape[0], LANES), 1)
    return sum(jnp.where(lane == place, column, 0.0) for place, column in enumerate(columns))


def split_low(column, parts):
    pieces = []
    for _ in range(parts):
        piece = column.astype(LOW).astype(WIDE)
        pieces.append(piece)
        column = column - piece
    return pieces


def plane_hots(facts, slots, capacity):
    tokens = facts.shape[0]
    plane = lax.broadcasted_iota(jnp.int32, (tokens, 1), 0) // (tokens // PLANES)
    place = lax.broadcasted_iota(jnp.int32, (tokens, slots), 1)

    def hot(route, rank):
        wanted = (route * (PLANES * capacity) + rank).astype(jnp.int32) + plane * capacity
        return jnp.where(place == wanted, 1.0, 0.0)

    return hot(facts[:, 0:1], facts[:, 1:2]), hot(facts[:, 2:3], facts[:, 3:4])


def plane_gates(facts):
    return facts[:, 4:5] + facts[:, 5:6] + facts[:, 6:7]


def slot_hots(facts, experts):
    place = lax.broadcasted_iota(jnp.int32, (facts.shape[0], experts * STRIDE), 1)
    return tuple(
        jnp.where(place == (facts[:, at : at + 1] * STRIDE + facts[:, at + 1 : at + 2]).astype(jnp.int32), 1.0, 0.0)
        for at in (0, 2)
    )


def route_signs(facts, experts):
    ids = lax.broadcasted_iota(jnp.int32, (facts.shape[0], experts), 1).astype(WIDE)
    return jnp.where(facts[:, 0:1] == ids, 1.0, 0.0) - jnp.where(facts[:, 2:3] == ids, 1.0, 0.0)


def spread_rows(rows, folded_ref):
    experts, stack, columns = folded_ref.shape
    capacity = stack // FOLD
    for e in range(experts):
        block = rows[e * STRIDE : e * STRIDE + capacity].astype(LOW)
        for place in range(FOLD):
            folded_ref[e, pl.ds(place * capacity, capacity), :] = block[
                :, place * columns : (place + 1) * columns
            ]


def pack_rows(folded_ref, packed):
    experts, stack, columns = folded_ref.shape
    capacity = stack // FOLD
    packed[...] = jnp.zeros_like(packed)
    for e in range(experts):
        for place in range(FOLD):
            packed[pl.ds(e * STRIDE, capacity), pl.ds(place * columns, columns)] = folded_ref[
                e, pl.ds(place * capacity, capacity), :
            ]


def unfold_kernel(folded_ref, rows_ref, token_ref, *, begin):
    token_ref[...] = jnp.zeros_like(token_ref)
    experts, stack, columns = folded_ref.shape
    capacity = stack // FOLD
    for e in range(experts):
        for place in range(FOLD // 2):
            rows_ref[pl.ds(e * capacity, capacity), pl.ds(place * columns, columns)] = folded_ref[
                e, pl.ds((begin + place) * capacity, capacity), :
            ]


def fold_kernel(*refs):
    folded_ref = refs[-1]
    experts, stack, columns = folded_ref.shape
    capacity = stack // FOLD
    for begin in range(2):
        base_ref, last_ref = refs[begin * 2 : begin * 2 + 2]
        total = (base_ref[...] + last_ref[...].astype(WIDE)).astype(LOW)
        for e in range(experts):
            for place in range(FOLD // 2):
                folded_ref[e, pl.ds((begin * FOLD // 2 + place) * capacity, capacity), :] = total[
                    e * capacity : (e + 1) * capacity, place * columns : (place + 1) * columns
                ]


def planes_kernel(place_ref, own_ref, behind_ref, ahead_ref, far_ref, token_ref, planes_ref):
    count = planes_ref.shape[0]
    for distance, ref in ((0, own_ref), (count - 1, behind_ref), (1, ahead_ref), (2, far_ref)):
        planes_ref[lax.rem(place_ref[0, 0] + distance, count)] = ref[...]


def dense_kernel(dense_ref, first_ref, second_ref, left_ref, right_ref):
    experts, _, double, width = dense_ref.shape
    rows = double // 2
    first_ref[...] = dense_ref[:, 0, :rows].reshape(experts * rows, width)
    second = dense_ref[:, 0, rows:]
    second_ref[...] = second.reshape(experts * rows, width)
    left_ref[...] = second[:, : rows // 2].reshape(experts * rows // 2, width)
    right_ref[...] = second[:, rows // 2 :].reshape(experts * rows // 2, width)


def dispatch_kernel(states_ref, routes_ref, router_ref, folded_ref, block_ref, facts_ref):
    experts = folded_ref.shape[0]
    tokens, columns = states_ref.shape
    near = folded_ref.shape[2] * FOLD
    ids = lax.broadcasted_iota(jnp.int32, (experts, tokens), 0)
    row = lax.broadcasted_iota(jnp.int32, (experts, experts), 0)
    column = lax.broadcasted_iota(jnp.int32, (experts, experts), 1)
    same = jnp.where(row == column, 1.0, 0.0).astype(LOW)
    hots = [
        dot_tn(jnp.where(routes_ref[k : k + 1, :] == ids, 1.0, 0.0).astype(LOW), same)
        for k in range(TOP)
    ]
    row = lax.broadcasted_iota(jnp.int32, (tokens, tokens), 0)
    column = lax.broadcasted_iota(jnp.int32, (tokens, tokens), 1)
    earlier = jnp.where(column < row, 1.0, 0.0).astype(LOW)
    rank = dot(earlier, (hots[0] + hots[1]).astype(LOW))
    number = lax.broadcasted_iota(jnp.int32, (tokens, experts), 1).astype(WIDE)
    facts = []
    for hot in hots:
        facts.append(jnp.sum(hot * number, axis=1, keepdims=True))
        facts.append(jnp.sum(hot * rank, axis=1, keepdims=True))
    normed = normalised(states_ref[...].astype(WIDE))[0].astype(LOW)
    logits = dot_nt(normed, router_ref[...])
    spread = jnp.sum(hots[0] * logits - hots[1] * logits, axis=1, keepdims=True)
    gate = jax.nn.sigmoid(spread)
    block_ref[:, : columns - near] = normed[:, near:]
    block_ref[:, columns - near :] = laned(facts + split_low(gate, 3)).astype(LOW)
    facts = laned(facts + [gate])
    facts_ref[...] = facts
    facts_ref.send()
    one, two = slot_hots(facts, experts)
    spread_rows(dot_tn((one + two).astype(LOW), normed[:, :near]), folded_ref)


def plane_dispatch_kernel(token_ref, own_ref, behind_ref, ahead_ref, far_ref, slots_ref, facts_ref):
    experts, rows, width = slots_ref.shape
    refs = (own_ref, behind_ref, ahead_ref, far_ref)
    facts = jnp.concatenate([ref[:, width:] for ref in refs], axis=0).astype(WIDE)
    facts_ref[...] = facts
    facts_ref.send()
    one, two = plane_hots(facts, experts * rows, rows // PLANES)
    table = jnp.concatenate([ref[:, :width] for ref in refs], axis=0)
    spread = dot_tn((one + two).astype(LOW), table)
    slots_ref[...] = spread.astype(LOW).reshape(slots_ref.shape)


def plane_combine_kernel(slots_ref, facts_ref, sum_ref, to_behind_ref, to_ahead_ref, to_far_ref, apart_ref):
    experts, rows, width = slots_ref.shape
    facts = facts_ref[...]
    one, two = plane_hots(facts, experts * rows, rows // PLANES)
    table = slots_ref[...].reshape(experts * rows, width)
    first, second = dot(one.astype(LOW), table), dot(two.astype(LOW), table)
    apart_ref[...] = first - second
    apart_ref.send()
    gate = plane_gates(facts)
    mixed = gate * first + (1.0 - gate) * second
    tokens = sum_ref.shape[0]
    sum_ref[...] = mixed[:tokens]
    for place, ref in enumerate((to_behind_ref, to_ahead_ref, to_far_ref)):
        ref[...] = mixed[(place + 1) * tokens : (place + 2) * tokens].astype(LOW)


def plane_slope_kernel(token_ref, own_ref, behind_ref, ahead_ref, far_ref, facts_ref, slots_ref, ups_ref):
    experts, rows, width = slots_ref.shape
    ups = jnp.concatenate([ref[...] for ref in (own_ref, behind_ref, ahead_ref, far_ref)], axis=0)
    ups_ref[...] = ups
    ups_ref.send()
    facts = facts_ref[...]
    one, two = plane_hots(facts, experts * rows, rows // PLANES)
    gate, ups = plane_gates(facts), ups.astype(WIDE)
    spread = dot_tn(one.astype(LOW), (gate * ups).astype(LOW)) + dot_tn(
        two.astype(LOW), ((1.0 - gate) * ups).astype(LOW)
    )
    slots_ref[...] = spread.astype(LOW).reshape(slots_ref.shape)


def plane_back_kernel(slots_ref, facts_ref, ups_ref, apart_ref, sum_ref, to_behind_ref, to_ahead_ref, to_far_ref):
    experts, rows, width = slots_ref.shape
    one, two = plane_hots(facts_ref[...], experts * rows, rows // PLANES)
    back = dot((one + two).astype(LOW), slots_ref[...].reshape(experts * rows, width))
    gate_grad = jnp.sum(ups_ref[...].astype(WIDE) * apart_ref[...], axis=1, keepdims=True)
    extra = laned(split_low(gate_grad, 2))
    tokens = sum_ref.shape[0]
    for place, ref in enumerate((sum_ref, to_behind_ref, to_ahead_ref, to_far_ref)):
        at = slice(place * tokens, (place + 1) * tokens)
        ref[:, :width] = back[at].astype(ref.dtype)
        ref[:, width:] = extra[at].astype(ref.dtype)


def unpack_kernel(slots_ref, *plane_refs):
    experts, rows, _ = slots_ref.shape
    capacity = rows // PLANES
    for e in range(experts):
        for place, ref in enumerate(plane_refs):
            ref[pl.ds(e * capacity, capacity), :] = slots_ref[e, pl.ds(place * capacity, capacity), :]


def pack_kernel(*refs):
    plane_refs, slots_ref = refs[:PLANES], refs[-1]
    experts, rows, _ = slots_ref.shape
    capacity = rows // PLANES
    for e in range(experts):
        for place, ref in enumerate(plane_refs):
            slots_ref[e, pl.ds(place * capacity, capacity), :] = ref[pl.ds(e * capacity, capacity), :]


def others_total(own_ref, behind_ref, ahead_ref, far_ref):
    total = own_ref[...] + behind_ref[...].astype(WIDE)
    return total + ahead_ref[...].astype(WIDE) + far_ref[...].astype(WIDE)


def combine_kernel(folded_ref, states_ref, facts_ref, ready_ref, own_ref, behind_ref, ahead_ref, far_ref, hidden_ref, normed_ref, packed):
    pack_rows(folded_ref, packed)
    rows = packed[...]
    near = rows.shape[1]
    facts = facts_ref[...]
    gate = facts[:, 4:5]
    one, two = slot_hots(facts, folded_ref.shape[0])
    mixed = gate * dot(one.astype(LOW), rows) + (1.0 - gate) * dot(two.astype(LOW), rows)
    others = others_total(own_ref, behind_ref, ahead_ref, far_ref)
    hidden = states_ref[...].astype(WIDE) + jnp.concatenate([mixed, others], axis=1)
    hidden_ref[...] = hidden
    hidden_ref.send()
    normed_ref[...] = normalised(hidden)[0].astype(LOW)


def attend_kernel(length_ref, q_ref, k_ref, grad_ref, v_grad_ref, attention_ref, kept_ref):
    kept_ref[0], kept_ref[1], kept_ref[2] = q_ref[...], k_ref[...], grad_ref[...]
    kept_ref.send()
    scale = HEAD ** (-0.5)
    live = lax.broadcasted_iota(jnp.int32, (LEN, LEN), 1) < length_ref[0, 0]
    for head in range(HEADS):
        at = slice(head * HEAD, (head + 1) * HEAD)
        scores = jnp.where(live, dot_nt(q_ref[:, at], k_ref[:, at]) * scale, NEG_FILL)
        exponent = jnp.exp(scores - jnp.max(scores, axis=-1, keepdims=True))
        attention = exponent / jnp.sum(exponent, axis=-1, keepdims=True)
        attention_ref[head] = attention
        v_grad_ref[:, at] = dot_tn(attention.astype(LOW), grad_ref[:, at]).astype(LOW)
    attention_ref.send()


def attend_back_kernel(v_ref, attention_ref, kept_ref, q_grad_ref, k_grad_ref, context_ref):
    scale = HEAD ** (-0.5)
    for head in range(HEADS):
        at = slice(head * HEAD, (head + 1) * HEAD)
        attention, v = attention_ref[head], v_ref[:, at]
        q, k, grad = kept_ref[0, :, at], kept_ref[1, :, at], kept_ref[2, :, at]
        weight_grad = dot_nt(grad, v)
        score_grad = (
            attention
            * (weight_grad - jnp.sum(attention * weight_grad, axis=-1, keepdims=True))
            * scale
        ).astype(LOW)
        k_grad_ref[:, at] = dot_tn(score_grad, q).astype(LOW)
        q_grad_ref[:, at] = dot(score_grad, k).astype(LOW)
        context_ref[:, at] = dot(attention.astype(LOW), v).astype(LOW)


def upstream_kernel(flags_ref, hidden_ref, back_ref, cotangent_ref, facts_ref, upstream_ref, folded_ref, up_ref):
    near = folded_ref.shape[2] * FOLD
    live = lax.broadcasted_iota(jnp.int32, (LEN, 1), 0) < flags_ref[0, 0]
    encoder = flags_ref[0, 1] == 1
    masked = jnp.where(live, cotangent_ref[...].astype(WIDE), 0.0)
    out_grad = jnp.where(encoder, 0.0, masked)
    normed_grad = back_ref[...] + jnp.where(encoder, masked, 0.0)
    upstream = out_grad + norm_back(hidden_ref[...], normed_grad)
    upstream_ref[...] = upstream
    upstream_ref.send()
    up_ref[...] = upstream[:, near:].astype(LOW)
    upstream = upstream[:, :near]
    facts = facts_ref[...]
    gate = facts[:, 4:5]
    one, two = slot_hots(facts, folded_ref.shape[0])
    rows = dot_tn(one.astype(LOW), (gate * upstream).astype(LOW)) + dot_tn(
        two.astype(LOW), ((1.0 - gate) * upstream).astype(LOW)
    )
    spread_rows(rows, folded_ref)


def gate_kernel(folded_ref, upstream_ref, facts_ref, gate_grad_ref, packed):
    pack_rows(folded_ref, packed)
    rows = packed[...]
    one, two = slot_hots(facts_ref[...], folded_ref.shape[0])
    apart = dot(one.astype(LOW), rows) - dot(two.astype(LOW), rows)
    gate_grad = jnp.sum(upstream_ref[:, : rows.shape[1]] * apart, axis=1, keepdims=True)
    gate_grad_ref[...] = laned([gate_grad])


def finish_kernel(folded_ref, states_ref, upstream_ref, gate_grad_ref, router_ref, facts_ref, own_ref, behind_ref, ahead_ref, far_ref, grads_ref, packed):
    pack_rows(folded_ref, packed)
    experts = folded_ref.shape[0]
    facts = facts_ref[...]
    one, two = slot_hots(facts, experts)
    back = dot((one + two).astype(LOW), packed[...])
    others = others_total(own_ref, behind_ref, ahead_ref, far_ref)
    far = others.shape[1] - LANES
    gate = facts[:, 4:5]
    gate_grad = gate_grad_ref[:, 0:1] + others[:, far : far + 1] + others[:, far + 1 : far + 2]
    logit_grad = gate_grad * gate * (1.0 - gate)
    router_term = jnp.dot(
        logit_grad * route_signs(facts, experts),
        router_ref[...].astype(WIDE),
        precision=lax.Precision.HIGHEST,
        preferred_element_type=WIDE,
    )
    input_total = jnp.concatenate([back, others[:, :far]], axis=1) + router_term
    grads_ref[...] = upstream_ref[...] + norm_back(states_ref[...].astype(WIDE), input_total)


def local(kernel, out_shape, *operands, scalars=0, scratch=(), late=(), sent=(), held=()):
    single = not isinstance(out_shape, tuple)
    shapes = (out_shape,) if single else out_shape
    count = len(operands)
    total = count + len(shapes)
    moved = [place for place in range(count) if place in late]
    moved += [count + place for place in range(len(shapes)) if place in sent]
    both = list(operands) + list(shapes)

    def body(*refs):
        refs, extra = list(refs[:total]), refs[total:]
        holds, semaphores = extra[: len(moved)], extra[len(moved)] if moved else None
        for number, place in enumerate(moved):
            made = Late if place < count else Sent
            refs[place] = made(refs[place], holds[number], semaphores.at[number])
        kernel(*refs, *extra[len(moved) + (1 if moved else 0) :])
        for place in moved:
            if place >= count:
                refs[place].copy.wait()

    scratches = [pltpu.VMEM(both[place].shape, both[place].dtype) for place in moved]
    if moved:
        scratches.append(pltpu.SemaphoreType.DMA((len(moved),)))
    specs = [SMEM] * scalars + [VMEM] * (total - scalars)
    for place in [*moved, *held]:
        specs[place] = pl.BlockSpec(memory_space=pltpu.HBM)
    cost = sum(x.size * x.dtype.itemsize for x in both)
    operands = [
        pltpu.with_memory_space_constraint(operand, pltpu.HBM) if place in [*late, *held] else operand
        for place, operand in enumerate(operands)
    ]
    shapes = tuple(
        pltpu.HBM(shape.shape, shape.dtype) if place in sent else shape
        for place, shape in enumerate(shapes)
    )
    result = pl.pallas_call(
        body,
        out_shape=shapes,
        in_specs=specs[:count],
        out_specs=tuple(specs[count:]),
        scratch_shapes=scratches + list(scratch),
        compiler_params=PARAMS,
        cost_estimate=pl.CostEstimate(flops=10**9, bytes_accessed=4 * cost, transcendentals=0),
    )(*operands)
    return result[0] if single else result


def shaped(shape, dtype):
    return jax.ShapeDtypeStruct(shape, dtype)


def shift(block, distance):
    count = lax.axis_size("dp")
    return lax.ppermute(block, "dp", [(i, (i + distance) % count) for i in range(count)])


def to_experts(block):
    return lax.all_to_all(block, "expert", split_axis=0, concat_axis=0, tiled=True)


def arrange(dense):
    experts, planes, double, width = dense.shape
    rows = experts * double // 2

    def blocks(count):
        return pl.BlockSpec((count, width), lambda plane: (plane, 0))

    whole, part = shaped((planes * rows, width), LOW), shaped((planes * rows // 2, width), LOW)
    return pl.pallas_call(
        dense_kernel,
        grid=(planes,),
        out_shape=(whole, whole, part, part),
        in_specs=[pl.BlockSpec((experts, 1, double, width), lambda plane: (0, plane, 0, 0))],
        out_specs=(blocks(rows), blocks(rows), blocks(rows // 2), blocks(rows // 2)),
        compiler_params=PARAMS,
        cost_estimate=pl.CostEstimate(flops=10**6, bytes_accessed=20 * 2**20, transcendentals=0),
    )(dense)


def from_planes(block):
    return block, shift(block, 1), shift(block, -1), shift(block, 2)


def to_planes(own, behind, ahead, far):
    return own, shift(behind, -1), shift(ahead, 1), shift(far, 2)


def to_holders(folded, spread):
    experts, stack, columns = folded.shape
    rows = shaped((experts * stack // FOLD, columns * FOLD // 2), LOW)
    folded = to_experts(folded)
    token = shaped((8, LANES), WIDE)
    one, token = local(functools.partial(unfold_kernel, begin=0), (rows, token), folded)
    two, _ = local(functools.partial(unfold_kernel, begin=FOLD // 2), (rows, token), folded)
    behind_one, ahead_one = shift(one, 1), shift(one, -1)
    behind_two, ahead_two = shift(two, 1), shift(two, -1)
    far_one, far_two = shift(behind_one, 1), shift(ahead_two, -1)
    slots, kept = spread(token)
    tail = shaped((experts * stack // FOLD, slots.shape[2]), LOW)
    tails = local(unpack_kernel, (tail,) * PLANES, to_experts(slots))
    nears = ((one, two), (behind_one, behind_two), (ahead_one, ahead_two), (far_one, far_two))
    return [near + (tail,) for near, tail in zip(nears, tails)], token, kept


def to_tokens(own, behind, ahead, far, block, far_block):
    step_one, step_two = far[0].astype(LOW), far[1].astype(LOW)
    tails = [term[2].astype(LOW) for term in (own, behind, ahead, far)]
    tails = to_experts(local(pack_kernel, far_block, *tails, step_one, step_two))
    step_one, step_two = shift(step_one, 1), shift(step_two, -1)
    side_one, side_two = shift(behind[0].astype(LOW), -1), shift(ahead[1].astype(LOW), 1)
    last_one = (ahead[0] + step_one.astype(WIDE)).astype(LOW)
    last_two = (behind[1] + step_two.astype(WIDE)).astype(LOW)
    base_one, base_two = own[0] + side_one.astype(WIDE), own[1] + side_two.astype(WIDE)
    last_one, last_two, base_one, base_two = lax.optimization_barrier(
        (last_one, last_two, base_one, base_two)
    )
    last_one, last_two = shift(last_one, 1), shift(last_two, -1)
    folded = local(fold_kernel, block, base_one, last_one, base_two, last_two)
    return to_experts(folded), tails


def per_device(
    states, routes, lengths, router, w_in, w_out, w_query, w_key, w_value, w_output, cotangent
):
    section = lax.axis_index("section")
    encoder_side = section == 0
    tokens_here = states[0]
    routes_here = routes[0]
    router_here = router[0].T
    routes_here = routes_here.T
    first_weight = w_in[0, 0]
    second_weight = w_out[0, 0]
    cotangent_here = cotangent[0]
    tokens, columns = tokens_here.shape
    experts = router_here.shape[0]
    capacity = max(2, 5 * TOP * tokens // (4 * experts))
    half = columns // 2
    width = HEADS * HEAD
    slot_count = experts * STRIDE
    far = columns // 4
    near = columns - far
    edges = (slice(0, near // 2), slice(near // 2, near), slice(near, columns))
    near_slots = shaped((experts, FOLD * capacity, near // FOLD), LOW)
    far_slots = shaped((experts, PLANES * capacity, far), LOW)
    far_low = shaped((tokens, far), LOW)
    packed = pltpu.VMEM((slot_count, near), LOW)

    facts_shape, wide_rows = shaped((tokens, LANES), WIDE), shaped((tokens, columns), WIDE)
    folded, block, facts = local(
        dispatch_kernel,
        (near_slots, shaped((tokens, far + LANES), LOW), facts_shape),
        tokens_here,
        routes_here,
        router_here,
        late=(0, 2),
        sent=(2,),
    )
    folded, w_query, w_key, w_value, w_output = lax.optimization_barrier(
        (folded, w_query, w_key, w_value, w_output)
    )
    own_a = jnp.where(encoder_side, w_key, w_query)
    output_wide = jnp.concatenate([w_output[:, :width], w_output[:, width:]], axis=0)
    own_b = jnp.where(encoder_side, w_value, output_wide)
    dense = jnp.concatenate([own_a, own_b], axis=0)
    others = shift(dense, 1), shift(dense, -1), shift(dense, 2)
    blocks = from_planes(block)
    plane_facts = shaped((PLANES * tokens, LANES), WIDE)

    def spread(token):
        return local(plane_dispatch_kernel, (far_slots, plane_facts), token, *blocks, sent=(1,))

    rows, token, plane_facts = to_holders(folded, spread)
    dense = local(
        planes_kernel,
        shaped((lax.axis_size("dp"),) + dense.shape, LOW),
        lax.axis_index("dp").reshape(1, 1),
        dense,
        *others,
        token,
        scalars=1,
    )
    dense = lax.all_gather(dense, "expert", axis=0, tiled=True)
    dense = dense.reshape(lax.axis_size("expert"), lax.axis_size("dp"), -1, width)

    actives = []

    def forward_term(rows):
        pre = sum(dot(part, first_weight[edge]) for part, edge in zip(rows, edges))
        active = jnp.maximum(pre, 0.0).astype(LOW)
        actives.append(active)
        return tuple(dot(active, second_weight[:, edge]) for edge in edges)

    back, far_back = to_tokens(*[forward_term(part) for part in rows], near_slots, far_slots)
    *far_sums, apart = local(
        plane_combine_kernel,
        (shaped((tokens, far), WIDE), far_low, far_low, far_low, shaped((PLANES * tokens, far), WIDE)),
        far_back,
        plane_facts,
        late=(1,),
        sent=(4,),
    )
    full_a, full_value, full_left, full_right = arrange(dense)

    hidden_state, normed_out = local(
        combine_kernel,
        (wide_rows, shaped((tokens, columns), LOW)),
        back,
        tokens_here,
        facts,
        full_a,
        *to_planes(*far_sums),
        scratch=(packed,),
        late=(1, 2),
        held=(3,),
        sent=(0,),
    )
    own_length = jnp.where(encoder_side, lengths[0, 0], lengths[1, 0])
    live = jnp.arange(LEN, dtype=jnp.int32)[:, None] < own_length
    out_low = jnp.where(live & ~encoder_side, cotangent_here, jnp.zeros((), LOW))
    context_grad = (
        dot_nt(out_low[:, :half], full_left) + dot_nt(out_low[:, half:], full_right)
    ).astype(LOW)

    own_rows = dot(normed_out, full_a).astype(LOW)
    own_values = dot(normed_out, full_value).astype(LOW)
    key_rows = lax.ppermute(own_rows, "section", [(0, 1)])
    value_rows = lax.ppermute(own_values, "section", [(0, 1)])
    low_rows = shaped((tokens, width), LOW)
    value_grad, attention, kept = local(
        attend_kernel,
        (low_rows, shaped((HEADS, LEN, LEN), WIDE), shaped((3, tokens, width), LOW)),
        lengths[0].reshape(1, 1),
        own_rows,
        key_rows,
        context_grad,
        scalars=1,
        sent=(1, 2),
    )
    value_back = lax.ppermute(value_grad, "section", [(1, 0)])
    query_grad, key_grad, context = local(
        attend_back_kernel,
        (low_rows,) * 3,
        value_rows,
        attention,
        kept,
        late=(1, 2),
    )
    key_back = lax.ppermute(key_grad, "section", [(1, 0)])
    attended = jnp.concatenate([dot(context, full_left), dot(context, full_right)], axis=1)
    decoder_out = (hidden_state + attended).astype(LOW)
    forward_out = jnp.where(encoder_side, normed_out, decoder_out)
    projection_back = dot_nt(jnp.where(encoder_side, key_back, query_grad), full_a) + dot_nt(
        value_back, full_value
    )
    flags = jnp.stack([own_length, encoder_side.astype(jnp.int32)])[None]
    upstream, folded, up = local(
        upstream_kernel,
        (wide_rows, near_slots, far_low),
        flags,
        hidden_state,
        projection_back,
        cotangent_here,
        facts,
        scalars=1,
        sent=(0,),
    )
    gate_grad = local(
        gate_kernel, facts_shape, back, upstream, facts, scratch=(packed,), late=(1, 2)
    )
    ups = from_planes(up)

    def spread_back(token):
        return local(
            plane_slope_kernel,
            (far_slots, shaped((PLANES * tokens, far), LOW)),
            token,
            *ups,
            plane_facts,
            late=(5,),
            sent=(1,),
        )

    rows, _, ups_kept = to_holders(folded, spread_back)

    def backward_term(rows, active):
        slope = sum(dot_nt(part, second_weight[:, edge]) for part, edge in zip(rows, edges))
        slope = jnp.where(active > 0, slope, 0.0).astype(LOW)
        return tuple(dot_nt(slope, first_weight[edge]) for edge in edges)

    terms = [backward_term(part, active) for part, active in zip(rows, actives)]
    back, far_back = to_tokens(*terms, near_slots, far_slots)
    far_low = shaped((tokens, far + LANES), LOW)
    far_sums = local(
        plane_back_kernel,
        (shaped((tokens, far + LANES), WIDE), far_low, far_low, far_low),
        far_back,
        plane_facts,
        ups_kept,
        apart,
        late=(1, 2, 3),
    )
    grads = local(
        finish_kernel,
        wide_rows,
        back,
        tokens_here,
        upstream,
        gate_grad,
        router_here,
        facts,
        *to_planes(*far_sums),
        scratch=(packed,),
        late=(1, 2, 3, 4, 5),
    )
    return (forward_out[None], grads[None])


def solution(mesh):
    in_specs = (
        P("section", ("dp", "expert"), None),
        P("section", ("dp", "expert"), None),
        P(None, ("dp", "expert")),
        P("section", None, None),
        P("section", "expert", None, "dp"),
        P("section", "expert", "dp", None),
        P(("dp", "expert"), None),
        P(("dp", "expert"), None),
        P(("dp", "expert"), None),
        P(("dp", "expert"), None),
        P("section", ("dp", "expert"), None),
    )
    out_specs = (P("section", ("dp", "expert"), None), P("section", ("dp", "expert"), None))
    return jax.shard_map(
        per_device, mesh=mesh, in_specs=in_specs, out_specs=out_specs, check_vma=False
    )
```

```python
import functools

import jax
import jax.numpy as jnp
from jax import lax
from jax.experimental import pallas as pl
from jax.experimental.pallas import tpu as pltpu
from jax.sharding import PartitionSpec as P

HEADS = 8
HEAD = 128
TOP = 2
LEN = 128
STRIDE = 32
FOLD = 4
LANES = 128


EPS = 1e-05
NEG_FILL = -1e30
LOW = jnp.bfloat16
WIDE = jnp.float32
VMEM = pl.BlockSpec(memory_space=pltpu.VMEM)
SMEM = pl.BlockSpec(memory_space=pltpu.SMEM)
PARAMS = pltpu.CompilerParams(vmem_limit_bytes=20 * 1024 * 1024)


def dot(a, b):
    return jnp.dot(a, b, preferred_element_type=WIDE)


def dot_nt(a, b):
    return lax.dot_general(a, b, (((1,), (1,)), ((), ())), preferred_element_type=WIDE)


def dot_tn(a, b):
    return lax.dot_general(a, b, (((0,), (0,)), ((), ())), preferred_element_type=WIDE)


def normalised(values):
    centred = values - jnp.mean(values, axis=-1, keepdims=True)
    variance = jnp.mean(centred * centred, axis=-1, keepdims=True)
    inverse = lax.rsqrt(variance + EPS)
    return centred * inverse, inverse


def norm_back(values, upstream):
    normed, inverse = normalised(values)
    return inverse * (
        upstream
        - jnp.mean(upstream, axis=-1, keepdims=True)
        - normed * jnp.mean(upstream * normed, axis=-1, keepdims=True)
    )


class Late:
    def __init__(self, source, held, semaphore):
        self.copy = pltpu.make_async_copy(source, held, semaphore)
        self.held, self.shape, self.dtype, self.waiting = held, held.shape, held.dtype, True
        self.copy.start()

    def __getitem__(self, index):
        if self.waiting:
            self.copy.wait()
            self.waiting = False
        return self.held[index]


class Sent:
    def __init__(self, target, held, semaphore):
        self.copy = pltpu.make_async_copy(held, target, semaphore)
        self.held, self.shape, self.dtype = held, held.shape, held.dtype

    def __setitem__(self, index, value):
        self.held[index] = value

    def send(self):
        self.copy.start()


def laned(columns):
    lane = lax.broadcasted_iota(jnp.int32, (columns[0].shape[0], LANES), 1)
    return sum(jnp.where(lane == place, column, 0.0) for place, column in enumerate(columns))


def slot_hots(facts, experts):
    place = lax.broadcasted_iota(jnp.int32, (facts.shape[0], experts * STRIDE), 1)
    return tuple(
        jnp.where(place == (facts[:, at : at + 1] * STRIDE + facts[:, at + 1 : at + 2]).astype(jnp.int32), 1.0, 0.0)
        for at in (0, 2)
    )


def route_signs(facts, experts):
    ids = lax.broadcasted_iota(jnp.int32, (facts.shape[0], experts), 1).astype(WIDE)
    return jnp.where(facts[:, 0:1] == ids, 1.0, 0.0) - jnp.where(facts[:, 2:3] == ids, 1.0, 0.0)


def spread_rows(rows, folded_ref):
    experts, stack, columns = folded_ref.shape
    capacity = stack // FOLD
    for e in range(experts):
        block = rows[e * STRIDE : e * STRIDE + capacity].astype(LOW)
        for place in range(FOLD):
            folded_ref[e, pl.ds(place * capacity, capacity), :] = block[
                :, place * columns : (place + 1) * columns
            ]


def pack_rows(folded_ref, packed):
    experts, stack, columns = folded_ref.shape
    capacity = stack // FOLD
    packed[...] = jnp.zeros_like(packed)
    for e in range(experts):
        for place in range(FOLD):
            packed[pl.ds(e * STRIDE, capacity), pl.ds(place * columns, columns)] = folded_ref[
                e, pl.ds(place * capacity, capacity), :
            ]


def unfold_kernel(folded_ref, rows_ref, token_ref, *, begin):
    token_ref[...] = jnp.zeros_like(token_ref)
    experts, stack, columns = folded_ref.shape
    capacity = stack // FOLD
    for e in range(experts):
        for place in range(FOLD // 2):
            rows_ref[pl.ds(e * capacity, capacity), pl.ds(place * columns, columns)] = folded_ref[
                e, pl.ds((begin + place) * capacity, capacity), :
            ]


def fold_kernel(*refs):
    folded_ref = refs[-1]
    experts, stack, columns = folded_ref.shape
    capacity = stack // FOLD
    for begin in range(2):
        own_ref, side_ref, last_ref = refs[begin * 3 : begin * 3 + 3]
        total = own_ref[...] + side_ref[...].astype(WIDE) + last_ref[...].astype(WIDE)
        total = total.astype(LOW)
        for e in range(experts):
            for place in range(FOLD // 2):
                folded_ref[e, pl.ds((begin * FOLD // 2 + place) * capacity, capacity), :] = total[
                    e * capacity : (e + 1) * capacity, place * columns : (place + 1) * columns
                ]


def planes_kernel(place_ref, own_ref, behind_ref, ahead_ref, far_ref, token_ref, planes_ref):
    count = planes_ref.shape[0]
    for distance, ref in ((0, own_ref), (count - 1, behind_ref), (1, ahead_ref), (2, far_ref)):
        planes_ref[lax.rem(place_ref[0, 0] + distance, count)] = ref[...]


def dense_kernel(dense_ref, first_ref, second_ref, left_ref, right_ref):
    experts, _, double, width = dense_ref.shape
    rows = double // 2
    first_ref[...] = dense_ref[:, 0, :rows].reshape(experts * rows, width)
    second = dense_ref[:, 0, rows:]
    second_ref[...] = second.reshape(experts * rows, width)
    left_ref[...] = second[:, : rows // 2].reshape(experts * rows // 2, width)
    right_ref[...] = second[:, rows // 2 :].reshape(experts * rows // 2, width)


def dispatch_kernel(states_ref, routes_ref, router_ref, folded_ref, facts_ref):
    experts = folded_ref.shape[0]
    tokens = states_ref.shape[0]
    ids = lax.broadcasted_iota(jnp.int32, (experts, tokens), 0)
    row = lax.broadcasted_iota(jnp.int32, (experts, experts), 0)
    column = lax.broadcasted_iota(jnp.int32, (experts, experts), 1)
    same = jnp.where(row == column, 1.0, 0.0).astype(LOW)
    hots = [
        dot_tn(jnp.where(routes_ref[k : k + 1, :] == ids, 1.0, 0.0).astype(LOW), same)
        for k in range(TOP)
    ]
    row = lax.broadcasted_iota(jnp.int32, (tokens, tokens), 0)
    column = lax.broadcasted_iota(jnp.int32, (tokens, tokens), 1)
    earlier = jnp.where(column < row, 1.0, 0.0).astype(LOW)
    rank = dot(earlier, (hots[0] + hots[1]).astype(LOW))
    number = lax.broadcasted_iota(jnp.int32, (tokens, experts), 1).astype(WIDE)
    facts = []
    for hot in hots:
        facts.append(jnp.sum(hot * number, axis=1, keepdims=True))
        facts.append(jnp.sum(hot * rank, axis=1, keepdims=True))
    normed = normalised(states_ref[...].astype(WIDE))[0].astype(LOW)
    logits = dot_nt(normed, router_ref[...])
    spread = jnp.sum(hots[0] * logits - hots[1] * logits, axis=1, keepdims=True)
    facts = laned(facts + [jax.nn.sigmoid(spread)])
    facts_ref[...] = facts
    facts_ref.send()
    one, two = slot_hots(facts, experts)
    spread_rows(dot_tn((one + two).astype(LOW), normed), folded_ref)


def combine_kernel(folded_ref, states_ref, facts_ref, ready_ref, hidden_ref, normed_ref, packed):
    pack_rows(folded_ref, packed)
    rows = packed[...]
    facts = facts_ref[...]
    gate = facts[:, 4:5]
    one, two = slot_hots(facts, folded_ref.shape[0])
    hidden = states_ref[...].astype(WIDE) + (
        gate * dot(one.astype(LOW), rows) + (1.0 - gate) * dot(two.astype(LOW), rows)
    )
    hidden_ref[...] = hidden
    hidden_ref.send()
    normed_ref[...] = normalised(hidden)[0].astype(LOW)


def attend_kernel(length_ref, q_ref, k_ref, grad_ref, v_grad_ref, attention_ref, kept_ref):
    kept_ref[0], kept_ref[1], kept_ref[2] = q_ref[...], k_ref[...], grad_ref[...]
    kept_ref.send()
    scale = HEAD ** (-0.5)
    live = lax.broadcasted_iota(jnp.int32, (LEN, LEN), 1) < length_ref[0, 0]
    for head in range(HEADS):
        at = slice(head * HEAD, (head + 1) * HEAD)
        scores = jnp.where(live, dot_nt(q_ref[:, at], k_ref[:, at]) * scale, NEG_FILL)
        exponent = jnp.exp(scores - jnp.max(scores, axis=-1, keepdims=True))
        attention = exponent / jnp.sum(exponent, axis=-1, keepdims=True)
        attention_ref[head] = attention
        v_grad_ref[:, at] = dot_tn(attention.astype(LOW), grad_ref[:, at]).astype(LOW)
    attention_ref.send()


def attend_back_kernel(v_ref, attention_ref, kept_ref, q_grad_ref, k_grad_ref, context_ref):
    scale = HEAD ** (-0.5)
    for head in range(HEADS):
        at = slice(head * HEAD, (head + 1) * HEAD)
        attention, v = attention_ref[head], v_ref[:, at]
        q, k, grad = kept_ref[0, :, at], kept_ref[1, :, at], kept_ref[2, :, at]
        weight_grad = dot_nt(grad, v)
        score_grad = (
            attention
            * (weight_grad - jnp.sum(attention * weight_grad, axis=-1, keepdims=True))
            * scale
        ).astype(LOW)
        k_grad_ref[:, at] = dot_tn(score_grad, q).astype(LOW)
        q_grad_ref[:, at] = dot(score_grad, k).astype(LOW)
        context_ref[:, at] = dot(attention.astype(LOW), v).astype(LOW)


def upstream_kernel(flags_ref, hidden_ref, back_ref, cotangent_ref, facts_ref, upstream_ref, folded_ref):
    live = lax.broadcasted_iota(jnp.int32, (LEN, 1), 0) < flags_ref[0, 0]
    encoder = flags_ref[0, 1] == 1
    masked = jnp.where(live, cotangent_ref[...].astype(WIDE), 0.0)
    out_grad = jnp.where(encoder, 0.0, masked)
    normed_grad = back_ref[...] + jnp.where(encoder, masked, 0.0)
    upstream = out_grad + norm_back(hidden_ref[...], normed_grad)
    upstream_ref[...] = upstream
    upstream_ref.send()
    facts = facts_ref[...]
    gate = facts[:, 4:5]
    one, two = slot_hots(facts, folded_ref.shape[0])
    rows = dot_tn(one.astype(LOW), (gate * upstream).astype(LOW)) + dot_tn(
        two.astype(LOW), ((1.0 - gate) * upstream).astype(LOW)
    )
    spread_rows(rows, folded_ref)


def router_kernel(folded_ref, upstream_ref, facts_ref, sign_ref, packed):
    pack_rows(folded_ref, packed)
    rows = packed[...]
    facts = facts_ref[...]
    gate = facts[:, 4:5]
    one, two = slot_hots(facts, folded_ref.shape[0])
    apart = dot(one.astype(LOW), rows) - dot(two.astype(LOW), rows)
    gate_grad = jnp.sum(upstream_ref[...] * apart, axis=1, keepdims=True)
    logit_grad = gate_grad * gate * (1.0 - gate)
    sign_ref[...] = logit_grad * route_signs(facts, folded_ref.shape[0])


def finish_kernel(folded_ref, states_ref, upstream_ref, sign_ref, router_ref, facts_ref, grads_ref, packed):
    pack_rows(folded_ref, packed)
    one, two = slot_hots(facts_ref[...], folded_ref.shape[0])
    back = dot((one + two).astype(LOW), packed[...])
    router_term = jnp.dot(
        sign_ref[...],
        router_ref[...].astype(WIDE),
        precision=lax.Precision.HIGHEST,
        preferred_element_type=WIDE,
    )
    input_total = back + router_term
    grads_ref[...] = upstream_ref[...] + norm_back(states_ref[...].astype(WIDE), input_total)


def local(kernel, out_shape, *operands, scalars=0, scratch=(), late=(), sent=(), held=()):
    single = not isinstance(out_shape, tuple)
    shapes = (out_shape,) if single else out_shape
    count = len(operands)
    total = count + len(shapes)
    moved = [place for place in range(count) if place in late]
    moved += [count + place for place in range(len(shapes)) if place in sent]
    both = list(operands) + list(shapes)

    def body(*refs):
        refs, extra = list(refs[:total]), refs[total:]
        holds, semaphores = extra[: len(moved)], extra[len(moved)] if moved else None
        for number, place in enumerate(moved):
            made = Late if place < count else Sent
            refs[place] = made(refs[place], holds[number], semaphores.at[number])
        kernel(*refs, *extra[len(moved) + (1 if moved else 0) :])
        for place in moved:
            if place >= count:
                refs[place].copy.wait()

    scratches = [pltpu.VMEM(both[place].shape, both[place].dtype) for place in moved]
    if moved:
        scratches.append(pltpu.SemaphoreType.DMA((len(moved),)))
    specs = [SMEM] * scalars + [VMEM] * (total - scalars)
    for place in [*moved, *held]:
        specs[place] = pl.BlockSpec(memory_space=pltpu.HBM)
    cost = sum(x.size * x.dtype.itemsize for x in both)
    operands = [
        pltpu.with_memory_space_constraint(operand, pltpu.HBM) if place in [*late, *held] else operand
        for place, operand in enumerate(operands)
    ]
    shapes = tuple(
        pltpu.HBM(shape.shape, shape.dtype) if place in sent else shape
        for place, shape in enumerate(shapes)
    )
    result = pl.pallas_call(
        body,
        out_shape=shapes,
        in_specs=specs[:count],
        out_specs=tuple(specs[count:]),
        scratch_shapes=scratches + list(scratch),
        compiler_params=PARAMS,
        cost_estimate=pl.CostEstimate(flops=10**9, bytes_accessed=4 * cost, transcendentals=0),
    )(*operands)
    return result[0] if single else result


def shaped(shape, dtype):
    return jax.ShapeDtypeStruct(shape, dtype)


def shift(block, distance):
    count = lax.axis_size("dp")
    return lax.ppermute(block, "dp", [(i, (i + distance) % count) for i in range(count)])


def to_experts(block):
    return lax.all_to_all(block, "expert", split_axis=0, concat_axis=0, tiled=True)


def arrange(dense):
    experts, planes, double, width = dense.shape
    rows = experts * double // 2

    def blocks(count):
        return pl.BlockSpec((count, width), lambda plane: (plane, 0))

    whole, part = shaped((planes * rows, width), LOW), shaped((planes * rows // 2, width), LOW)
    return pl.pallas_call(
        dense_kernel,
        grid=(planes,),
        out_shape=(whole, whole, part, part),
        in_specs=[pl.BlockSpec((experts, 1, double, width), lambda plane: (0, plane, 0, 0))],
        out_specs=(blocks(rows), blocks(rows), blocks(rows // 2), blocks(rows // 2)),
        compiler_params=PARAMS,
        cost_estimate=pl.CostEstimate(flops=10**6, bytes_accessed=20 * 2**20, transcendentals=0),
    )(dense)


def to_holders(folded):
    experts, stack, columns = folded.shape
    rows = shaped((experts * stack // FOLD, columns * FOLD // 2), LOW)
    folded = to_experts(folded)
    token = shaped((8, LANES), WIDE)
    one, token = local(functools.partial(unfold_kernel, begin=0), (rows, token), folded)
    two, _ = local(functools.partial(unfold_kernel, begin=FOLD // 2), (rows, token), folded)
    behind_one, ahead_one = shift(one, 1), shift(one, -1)
    behind_two, ahead_two = shift(two, 1), shift(two, -1)
    far_one, far_two = shift(behind_one, 1), shift(ahead_two, -1)
    return ((one, two), (behind_one, behind_two), (ahead_one, ahead_two), (far_one, far_two)), token


def through_experts(rows, term, block):
    behind, ahead = term(rows[1], 1), term(rows[2], 2)
    sides = (behind[0].astype(LOW), ahead[1].astype(LOW))
    far, sides = lax.optimization_barrier((rows[3], sides))
    far = term(far, 3)
    step_one, step_two = shift(far[0].astype(LOW), 1), shift(far[1].astype(LOW), -1)
    side_one, side_two = shift(sides[0], -1), shift(sides[1], 1)
    last_one = (ahead[0] + step_one.astype(WIDE)).astype(LOW)
    last_two = (behind[1] + step_two.astype(WIDE)).astype(LOW)
    last_one, last_two, side_one, side_two, own = lax.optimization_barrier(
        (last_one, last_two, side_one, side_two, rows[0])
    )
    last_one, last_two = shift(last_one, 1), shift(last_two, -1)
    own = term(own, 0)
    folded = local(fold_kernel, block, own[0], side_one, last_one, own[1], side_two, last_two)
    return to_experts(folded)


def per_device(
    states, routes, lengths, router, w_in, w_out, w_query, w_key, w_value, w_output, cotangent
):
    section = lax.axis_index("section")
    encoder_side = section == 0
    tokens_here = states[0]
    routes_here = routes[0]
    router_here = router[0].T
    routes_here = routes_here.T
    first_weight = w_in[0, 0]
    second_weight = w_out[0, 0]
    cotangent_here = cotangent[0]
    tokens, columns = tokens_here.shape
    experts = router_here.shape[0]
    capacity = max(2, 5 * TOP * tokens // (4 * experts))
    half = columns // 2
    width = HEADS * HEAD
    slot_count = experts * STRIDE
    block = shaped((experts, FOLD * capacity, columns // FOLD), LOW)
    packed = pltpu.VMEM((slot_count, columns), LOW)

    facts_shape, wide_rows = shaped((tokens, LANES), WIDE), shaped((tokens, columns), WIDE)
    folded, facts = local(
        dispatch_kernel,
        (block, facts_shape),
        tokens_here,
        routes_here,
        router_here,
        late=(0, 2),
        sent=(1,),
    )
    folded, w_query, w_key, w_value, w_output = lax.optimization_barrier(
        (folded, w_query, w_key, w_value, w_output)
    )
    own_a = jnp.where(encoder_side, w_key, w_query)
    output_wide = jnp.concatenate([w_output[:, :width], w_output[:, width:]], axis=0)
    own_b = jnp.where(encoder_side, w_value, output_wide)
    dense = jnp.concatenate([own_a, own_b], axis=0)
    others = shift(dense, 1), shift(dense, -1), shift(dense, 2)
    blocks, token = to_holders(folded)
    dense = local(
        planes_kernel,
        shaped((lax.axis_size("dp"),) + dense.shape, LOW),
        lax.axis_index("dp").reshape(1, 1),
        dense,
        *others,
        token,
        scalars=1,
    )
    dense = lax.all_gather(dense, "expert", axis=0, tiled=True)
    dense = dense.reshape(lax.axis_size("expert"), lax.axis_size("dp"), -1, width)

    actives = [None] * 4

    def forward_term(rows, place):
        pre = dot(rows[0], first_weight[:half]) + dot(rows[1], first_weight[half:])
        active = jnp.maximum(pre, 0.0).astype(LOW)
        actives[place] = active
        return dot(active, second_weight[:, :half]), dot(active, second_weight[:, half:])

    back = through_experts(blocks, forward_term, block)
    full_a, full_value, full_left, full_right = arrange(dense)

    hidden_state, normed_out = local(
        combine_kernel,
        (wide_rows, shaped((tokens, columns), LOW)),
        back,
        tokens_here,
        facts,
        full_a,
        scratch=(packed,),
        late=(1, 2),
        held=(3,),
        sent=(0,),
    )
    own_length = jnp.where(encoder_side, lengths[0, 0], lengths[1, 0])
    live = jnp.arange(LEN, dtype=jnp.int32)[:, None] < own_length
    out_low = jnp.where(live & ~encoder_side, cotangent_here, jnp.zeros((), LOW))
    context_grad = (
        dot_nt(out_low[:, :half], full_left) + dot_nt(out_low[:, half:], full_right)
    ).astype(LOW)

    own_rows = dot(normed_out, full_a).astype(LOW)
    own_values = dot(normed_out, full_value).astype(LOW)
    key_rows = lax.ppermute(own_rows, "section", [(0, 1)])
    value_rows = lax.ppermute(own_values, "section", [(0, 1)])
    low_rows = shaped((tokens, width), LOW)
    value_grad, attention, kept = local(
        attend_kernel,
        (low_rows, shaped((HEADS, LEN, LEN), WIDE), shaped((3, tokens, width), LOW)),
        lengths[0].reshape(1, 1),
        own_rows,
        key_rows,
        context_grad,
        scalars=1,
        sent=(1, 2),
    )
    value_back = lax.ppermute(value_grad, "section", [(1, 0)])
    query_grad, key_grad, context = local(
        attend_back_kernel,
        (low_rows,) * 3,
        value_rows,
        attention,
        kept,
        late=(1, 2),
    )
    key_back = lax.ppermute(key_grad, "section", [(1, 0)])
    attended = jnp.concatenate([dot(context, full_left), dot(context, full_right)], axis=1)
    decoder_out = (hidden_state + attended).astype(LOW)
    forward_out = jnp.where(encoder_side, normed_out, decoder_out)
    projection_back = dot_nt(jnp.where(encoder_side, key_back, query_grad), full_a) + dot_nt(
        value_back, full_value
    )
    flags = jnp.stack([own_length, encoder_side.astype(jnp.int32)])[None]
    upstream, folded = local(
        upstream_kernel,
        (wide_rows, block),
        flags,
        hidden_state,
        projection_back,
        cotangent_here,
        facts,
        scalars=1,
        sent=(0,),
    )
    sign_grad = local(
        router_kernel,
        shaped((tokens, experts), WIDE),
        back,
        upstream,
        facts,
        scratch=(packed,),
        late=(1, 2),
    )

    def backward_term(rows, place):
        slope = dot_nt(rows[0], second_weight[:, :half]) + dot_nt(rows[1], second_weight[:, half:])
        slope = jnp.where(actives[place] > 0, slope, 0.0).astype(LOW)
        return dot_nt(slope, first_weight[:half]), dot_nt(slope, first_weight[half:])

    back = through_experts(to_holders(folded)[0], backward_term, block)
    grads = local(
        finish_kernel,
        wide_rows,
        back,
        tokens_here,
        upstream,
        sign_grad,
        router_here,
        facts,
        scratch=(packed,),
        late=(1, 2, 3, 4, 5),
    )
    return (forward_out[None], grads[None])


def solution(mesh):
    in_specs = (
        P("section", ("dp", "expert"), None),
        P("section", ("dp", "expert"), None),
        P(None, ("dp", "expert")),
        P("section", None, None),
        P("section", "expert", None, "dp"),
        P("section", "expert", "dp", None),
        P(("dp", "expert"), None),
        P(("dp", "expert"), None),
        P(("dp", "expert"), None),
        P(("dp", "expert"), None),
        P("section", ("dp", "expert"), None),
    )
    out_specs = (P("section", ("dp", "expert"), None), P("section", ("dp", "expert"), None))
    return jax.shard_map(
        per_device, mesh=mesh, in_specs=in_specs, out_specs=out_specs, check_vma=False
    )
```

```python
import functools

import jax
import jax.numpy as jnp
from jax import lax
from jax.experimental import pallas as pl
from jax.experimental.pallas import tpu as pltpu
from jax.sharding import PartitionSpec as P

HEADS = 8
HEAD = 128
TOP = 2
LEN = 128
STRIDE = 32
FOLD = 4
LANES = 128


EPS = 1e-05
NEG_FILL = -1e30
LOW = jnp.bfloat16
WIDE = jnp.float32
VMEM = pl.BlockSpec(memory_space=pltpu.VMEM)
SMEM = pl.BlockSpec(memory_space=pltpu.SMEM)
PARAMS = pltpu.CompilerParams(vmem_limit_bytes=20 * 1024 * 1024)


def dot(a, b):
    return jnp.dot(a, b, preferred_element_type=WIDE)


def dot_nt(a, b):
    return lax.dot_general(a, b, (((1,), (1,)), ((), ())), preferred_element_type=WIDE)


def dot_tn(a, b):
    return lax.dot_general(a, b, (((0,), (0,)), ((), ())), preferred_element_type=WIDE)


def normalised(values):
    centred = values - jnp.mean(values, axis=-1, keepdims=True)
    variance = jnp.mean(centred * centred, axis=-1, keepdims=True)
    inverse = lax.rsqrt(variance + EPS)
    return centred * inverse, inverse


def norm_back(values, upstream):
    normed, inverse = normalised(values)
    return inverse * (
        upstream
        - jnp.mean(upstream, axis=-1, keepdims=True)
        - normed * jnp.mean(upstream * normed, axis=-1, keepdims=True)
    )


class Late:
    def __init__(self, source, held, semaphore):
        self.copy = pltpu.make_async_copy(source, held, semaphore)
        self.held, self.shape, self.dtype, self.waiting = held, held.shape, held.dtype, True
        self.copy.start()

    def __getitem__(self, index):
        if self.waiting:
            self.copy.wait()
            self.waiting = False
        return self.held[index]


class Sent:
    def __init__(self, target, held, semaphore):
        self.copy = pltpu.make_async_copy(held, target, semaphore)
        self.held, self.shape, self.dtype = held, held.shape, held.dtype

    def __setitem__(self, index, value):
        self.held[index] = value

    def send(self):
        self.copy.start()


def laned(columns):
    lane = lax.broadcasted_iota(jnp.int32, (columns[0].shape[0], LANES), 1)
    return sum(jnp.where(lane == place, column, 0.0) for place, column in enumerate(columns))


def slot_hots(facts, experts):
    place = lax.broadcasted_iota(jnp.int32, (facts.shape[0], experts * STRIDE), 1)
    return tuple(
        jnp.where(place == (facts[:, at : at + 1] * STRIDE + facts[:, at + 1 : at + 2]).astype(jnp.int32), 1.0, 0.0)
        for at in (0, 2)
    )


def route_signs(facts, experts):
    ids = lax.broadcasted_iota(jnp.int32, (facts.shape[0], experts), 1).astype(WIDE)
    return jnp.where(facts[:, 0:1] == ids, 1.0, 0.0) - jnp.where(facts[:, 2:3] == ids, 1.0, 0.0)


def spread_rows(rows, folded_ref):
    experts, stack, columns = folded_ref.shape
    capacity = stack // FOLD
    for e in range(experts):
        block = rows[e * STRIDE : e * STRIDE + capacity].astype(LOW)
        for place in range(FOLD):
            folded_ref[e, pl.ds(place * capacity, capacity), :] = block[
                :, place * columns : (place + 1) * columns
            ]


def pack_rows(folded_ref, packed):
    experts, stack, columns = folded_ref.shape
    capacity = stack // FOLD
    packed[...] = jnp.zeros_like(packed)
    for e in range(experts):
        for place in range(FOLD):
            packed[pl.ds(e * STRIDE, capacity), pl.ds(place * columns, columns)] = folded_ref[
                e, pl.ds(place * capacity, capacity), :
            ]


def unfold_kernel(folded_ref, rows_ref, token_ref, *, begin):
    token_ref[...] = jnp.zeros_like(token_ref)
    experts, stack, columns = folded_ref.shape
    capacity = stack // FOLD
    for e in range(experts):
        for place in range(FOLD // 2):
            rows_ref[pl.ds(e * capacity, capacity), pl.ds(place * columns, columns)] = folded_ref[
                e, pl.ds((begin + place) * capacity, capacity), :
            ]


def fold_kernel(*refs):
    folded_ref = refs[-1]
    experts, stack, columns = folded_ref.shape
    capacity = stack // FOLD
    for begin in range(2):
        base_ref, last_ref = refs[begin * 2 : begin * 2 + 2]
        total = (base_ref[...] + last_ref[...].astype(WIDE)).astype(LOW)
        for e in range(experts):
            for place in range(FOLD // 2):
                folded_ref[e, pl.ds((begin * FOLD // 2 + place) * capacity, capacity), :] = total[
                    e * capacity : (e + 1) * capacity, place * columns : (place + 1) * columns
                ]


def planes_kernel(place_ref, own_ref, behind_ref, ahead_ref, far_ref, token_ref, planes_ref):
    count = planes_ref.shape[0]
    for distance, ref in ((0, own_ref), (count - 1, behind_ref), (1, ahead_ref), (2, far_ref)):
        planes_ref[lax.rem(place_ref[0, 0] + distance, count)] = ref[...]


def dense_kernel(dense_ref, first_ref, second_ref, left_ref, right_ref):
    experts, _, double, width = dense_ref.shape
    rows = double // 2
    first_ref[...] = dense_ref[:, 0, :rows].reshape(experts * rows, width)
    second = dense_ref[:, 0, rows:]
    second_ref[...] = second.reshape(experts * rows, width)
    left_ref[...] = second[:, : rows // 2].reshape(experts * rows // 2, width)
    right_ref[...] = second[:, rows // 2 :].reshape(experts * rows // 2, width)


def dispatch_kernel(states_ref, routes_ref, router_ref, folded_ref, facts_ref):
    experts = folded_ref.shape[0]
    tokens = states_ref.shape[0]
    ids = lax.broadcasted_iota(jnp.int32, (experts, tokens), 0)
    row = lax.broadcasted_iota(jnp.int32, (experts, experts), 0)
    column = lax.broadcasted_iota(jnp.int32, (experts, experts), 1)
    same = jnp.where(row == column, 1.0, 0.0).astype(LOW)
    hots = [
        dot_tn(jnp.where(routes_ref[k : k + 1, :] == ids, 1.0, 0.0).astype(LOW), same)
        for k in range(TOP)
    ]
    row = lax.broadcasted_iota(jnp.int32, (tokens, tokens), 0)
    column = lax.broadcasted_iota(jnp.int32, (tokens, tokens), 1)
    earlier = jnp.where(column < row, 1.0, 0.0).astype(LOW)
    rank = dot(earlier, (hots[0] + hots[1]).astype(LOW))
    number = lax.broadcasted_iota(jnp.int32, (tokens, experts), 1).astype(WIDE)
    facts = []
    for hot in hots:
        facts.append(jnp.sum(hot * number, axis=1, keepdims=True))
        facts.append(jnp.sum(hot * rank, axis=1, keepdims=True))
    normed = normalised(states_ref[...].astype(WIDE))[0].astype(LOW)
    logits = dot_nt(normed, router_ref[...])
    spread = jnp.sum(hots[0] * logits - hots[1] * logits, axis=1, keepdims=True)
    facts = laned(facts + [jax.nn.sigmoid(spread)])
    facts_ref[...] = facts
    facts_ref.send()
    one, two = slot_hots(facts, experts)
    spread_rows(dot_tn((one + two).astype(LOW), normed), folded_ref)


def combine_kernel(folded_ref, states_ref, facts_ref, ready_ref, hidden_ref, normed_ref, packed):
    pack_rows(folded_ref, packed)
    rows = packed[...]
    facts = facts_ref[...]
    gate = facts[:, 4:5]
    one, two = slot_hots(facts, folded_ref.shape[0])
    hidden = states_ref[...].astype(WIDE) + (
        gate * dot(one.astype(LOW), rows) + (1.0 - gate) * dot(two.astype(LOW), rows)
    )
    hidden_ref[...] = hidden
    hidden_ref.send()
    normed_ref[...] = normalised(hidden)[0].astype(LOW)


def attend_kernel(length_ref, q_ref, k_ref, grad_ref, v_grad_ref, attention_ref, kept_ref):
    kept_ref[0], kept_ref[1], kept_ref[2] = q_ref[...], k_ref[...], grad_ref[...]
    kept_ref.send()
    scale = HEAD ** (-0.5)
    live = lax.broadcasted_iota(jnp.int32, (LEN, LEN), 1) < length_ref[0, 0]
    for head in range(HEADS):
        at = slice(head * HEAD, (head + 1) * HEAD)
        scores = jnp.where(live, dot_nt(q_ref[:, at], k_ref[:, at]) * scale, NEG_FILL)
        exponent = jnp.exp(scores - jnp.max(scores, axis=-1, keepdims=True))
        attention = exponent / jnp.sum(exponent, axis=-1, keepdims=True)
        attention_ref[head] = attention
        v_grad_ref[:, at] = dot_tn(attention.astype(LOW), grad_ref[:, at]).astype(LOW)
    attention_ref.send()


def attend_back_kernel(v_ref, attention_ref, kept_ref, q_grad_ref, k_grad_ref, context_ref):
    scale = HEAD ** (-0.5)
    for head in range(HEADS):
        at = slice(head * HEAD, (head + 1) * HEAD)
        attention, v = attention_ref[head], v_ref[:, at]
        q, k, grad = kept_ref[0, :, at], kept_ref[1, :, at], kept_ref[2, :, at]
        weight_grad = dot_nt(grad, v)
        score_grad = (
            attention
            * (weight_grad - jnp.sum(attention * weight_grad, axis=-1, keepdims=True))
            * scale
        ).astype(LOW)
        k_grad_ref[:, at] = dot_tn(score_grad, q).astype(LOW)
        q_grad_ref[:, at] = dot(score_grad, k).astype(LOW)
        context_ref[:, at] = dot(attention.astype(LOW), v).astype(LOW)


def upstream_kernel(flags_ref, hidden_ref, back_ref, cotangent_ref, facts_ref, upstream_ref, folded_ref):
    live = lax.broadcasted_iota(jnp.int32, (LEN, 1), 0) < flags_ref[0, 0]
    encoder = flags_ref[0, 1] == 1
    masked = jnp.where(live, cotangent_ref[...].astype(WIDE), 0.0)
    out_grad = jnp.where(encoder, 0.0, masked)
    normed_grad = back_ref[...] + jnp.where(encoder, masked, 0.0)
    upstream = out_grad + norm_back(hidden_ref[...], normed_grad)
    upstream_ref[...] = upstream
    upstream_ref.send()
    facts = facts_ref[...]
    gate = facts[:, 4:5]
    one, two = slot_hots(facts, folded_ref.shape[0])
    rows = dot_tn(one.astype(LOW), (gate * upstream).astype(LOW)) + dot_tn(
        two.astype(LOW), ((1.0 - gate) * upstream).astype(LOW)
    )
    spread_rows(rows, folded_ref)


def router_kernel(folded_ref, upstream_ref, facts_ref, sign_ref, packed):
    pack_rows(folded_ref, packed)
    rows = packed[...]
    facts = facts_ref[...]
    gate = facts[:, 4:5]
    one, two = slot_hots(facts, folded_ref.shape[0])
    apart = dot(one.astype(LOW), rows) - dot(two.astype(LOW), rows)
    gate_grad = jnp.sum(upstream_ref[...] * apart, axis=1, keepdims=True)
    logit_grad = gate_grad * gate * (1.0 - gate)
    sign_ref[...] = logit_grad * route_signs(facts, folded_ref.shape[0])


def finish_kernel(folded_ref, states_ref, upstream_ref, sign_ref, router_ref, facts_ref, grads_ref, packed):
    pack_rows(folded_ref, packed)
    one, two = slot_hots(facts_ref[...], folded_ref.shape[0])
    back = dot((one + two).astype(LOW), packed[...])
    router_term = jnp.dot(
        sign_ref[...],
        router_ref[...].astype(WIDE),
        precision=lax.Precision.HIGHEST,
        preferred_element_type=WIDE,
    )
    input_total = back + router_term
    grads_ref[...] = upstream_ref[...] + norm_back(states_ref[...].astype(WIDE), input_total)


def local(kernel, out_shape, *operands, scalars=0, scratch=(), late=(), sent=(), held=()):
    single = not isinstance(out_shape, tuple)
    shapes = (out_shape,) if single else out_shape
    count = len(operands)
    total = count + len(shapes)
    moved = [place for place in range(count) if place in late]
    moved += [count + place for place in range(len(shapes)) if place in sent]
    both = list(operands) + list(shapes)

    def body(*refs):
        refs, extra = list(refs[:total]), refs[total:]
        holds, semaphores = extra[: len(moved)], extra[len(moved)] if moved else None
        for number, place in enumerate(moved):
            made = Late if place < count else Sent
            refs[place] = made(refs[place], holds[number], semaphores.at[number])
        kernel(*refs, *extra[len(moved) + (1 if moved else 0) :])
        for place in moved:
            if place >= count:
                refs[place].copy.wait()

    scratches = [pltpu.VMEM(both[place].shape, both[place].dtype) for place in moved]
    if moved:
        scratches.append(pltpu.SemaphoreType.DMA((len(moved),)))
    specs = [SMEM] * scalars + [VMEM] * (total - scalars)
    for place in [*moved, *held]:
        specs[place] = pl.BlockSpec(memory_space=pltpu.HBM)
    cost = sum(x.size * x.dtype.itemsize for x in both)
    operands = [
        pltpu.with_memory_space_constraint(operand, pltpu.HBM) if place in [*late, *held] else operand
        for place, operand in enumerate(operands)
    ]
    shapes = tuple(
        pltpu.HBM(shape.shape, shape.dtype) if place in sent else shape
        for place, shape in enumerate(shapes)
    )
    result = pl.pallas_call(
        body,
        out_shape=shapes,
        in_specs=specs[:count],
        out_specs=tuple(specs[count:]),
        scratch_shapes=scratches + list(scratch),
        compiler_params=PARAMS,
        cost_estimate=pl.CostEstimate(flops=10**9, bytes_accessed=4 * cost, transcendentals=0),
    )(*operands)
    return result[0] if single else result


def shaped(shape, dtype):
    return jax.ShapeDtypeStruct(shape, dtype)


def shift(block, distance):
    count = lax.axis_size("dp")
    return lax.ppermute(block, "dp", [(i, (i + distance) % count) for i in range(count)])


def to_experts(block):
    return lax.all_to_all(block, "expert", split_axis=0, concat_axis=0, tiled=True)


def arrange(dense):
    experts, planes, double, width = dense.shape
    rows = experts * double // 2

    def blocks(count):
        return pl.BlockSpec((count, width), lambda plane: (plane, 0))

    whole, part = shaped((planes * rows, width), LOW), shaped((planes * rows // 2, width), LOW)
    return pl.pallas_call(
        dense_kernel,
        grid=(planes,),
        out_shape=(whole, whole, part, part),
        in_specs=[pl.BlockSpec((experts, 1, double, width), lambda plane: (0, plane, 0, 0))],
        out_specs=(blocks(rows), blocks(rows), blocks(rows // 2), blocks(rows // 2)),
        compiler_params=PARAMS,
        cost_estimate=pl.CostEstimate(flops=10**6, bytes_accessed=20 * 2**20, transcendentals=0),
    )(dense)


def to_holders(folded):
    experts, stack, columns = folded.shape
    rows = shaped((experts * stack // FOLD, columns * FOLD // 2), LOW)
    folded = to_experts(folded)
    token = shaped((8, LANES), WIDE)
    one, token = local(functools.partial(unfold_kernel, begin=0), (rows, token), folded)
    two, _ = local(functools.partial(unfold_kernel, begin=FOLD // 2), (rows, token), folded)
    behind_one, ahead_one = shift(one, 1), shift(one, -1)
    behind_two, ahead_two = shift(two, 1), shift(two, -1)
    far_one, far_two = shift(behind_one, 1), shift(ahead_two, -1)
    return ((one, two), (behind_one, behind_two), (ahead_one, ahead_two), (far_one, far_two)), token


def through_experts(rows, term, block):
    behind, ahead = term(rows[1], 1), term(rows[2], 2)
    far_one, side_two = lax.optimization_barrier((rows[3][0], ahead[1].astype(LOW)))
    far_two, side_one = lax.optimization_barrier((rows[3][1], behind[0].astype(LOW)))
    side_one, side_two = shift(side_one, -1), shift(side_two, 1)
    far = term((far_one, far_two), 3)
    step_one, step_two = shift(far[0].astype(LOW), 1), shift(far[1].astype(LOW), -1)
    step_one, own = lax.optimization_barrier((step_one, rows[0]))
    own = term(own, 0)
    last_one = (ahead[0] + step_one.astype(WIDE)).astype(LOW)
    last_two = (behind[1] + step_two.astype(WIDE)).astype(LOW)
    base_one, base_two = own[0] + side_one.astype(WIDE), own[1] + side_two.astype(WIDE)
    last_one, last_two, base_one, base_two = lax.optimization_barrier(
        (last_one, last_two, base_one, base_two)
    )
    last_one, last_two = shift(last_one, 1), shift(last_two, -1)
    return to_experts(local(fold_kernel, block, base_one, last_one, base_two, last_two))


def per_device(
    states, routes, lengths, router, w_in, w_out, w_query, w_key, w_value, w_output, cotangent
):
    section = lax.axis_index("section")
    encoder_side = section == 0
    tokens_here = states[0]
    routes_here = routes[0]
    router_here = router[0].T
    routes_here = routes_here.T
    first_weight = w_in[0, 0]
    second_weight = w_out[0, 0]
    cotangent_here = cotangent[0]
    tokens, columns = tokens_here.shape
    experts = router_here.shape[0]
    capacity = max(2, 5 * TOP * tokens // (4 * experts))
    half = columns // 2
    width = HEADS * HEAD
    slot_count = experts * STRIDE
    block = shaped((experts, FOLD * capacity, columns // FOLD), LOW)
    packed = pltpu.VMEM((slot_count, columns), LOW)

    facts_shape, wide_rows = shaped((tokens, LANES), WIDE), shaped((tokens, columns), WIDE)
    folded, facts = local(
        dispatch_kernel,
        (block, facts_shape),
        tokens_here,
        routes_here,
        router_here,
        late=(0, 2),
        sent=(1,),
    )
    folded, w_query, w_key, w_value, w_output = lax.optimization_barrier(
        (folded, w_query, w_key, w_value, w_output)
    )
    own_a = jnp.where(encoder_side, w_key, w_query)
    output_wide = jnp.concatenate([w_output[:, :width], w_output[:, width:]], axis=0)
    own_b = jnp.where(encoder_side, w_value, output_wide)
    dense = jnp.concatenate([own_a, own_b], axis=0)
    others = shift(dense, 1), shift(dense, -1), shift(dense, 2)
    blocks, token = to_holders(folded)
    dense = local(
        planes_kernel,
        shaped((lax.axis_size("dp"),) + dense.shape, LOW),
        lax.axis_index("dp").reshape(1, 1),
        dense,
        *others,
        token,
        scalars=1,
    )
    dense = lax.all_gather(dense, "expert", axis=0, tiled=True)
    dense = dense.reshape(lax.axis_size("expert"), lax.axis_size("dp"), -1, width)

    actives = [None] * 4

    def forward_term(rows, place):
        pre = dot(rows[0], first_weight[:half]) + dot(rows[1], first_weight[half:])
        active = jnp.maximum(pre, 0.0).astype(LOW)
        actives[place] = active
        return dot(active, second_weight[:, :half]), dot(active, second_weight[:, half:])

    back = through_experts(blocks, forward_term, block)
    full_a, full_value, full_left, full_right = arrange(dense)

    hidden_state, normed_out = local(
        combine_kernel,
        (wide_rows, shaped((tokens, columns), LOW)),
        back,
        tokens_here,
        facts,
        full_a,
        scratch=(packed,),
        late=(1, 2),
        held=(3,),
        sent=(0,),
    )
    own_length = jnp.where(encoder_side, lengths[0, 0], lengths[1, 0])
    live = jnp.arange(LEN, dtype=jnp.int32)[:, None] < own_length
    out_low = jnp.where(live & ~encoder_side, cotangent_here, jnp.zeros((), LOW))
    context_grad = (
        dot_nt(out_low[:, :half], full_left) + dot_nt(out_low[:, half:], full_right)
    ).astype(LOW)

    own_rows = dot(normed_out, full_a).astype(LOW)
    own_values = dot(normed_out, full_value).astype(LOW)
    key_rows = lax.ppermute(own_rows, "section", [(0, 1)])
    value_rows = lax.ppermute(own_values, "section", [(0, 1)])
    low_rows = shaped((tokens, width), LOW)
    value_grad, attention, kept = local(
        attend_kernel,
        (low_rows, shaped((HEADS, LEN, LEN), WIDE), shaped((3, tokens, width), LOW)),
        lengths[0].reshape(1, 1),
        own_rows,
        key_rows,
        context_grad,
        scalars=1,
        sent=(1, 2),
    )
    value_back = lax.ppermute(value_grad, "section", [(1, 0)])
    query_grad, key_grad, context = local(
        attend_back_kernel,
        (low_rows,) * 3,
        value_rows,
        attention,
        kept,
        late=(1, 2),
    )
    key_back = lax.ppermute(key_grad, "section", [(1, 0)])
    attended = jnp.concatenate([dot(context, full_left), dot(context, full_right)], axis=1)
    decoder_out = (hidden_state + attended).astype(LOW)
    forward_out = jnp.where(encoder_side, normed_out, decoder_out)
    projection_back = dot_nt(jnp.where(encoder_side, key_back, query_grad), full_a) + dot_nt(
        value_back, full_value
    )
    flags = jnp.stack([own_length, encoder_side.astype(jnp.int32)])[None]
    upstream, folded = local(
        upstream_kernel,
        (wide_rows, block),
        flags,
        hidden_state,
        projection_back,
        cotangent_here,
        facts,
        scalars=1,
        sent=(0,),
    )
    sign_grad = local(
        router_kernel,
        shaped((tokens, experts), WIDE),
        back,
        upstream,
        facts,
        scratch=(packed,),
        late=(1, 2),
    )

    def backward_term(rows, place):
        slope = dot_nt(rows[0], second_weight[:, :half]) + dot_nt(rows[1], second_weight[:, half:])
        slope = jnp.where(actives[place] > 0, slope, 0.0).astype(LOW)
        return dot_nt(slope, first_weight[:half]), dot_nt(slope, first_weight[half:])

    back = through_experts(to_holders(folded)[0], backward_term, block)
    grads = local(
        finish_kernel,
        wide_rows,
        back,
        tokens_here,
        upstream,
        sign_grad,
        router_here,
        facts,
        scratch=(packed,),
        late=(1, 2, 3, 4, 5),
    )
    return (forward_out[None], grads[None])


def solution(mesh):
    in_specs = (
        P("section", ("dp", "expert"), None),
        P("section", ("dp", "expert"), None),
        P(None, ("dp", "expert")),
        P("section", None, None),
        P("section", "expert", None, "dp"),
        P("section", "expert", "dp", None),
        P(("dp", "expert"), None),
        P(("dp", "expert"), None),
        P(("dp", "expert"), None),
        P(("dp", "expert"), None),
        P("section", ("dp", "expert"), None),
    )
    out_specs = (P("section", ("dp", "expert"), None), P("section", ("dp", "expert"), None))
    return jax.shard_map(
        per_device, mesh=mesh, in_specs=in_specs, out_specs=out_specs, check_vma=False
    )
```

```python
import functools

import jax
import jax.numpy as jnp
from jax import lax
from jax.experimental import pallas as pl
from jax.experimental.pallas import tpu as pltpu
from jax.sharding import PartitionSpec as P

HEADS = 8
HEAD = 128
TOP = 2
LEN = 128
STRIDE = 32
FOLD = 4
LANES = 128


EPS = 1e-05
NEG_FILL = -1e30
LOW = jnp.bfloat16
WIDE = jnp.float32
VMEM = pl.BlockSpec(memory_space=pltpu.VMEM)
SMEM = pl.BlockSpec(memory_space=pltpu.SMEM)
PARAMS = pltpu.CompilerParams(vmem_limit_bytes=20 * 1024 * 1024)


def dot(a, b):
    return jnp.dot(a, b, preferred_element_type=WIDE)


def dot_nt(a, b):
    return lax.dot_general(a, b, (((1,), (1,)), ((), ())), preferred_element_type=WIDE)


def dot_tn(a, b):
    return lax.dot_general(a, b, (((0,), (0,)), ((), ())), preferred_element_type=WIDE)


def normalised(values):
    centred = values - jnp.mean(values, axis=-1, keepdims=True)
    variance = jnp.mean(centred * centred, axis=-1, keepdims=True)
    inverse = lax.rsqrt(variance + EPS)
    return centred * inverse, inverse


def norm_back(values, upstream):
    normed, inverse = normalised(values)
    return inverse * (
        upstream
        - jnp.mean(upstream, axis=-1, keepdims=True)
        - normed * jnp.mean(upstream * normed, axis=-1, keepdims=True)
    )


class Late:
    def __init__(self, source, held, semaphore):
        self.copy = pltpu.make_async_copy(source, held, semaphore)
        self.held, self.shape, self.dtype, self.waiting = held, held.shape, held.dtype, True
        self.copy.start()

    def __getitem__(self, index):
        if self.waiting:
            self.copy.wait()
            self.waiting = False
        return self.held[index]


class Sent:
    def __init__(self, target, held, semaphore):
        self.copy = pltpu.make_async_copy(held, target, semaphore)
        self.held, self.shape, self.dtype = held, held.shape, held.dtype

    def __setitem__(self, index, value):
        self.held[index] = value

    def send(self):
        self.copy.start()


def laned(columns):
    lane = lax.broadcasted_iota(jnp.int32, (columns[0].shape[0], LANES), 1)
    return sum(jnp.where(lane == place, column, 0.0) for place, column in enumerate(columns))


def slot_hots(facts, experts):
    place = lax.broadcasted_iota(jnp.int32, (facts.shape[0], experts * STRIDE), 1)
    return tuple(
        jnp.where(place == (facts[:, at : at + 1] * STRIDE + facts[:, at + 1 : at + 2]).astype(jnp.int32), 1.0, 0.0)
        for at in (0, 2)
    )


def route_signs(facts, experts):
    ids = lax.broadcasted_iota(jnp.int32, (facts.shape[0], experts), 1).astype(WIDE)
    return jnp.where(facts[:, 0:1] == ids, 1.0, 0.0) - jnp.where(facts[:, 2:3] == ids, 1.0, 0.0)


def spread_rows(rows, folded_ref):
    experts, stack, columns = folded_ref.shape
    capacity = stack // FOLD
    for e in range(experts):
        block = rows[e * STRIDE : e * STRIDE + capacity].astype(LOW)
        for place in range(FOLD):
            folded_ref[e, pl.ds(place * capacity, capacity), :] = block[
                :, place * columns : (place + 1) * columns
            ]


def pack_rows(folded_ref, packed):
    experts, stack, columns = folded_ref.shape
    capacity = stack // FOLD
    packed[...] = jnp.zeros_like(packed)
    for e in range(experts):
        for place in range(FOLD):
            packed[pl.ds(e * STRIDE, capacity), pl.ds(place * columns, columns)] = folded_ref[
                e, pl.ds(place * capacity, capacity), :
            ]


def unfold_kernel(folded_ref, rows_ref, token_ref, *, begin):
    token_ref[...] = jnp.zeros_like(token_ref)
    experts, stack, columns = folded_ref.shape
    capacity = stack // FOLD
    for e in range(experts):
        for place in range(FOLD // 2):
            rows_ref[pl.ds(e * capacity, capacity), pl.ds(place * columns, columns)] = folded_ref[
                e, pl.ds((begin + place) * capacity, capacity), :
            ]


def fold_kernel(*refs):
    folded_ref = refs[-1]
    experts, stack, columns = folded_ref.shape
    capacity = stack // FOLD
    for begin in range(2):
        base_ref, last_ref = refs[begin * 2 : begin * 2 + 2]
        total = (base_ref[...] + last_ref[...].astype(WIDE)).astype(LOW)
        for e in range(experts):
            for place in range(FOLD // 2):
                folded_ref[e, pl.ds((begin * FOLD // 2 + place) * capacity, capacity), :] = total[
                    e * capacity : (e + 1) * capacity, place * columns : (place + 1) * columns
                ]


def planes_kernel(place_ref, own_ref, behind_ref, ahead_ref, far_ref, token_ref, planes_ref):
    count = planes_ref.shape[0]
    for distance, ref in ((0, own_ref), (count - 1, behind_ref), (1, ahead_ref), (2, far_ref)):
        planes_ref[lax.rem(place_ref[0, 0] + distance, count)] = ref[...]


def dense_kernel(dense_ref, first_ref, second_ref, left_ref, right_ref):
    experts, _, double, width = dense_ref.shape
    rows = double // 2
    first_ref[...] = dense_ref[:, 0, :rows].reshape(experts * rows, width)
    second = dense_ref[:, 0, rows:]
    second_ref[...] = second.reshape(experts * rows, width)
    left_ref[...] = second[:, : rows // 2].reshape(experts * rows // 2, width)
    right_ref[...] = second[:, rows // 2 :].reshape(experts * rows // 2, width)


def dispatch_kernel(states_ref, routes_ref, router_ref, folded_ref, facts_ref):
    experts = folded_ref.shape[0]
    tokens = states_ref.shape[0]
    ids = lax.broadcasted_iota(jnp.int32, (experts, tokens), 0)
    row = lax.broadcasted_iota(jnp.int32, (experts, experts), 0)
    column = lax.broadcasted_iota(jnp.int32, (experts, experts), 1)
    same = jnp.where(row == column, 1.0, 0.0).astype(LOW)
    hots = [
        dot_tn(jnp.where(routes_ref[k : k + 1, :] == ids, 1.0, 0.0).astype(LOW), same)
        for k in range(TOP)
    ]
    row = lax.broadcasted_iota(jnp.int32, (tokens, tokens), 0)
    column = lax.broadcasted_iota(jnp.int32, (tokens, tokens), 1)
    earlier = jnp.where(column < row, 1.0, 0.0).astype(LOW)
    rank = dot(earlier, (hots[0] + hots[1]).astype(LOW))
    number = lax.broadcasted_iota(jnp.int32, (tokens, experts), 1).astype(WIDE)
    facts = []
    for hot in hots:
        facts.append(jnp.sum(hot * number, axis=1, keepdims=True))
        facts.append(jnp.sum(hot * rank, axis=1, keepdims=True))
    normed = normalised(states_ref[...].astype(WIDE))[0].astype(LOW)
    logits = dot_nt(normed, router_ref[...])
    spread = jnp.sum(hots[0] * logits - hots[1] * logits, axis=1, keepdims=True)
    facts = laned(facts + [jax.nn.sigmoid(spread)])
    facts_ref[...] = facts
    facts_ref.send()
    one, two = slot_hots(facts, experts)
    spread_rows(dot_tn((one + two).astype(LOW), normed), folded_ref)


def combine_kernel(folded_ref, states_ref, facts_ref, ready_ref, hidden_ref, normed_ref, packed):
    pack_rows(folded_ref, packed)
    rows = packed[...]
    facts = facts_ref[...]
    gate = facts[:, 4:5]
    one, two = slot_hots(facts, folded_ref.shape[0])
    hidden = states_ref[...].astype(WIDE) + (
        gate * dot(one.astype(LOW), rows) + (1.0 - gate) * dot(two.astype(LOW), rows)
    )
    hidden_ref[...] = hidden
    hidden_ref.send()
    normed_ref[...] = normalised(hidden)[0].astype(LOW)


def heads_of(ref, *lead):
    return [ref[(*lead, slice(None), slice(h * HEAD, (h + 1) * HEAD))] for h in range(HEADS)]


def attend_kernel(length_ref, q_ref, k_ref, grad_ref, v_grad_ref, attention_ref, kept_ref):
    kept_ref[0], kept_ref[1], kept_ref[2] = q_ref[...], k_ref[...], grad_ref[...]
    kept_ref.send()
    scale = HEAD ** (-0.5)
    live = lax.broadcasted_iota(jnp.int32, (HEADS * LEN, LEN), 1) < length_ref[0, 0]
    scores = [dot_nt(q, k) for q, k in zip(heads_of(q_ref), heads_of(k_ref))]
    scores = jnp.where(live, jnp.concatenate(scores, axis=0) * scale, NEG_FILL)
    exponent = jnp.exp(scores - jnp.max(scores, axis=-1, keepdims=True))
    attention = exponent / jnp.sum(exponent, axis=-1, keepdims=True)
    attention_ref[...] = attention.reshape(HEADS, LEN, LEN)
    attention_ref.send()
    attention = attention.astype(LOW)
    for head, grad in enumerate(heads_of(grad_ref)):
        at = slice(head * HEAD, (head + 1) * HEAD)
        v_grad_ref[:, at] = dot_tn(attention[head * LEN : (head + 1) * LEN], grad).astype(LOW)


def attend_back_kernel(v_ref, attention_ref, kept_ref, q_grad_ref, k_grad_ref, context_ref):
    scale = HEAD ** (-0.5)
    weight_grad = [dot_nt(grad, v) for grad, v in zip(heads_of(kept_ref, 2), heads_of(v_ref))]
    weight_grad = jnp.concatenate(weight_grad, axis=0)
    attention = attention_ref[...].reshape(HEADS * LEN, LEN)
    score_grad = (
        attention
        * (weight_grad - jnp.sum(attention * weight_grad, axis=-1, keepdims=True))
        * scale
    ).astype(LOW)
    attention = attention.astype(LOW)
    parts = zip(heads_of(kept_ref, 0), heads_of(kept_ref, 1), heads_of(v_ref))
    for head, (q, k, v) in enumerate(parts):
        at = slice(head * HEAD, (head + 1) * HEAD)
        rows = slice(head * LEN, (head + 1) * LEN)
        k_grad_ref[:, at] = dot_tn(score_grad[rows], q).astype(LOW)
        q_grad_ref[:, at] = dot(score_grad[rows], k).astype(LOW)
        context_ref[:, at] = dot(attention[rows], v).astype(LOW)


def upstream_kernel(flags_ref, hidden_ref, back_ref, cotangent_ref, facts_ref, upstream_ref, folded_ref):
    live = lax.broadcasted_iota(jnp.int32, (LEN, 1), 0) < flags_ref[0, 0]
    encoder = flags_ref[0, 1] == 1
    masked = jnp.where(live, cotangent_ref[...].astype(WIDE), 0.0)
    out_grad = jnp.where(encoder, 0.0, masked)
    normed_grad = back_ref[...] + jnp.where(encoder, masked, 0.0)
    upstream = out_grad + norm_back(hidden_ref[...], normed_grad)
    upstream_ref[...] = upstream
    upstream_ref.send()
    facts = facts_ref[...]
    gate = facts[:, 4:5]
    one, two = slot_hots(facts, folded_ref.shape[0])
    rows = dot_tn(one.astype(LOW), (gate * upstream).astype(LOW)) + dot_tn(
        two.astype(LOW), ((1.0 - gate) * upstream).astype(LOW)
    )
    spread_rows(rows, folded_ref)


def router_kernel(folded_ref, upstream_ref, facts_ref, sign_ref, packed):
    pack_rows(folded_ref, packed)
    rows = packed[...]
    facts = facts_ref[...]
    gate = facts[:, 4:5]
    one, two = slot_hots(facts, folded_ref.shape[0])
    apart = dot(one.astype(LOW), rows) - dot(two.astype(LOW), rows)
    gate_grad = jnp.sum(upstream_ref[...] * apart, axis=1, keepdims=True)
    logit_grad = gate_grad * gate * (1.0 - gate)
    sign_ref[...] = logit_grad * route_signs(facts, folded_ref.shape[0])


def finish_kernel(folded_ref, states_ref, upstream_ref, sign_ref, router_ref, facts_ref, grads_ref, packed):
    pack_rows(folded_ref, packed)
    one, two = slot_hots(facts_ref[...], folded_ref.shape[0])
    back = dot((one + two).astype(LOW), packed[...])
    router_term = jnp.dot(
        sign_ref[...],
        router_ref[...].astype(WIDE),
        precision=lax.Precision.HIGHEST,
        preferred_element_type=WIDE,
    )
    input_total = back + router_term
    grads_ref[...] = upstream_ref[...] + norm_back(states_ref[...].astype(WIDE), input_total)


def local(kernel, out_shape, *operands, scalars=0, scratch=(), late=(), sent=(), held=()):
    single = not isinstance(out_shape, tuple)
    shapes = (out_shape,) if single else out_shape
    count = len(operands)
    total = count + len(shapes)
    moved = [place for place in range(count) if place in late]
    moved += [count + place for place in range(len(shapes)) if place in sent]
    both = list(operands) + list(shapes)

    def body(*refs):
        refs, extra = list(refs[:total]), refs[total:]
        holds, semaphores = extra[: len(moved)], extra[len(moved)] if moved else None
        for number, place in enumerate(moved):
            made = Late if place < count else Sent
            refs[place] = made(refs[place], holds[number], semaphores.at[number])
        kernel(*refs, *extra[len(moved) + (1 if moved else 0) :])
        for place in moved:
            if place >= count:
                refs[place].copy.wait()

    scratches = [pltpu.VMEM(both[place].shape, both[place].dtype) for place in moved]
    if moved:
        scratches.append(pltpu.SemaphoreType.DMA((len(moved),)))
    specs = [SMEM] * scalars + [VMEM] * (total - scalars)
    for place in [*moved, *held]:
        specs[place] = pl.BlockSpec(memory_space=pltpu.HBM)
    cost = sum(x.size * x.dtype.itemsize for x in both)
    operands = [
        pltpu.with_memory_space_constraint(operand, pltpu.HBM) if place in [*late, *held] else operand
        for place, operand in enumerate(operands)
    ]
    shapes = tuple(
        pltpu.HBM(shape.shape, shape.dtype) if place in sent else shape
        for place, shape in enumerate(shapes)
    )
    result = pl.pallas_call(
        body,
        out_shape=shapes,
        in_specs=specs[:count],
        out_specs=tuple(specs[count:]),
        scratch_shapes=scratches + list(scratch),
        compiler_params=PARAMS,
        cost_estimate=pl.CostEstimate(flops=10**9, bytes_accessed=4 * cost, transcendentals=0),
    )(*operands)
    return result[0] if single else result


def shaped(shape, dtype):
    return jax.ShapeDtypeStruct(shape, dtype)


def shift(block, distance):
    count = lax.axis_size("dp")
    return lax.ppermute(block, "dp", [(i, (i + distance) % count) for i in range(count)])


def to_experts(block):
    return lax.all_to_all(block, "expert", split_axis=0, concat_axis=0, tiled=True)


def arrange(dense):
    experts, planes, double, width = dense.shape
    rows = experts * double // 2

    def blocks(count):
        return pl.BlockSpec((count, width), lambda plane: (plane, 0))

    whole, part = shaped((planes * rows, width), LOW), shaped((planes * rows // 2, width), LOW)
    return pl.pallas_call(
        dense_kernel,
        grid=(planes,),
        out_shape=(whole, whole, part, part),
        in_specs=[pl.BlockSpec((experts, 1, double, width), lambda plane: (0, plane, 0, 0))],
        out_specs=(blocks(rows), blocks(rows), blocks(rows // 2), blocks(rows // 2)),
        compiler_params=PARAMS,
        cost_estimate=pl.CostEstimate(flops=10**6, bytes_accessed=20 * 2**20, transcendentals=0),
    )(dense)


def to_holders(folded):
    experts, stack, columns = folded.shape
    rows = shaped((experts * stack // FOLD, columns * FOLD // 2), LOW)
    folded = to_experts(folded)
    token = shaped((8, LANES), WIDE)
    one, token = local(functools.partial(unfold_kernel, begin=0), (rows, token), folded)
    two, _ = local(functools.partial(unfold_kernel, begin=FOLD // 2), (rows, token), folded)
    behind_one, ahead_one = shift(one, 1), shift(one, -1)
    behind_two, ahead_two = shift(two, 1), shift(two, -1)
    far_one, far_two = shift(behind_one, 1), shift(ahead_two, -1)
    return ((one, two), (behind_one, behind_two), (ahead_one, ahead_two), (far_one, far_two)), token


def through_experts(rows, term, block):
    behind, ahead = term(rows[1], 1), term(rows[2], 2)
    far_one, side_two = lax.optimization_barrier((rows[3][0], ahead[1].astype(LOW)))
    far_two, side_one = lax.optimization_barrier((rows[3][1], behind[0].astype(LOW)))
    side_one, side_two = shift(side_one, -1), shift(side_two, 1)
    far = term((far_one, far_two), 3)
    step_one, step_two = shift(far[0].astype(LOW), 1), shift(far[1].astype(LOW), -1)
    step_one, own = lax.optimization_barrier((step_one, rows[0]))
    own = term(own, 0)
    last_one = (ahead[0] + step_one.astype(WIDE)).astype(LOW)
    last_two = (behind[1] + step_two.astype(WIDE)).astype(LOW)
    base_one, base_two = own[0] + side_one.astype(WIDE), own[1] + side_two.astype(WIDE)
    last_one, last_two, base_one, base_two = lax.optimization_barrier(
        (last_one, last_two, base_one, base_two)
    )
    last_one, last_two = shift(last_one, 1), shift(last_two, -1)
    return to_experts(local(fold_kernel, block, base_one, last_one, base_two, last_two))


def per_device(
    states, routes, lengths, router, w_in, w_out, w_query, w_key, w_value, w_output, cotangent
):
    section = lax.axis_index("section")
    encoder_side = section == 0
    tokens_here = states[0]
    routes_here = routes[0]
    router_here = router[0].T
    routes_here = routes_here.T
    first_weight = w_in[0, 0]
    second_weight = w_out[0, 0]
    cotangent_here = cotangent[0]
    tokens, columns = tokens_here.shape
    experts = router_here.shape[0]
    capacity = max(2, 5 * TOP * tokens // (4 * experts))
    half = columns // 2
    width = HEADS * HEAD
    slot_count = experts * STRIDE
    block = shaped((experts, FOLD * capacity, columns // FOLD), LOW)
    packed = pltpu.VMEM((slot_count, columns), LOW)

    facts_shape, wide_rows = shaped((tokens, LANES), WIDE), shaped((tokens, columns), WIDE)
    folded, facts = local(
        dispatch_kernel,
        (block, facts_shape),
        tokens_here,
        routes_here,
        router_here,
        late=(0, 2),
        sent=(1,),
    )
    folded, w_query, w_key, w_value, w_output = lax.optimization_barrier(
        (folded, w_query, w_key, w_value, w_output)
    )
    own_a = jnp.where(encoder_side, w_key, w_query)
    output_wide = jnp.concatenate([w_output[:, :width], w_output[:, width:]], axis=0)
    own_b = jnp.where(encoder_side, w_value, output_wide)
    dense = jnp.concatenate([own_a, own_b], axis=0)
    others = shift(dense, 1), shift(dense, -1), shift(dense, 2)
    blocks, token = to_holders(folded)
    dense = local(
        planes_kernel,
        shaped((lax.axis_size("dp"),) + dense.shape, LOW),
        lax.axis_index("dp").reshape(1, 1),
        dense,
        *others,
        token,
        scalars=1,
    )
    dense = lax.all_gather(dense, "expert", axis=0, tiled=True)
    dense = dense.reshape(lax.axis_size("expert"), lax.axis_size("dp"), -1, width)

    actives = [None] * 4

    def forward_term(rows, place):
        pre = dot(rows[0], first_weight[:half]) + dot(rows[1], first_weight[half:])
        active = jnp.maximum(pre, 0.0).astype(LOW)
        actives[place] = active
        return dot(active, second_weight[:, :half]), dot(active, second_weight[:, half:])

    back = through_experts(blocks, forward_term, block)
    full_a, full_value, full_left, full_right = arrange(dense)

    hidden_state, normed_out = local(
        combine_kernel,
        (wide_rows, shaped((tokens, columns), LOW)),
        back,
        tokens_here,
        facts,
        full_a,
        scratch=(packed,),
        late=(1, 2),
        held=(3,),
        sent=(0,),
    )
    own_length = jnp.where(encoder_side, lengths[0, 0], lengths[1, 0])
    live = jnp.arange(LEN, dtype=jnp.int32)[:, None] < own_length
    out_low = jnp.where(live & ~encoder_side, cotangent_here, jnp.zeros((), LOW))
    context_grad = (
        dot_nt(out_low[:, :half], full_left) + dot_nt(out_low[:, half:], full_right)
    ).astype(LOW)

    own_rows = dot(normed_out, full_a).astype(LOW)
    own_values = dot(normed_out, full_value).astype(LOW)
    key_rows = lax.ppermute(own_rows, "section", [(0, 1)])
    value_rows = lax.ppermute(own_values, "section", [(0, 1)])
    low_rows = shaped((tokens, width), LOW)
    value_grad, attention, kept = local(
        attend_kernel,
        (low_rows, shaped((HEADS, LEN, LEN), WIDE), shaped((3, tokens, width), LOW)),
        lengths[0].reshape(1, 1),
        own_rows,
        key_rows,
        context_grad,
        scalars=1,
        sent=(1, 2),
    )
    value_back = lax.ppermute(value_grad, "section", [(1, 0)])
    query_grad, key_grad, context = local(
        attend_back_kernel,
        (low_rows,) * 3,
        value_rows,
        attention,
        kept,
        late=(1, 2),
    )
    key_back = lax.ppermute(key_grad, "section", [(1, 0)])
    attended = jnp.concatenate([dot(context, full_left), dot(context, full_right)], axis=1)
    decoder_out = (hidden_state + attended).astype(LOW)
    forward_out = jnp.where(encoder_side, normed_out, decoder_out)
    projection_back = dot_nt(jnp.where(encoder_side, key_back, query_grad), full_a) + dot_nt(
        value_back, full_value
    )
    flags = jnp.stack([own_length, encoder_side.astype(jnp.int32)])[None]
    upstream, folded = local(
        upstream_kernel,
        (wide_rows, block),
        flags,
        hidden_state,
        projection_back,
        cotangent_here,
        facts,
        scalars=1,
        sent=(0,),
    )
    sign_grad = local(
        router_kernel,
        shaped((tokens, experts), WIDE),
        back,
        upstream,
        facts,
        scratch=(packed,),
        late=(1, 2),
    )

    def backward_term(rows, place):
        slope = dot_nt(rows[0], second_weight[:, :half]) + dot_nt(rows[1], second_weight[:, half:])
        slope = jnp.where(actives[place] > 0, slope, 0.0).astype(LOW)
        return dot_nt(slope, first_weight[:half]), dot_nt(slope, first_weight[half:])

    back = through_experts(to_holders(folded)[0], backward_term, block)
    grads = local(
        finish_kernel,
        wide_rows,
        back,
        tokens_here,
        upstream,
        sign_grad,
        router_here,
        facts,
        scratch=(packed,),
        late=(1, 2, 3, 4, 5),
    )
    return (forward_out[None], grads[None])


def solution(mesh):
    in_specs = (
        P("section", ("dp", "expert"), None),
        P("section", ("dp", "expert"), None),
        P(None, ("dp", "expert")),
        P("section", None, None),
        P("section", "expert", None, "dp"),
        P("section", "expert", "dp", None),
        P(("dp", "expert"), None),
        P(("dp", "expert"), None),
        P(("dp", "expert"), None),
        P(("dp", "expert"), None),
        P("section", ("dp", "expert"), None),
    )
    out_specs = (P("section", ("dp", "expert"), None), P("section", ("dp", "expert"), None))
    return jax.shard_map(
        per_device, mesh=mesh, in_specs=in_specs, out_specs=out_specs, check_vma=False
    )
```

```python
import functools

import jax
import jax.numpy as jnp
from jax import lax
from jax.experimental import pallas as pl
from jax.experimental.pallas import tpu as pltpu
from jax.sharding import PartitionSpec as P

HEADS = 8
HEAD = 128
TOP = 2
LEN = 128
STRIDE = 32
FOLD = 4
LANES = 128


EPS = 1e-05
NEG_FILL = -1e30
LOW = jnp.bfloat16
WIDE = jnp.float32
VMEM = pl.BlockSpec(memory_space=pltpu.VMEM)
SMEM = pl.BlockSpec(memory_space=pltpu.SMEM)
PARAMS = pltpu.CompilerParams(vmem_limit_bytes=20 * 1024 * 1024)


def dot(a, b):
    return jnp.dot(a, b, preferred_element_type=WIDE)


def dot_nt(a, b):
    return lax.dot_general(a, b, (((1,), (1,)), ((), ())), preferred_element_type=WIDE)


def dot_tn(a, b):
    return lax.dot_general(a, b, (((0,), (0,)), ((), ())), preferred_element_type=WIDE)


def normalised(values):
    centred = values - jnp.mean(values, axis=-1, keepdims=True)
    variance = jnp.mean(centred * centred, axis=-1, keepdims=True)
    inverse = lax.rsqrt(variance + EPS)
    return centred * inverse, inverse


def norm_back(values, upstream):
    normed, inverse = normalised(values)
    return inverse * (
        upstream
        - jnp.mean(upstream, axis=-1, keepdims=True)
        - normed * jnp.mean(upstream * normed, axis=-1, keepdims=True)
    )


class Late:
    def __init__(self, source, held, semaphore):
        self.copy = pltpu.make_async_copy(source, held, semaphore)
        self.held, self.shape, self.dtype, self.waiting = held, held.shape, held.dtype, True
        self.copy.start()

    def __getitem__(self, index):
        if self.waiting:
            self.copy.wait()
            self.waiting = False
        return self.held[index]


class Sent:
    def __init__(self, target, held, semaphore):
        self.copy = pltpu.make_async_copy(held, target, semaphore)
        self.held, self.shape, self.dtype = held, held.shape, held.dtype

    def __setitem__(self, index, value):
        self.held[index] = value

    def send(self):
        self.copy.start()


def laned(columns):
    lane = lax.broadcasted_iota(jnp.int32, (columns[0].shape[0], LANES), 1)
    return sum(jnp.where(lane == place, column, 0.0) for place, column in enumerate(columns))


def slot_hots(facts, experts):
    place = lax.broadcasted_iota(jnp.int32, (facts.shape[0], experts * STRIDE), 1)
    return tuple(
        jnp.where(place == (facts[:, at : at + 1] * STRIDE + facts[:, at + 1 : at + 2]).astype(jnp.int32), 1.0, 0.0)
        for at in (0, 2)
    )


def route_signs(facts, experts):
    ids = lax.broadcasted_iota(jnp.int32, (facts.shape[0], experts), 1).astype(WIDE)
    return jnp.where(facts[:, 0:1] == ids, 1.0, 0.0) - jnp.where(facts[:, 2:3] == ids, 1.0, 0.0)


def spread_rows(rows, folded_ref):
    experts, stack, columns = folded_ref.shape
    capacity = stack // FOLD
    for e in range(experts):
        block = rows[e * STRIDE : e * STRIDE + capacity].astype(LOW)
        for place in range(FOLD):
            folded_ref[e, pl.ds(place * capacity, capacity), :] = block[
                :, place * columns : (place + 1) * columns
            ]


def pack_rows(folded_ref, packed):
    experts, stack, columns = folded_ref.shape
    capacity = stack // FOLD
    packed[...] = jnp.zeros_like(packed)
    for e in range(experts):
        for place in range(FOLD):
            packed[pl.ds(e * STRIDE, capacity), pl.ds(place * columns, columns)] = folded_ref[
                e, pl.ds(place * capacity, capacity), :
            ]


def unfold_kernel(folded_ref, rows_ref, token_ref, *, begin):
    token_ref[...] = jnp.zeros_like(token_ref)
    experts, stack, columns = folded_ref.shape
    capacity = stack // FOLD
    for e in range(experts):
        for place in range(FOLD // 2):
            rows_ref[pl.ds(e * capacity, capacity), pl.ds(place * columns, columns)] = folded_ref[
                e, pl.ds((begin + place) * capacity, capacity), :
            ]


def fold_kernel(*refs):
    folded_ref = refs[-1]
    experts, stack, columns = folded_ref.shape
    capacity = stack // FOLD
    for begin in range(2):
        own_ref, side_ref, last_ref = refs[begin * 3 : begin * 3 + 3]
        total = own_ref[...] + side_ref[...].astype(WIDE) + last_ref[...].astype(WIDE)
        total = total.astype(LOW)
        for e in range(experts):
            for place in range(FOLD // 2):
                folded_ref[e, pl.ds((begin * FOLD // 2 + place) * capacity, capacity), :] = total[
                    e * capacity : (e + 1) * capacity, place * columns : (place + 1) * columns
                ]


def planes_kernel(place_ref, own_ref, behind_ref, ahead_ref, far_ref, token_ref, planes_ref):
    count = planes_ref.shape[0]
    for distance, ref in ((0, own_ref), (count - 1, behind_ref), (1, ahead_ref), (2, far_ref)):
        planes_ref[lax.rem(place_ref[0, 0] + distance, count)] = ref[...]


def dense_kernel(dense_ref, first_ref, second_ref, left_ref, right_ref):
    experts, _, double, width = dense_ref.shape
    rows = double // 2
    first_ref[...] = dense_ref[:, 0, :rows].reshape(experts * rows, width)
    second = dense_ref[:, 0, rows:]
    second_ref[...] = second.reshape(experts * rows, width)
    left_ref[...] = second[:, : rows // 2].reshape(experts * rows // 2, width)
    right_ref[...] = second[:, rows // 2 :].reshape(experts * rows // 2, width)


def dispatch_kernel(states_ref, routes_ref, router_ref, folded_ref, facts_ref):
    experts = folded_ref.shape[0]
    tokens = states_ref.shape[0]
    ids = lax.broadcasted_iota(jnp.int32, (experts, tokens), 0)
    row = lax.broadcasted_iota(jnp.int32, (experts, experts), 0)
    column = lax.broadcasted_iota(jnp.int32, (experts, experts), 1)
    same = jnp.where(row == column, 1.0, 0.0).astype(LOW)
    hots = [
        dot_tn(jnp.where(routes_ref[k : k + 1, :] == ids, 1.0, 0.0).astype(LOW), same)
        for k in range(TOP)
    ]
    row = lax.broadcasted_iota(jnp.int32, (tokens, tokens), 0)
    column = lax.broadcasted_iota(jnp.int32, (tokens, tokens), 1)
    earlier = jnp.where(column < row, 1.0, 0.0).astype(LOW)
    rank = dot(earlier, (hots[0] + hots[1]).astype(LOW))
    number = lax.broadcasted_iota(jnp.int32, (tokens, experts), 1).astype(WIDE)
    facts = []
    for hot in hots:
        facts.append(jnp.sum(hot * number, axis=1, keepdims=True))
        facts.append(jnp.sum(hot * rank, axis=1, keepdims=True))
    normed = normalised(states_ref[...].astype(WIDE))[0].astype(LOW)
    logits = dot_nt(normed, router_ref[...])
    spread = jnp.sum(hots[0] * logits - hots[1] * logits, axis=1, keepdims=True)
    facts = laned(facts + [jax.nn.sigmoid(spread)])
    facts_ref[...] = facts
    facts_ref.send()
    one, two = slot_hots(facts, experts)
    spread_rows(dot_tn((one + two).astype(LOW), normed), folded_ref)


def combine_kernel(folded_ref, states_ref, facts_ref, ready_ref, hidden_ref, normed_ref, packed):
    pack_rows(folded_ref, packed)
    rows = packed[...]
    facts = facts_ref[...]
    gate = facts[:, 4:5]
    one, two = slot_hots(facts, folded_ref.shape[0])
    hidden = states_ref[...].astype(WIDE) + (
        gate * dot(one.astype(LOW), rows) + (1.0 - gate) * dot(two.astype(LOW), rows)
    )
    hidden_ref[...] = hidden
    hidden_ref.send()
    normed_ref[...] = normalised(hidden)[0].astype(LOW)


def heads_of(ref, *lead):
    return [ref[(*lead, slice(None), slice(h * HEAD, (h + 1) * HEAD))] for h in range(HEADS)]


def attend_kernel(length_ref, q_ref, k_ref, grad_ref, v_grad_ref, attention_ref, kept_ref):
    kept_ref[0], kept_ref[1], kept_ref[2] = q_ref[...], k_ref[...], grad_ref[...]
    kept_ref.send()
    scale = HEAD ** (-0.5)
    live = lax.broadcasted_iota(jnp.int32, (HEADS * LEN, LEN), 1) < length_ref[0, 0]
    scores = [dot_nt(q, k) for q, k in zip(heads_of(q_ref), heads_of(k_ref))]
    scores = jnp.where(live, jnp.concatenate(scores, axis=0) * scale, NEG_FILL)
    exponent = jnp.exp(scores - jnp.max(scores, axis=-1, keepdims=True))
    attention = exponent / jnp.sum(exponent, axis=-1, keepdims=True)
    attention_ref[...] = attention.reshape(HEADS, LEN, LEN)
    attention_ref.send()
    attention = attention.astype(LOW)
    for head, grad in enumerate(heads_of(grad_ref)):
        at = slice(head * HEAD, (head + 1) * HEAD)
        v_grad_ref[:, at] = dot_tn(attention[head * LEN : (head + 1) * LEN], grad).astype(LOW)


def attend_back_kernel(v_ref, attention_ref, kept_ref, q_grad_ref, k_grad_ref, context_ref):
    scale = HEAD ** (-0.5)
    weight_grad = [dot_nt(grad, v) for grad, v in zip(heads_of(kept_ref, 2), heads_of(v_ref))]
    weight_grad = jnp.concatenate(weight_grad, axis=0)
    attention = attention_ref[...].reshape(HEADS * LEN, LEN)
    score_grad = (
        attention
        * (weight_grad - jnp.sum(attention * weight_grad, axis=-1, keepdims=True))
        * scale
    ).astype(LOW)
    attention = attention.astype(LOW)
    parts = zip(heads_of(kept_ref, 0), heads_of(kept_ref, 1), heads_of(v_ref))
    for head, (q, k, v) in enumerate(parts):
        at = slice(head * HEAD, (head + 1) * HEAD)
        rows = slice(head * LEN, (head + 1) * LEN)
        k_grad_ref[:, at] = dot_tn(score_grad[rows], q).astype(LOW)
        q_grad_ref[:, at] = dot(score_grad[rows], k).astype(LOW)
        context_ref[:, at] = dot(attention[rows], v).astype(LOW)


def upstream_kernel(flags_ref, hidden_ref, back_ref, cotangent_ref, facts_ref, upstream_ref, folded_ref):
    live = lax.broadcasted_iota(jnp.int32, (LEN, 1), 0) < flags_ref[0, 0]
    encoder = flags_ref[0, 1] == 1
    masked = jnp.where(live, cotangent_ref[...].astype(WIDE), 0.0)
    out_grad = jnp.where(encoder, 0.0, masked)
    normed_grad = back_ref[...] + jnp.where(encoder, masked, 0.0)
    upstream = out_grad + norm_back(hidden_ref[...], normed_grad)
    upstream_ref[...] = upstream
    upstream_ref.send()
    facts = facts_ref[...]
    gate = facts[:, 4:5]
    one, two = slot_hots(facts, folded_ref.shape[0])
    rows = dot_tn(one.astype(LOW), (gate * upstream).astype(LOW)) + dot_tn(
        two.astype(LOW), ((1.0 - gate) * upstream).astype(LOW)
    )
    spread_rows(rows, folded_ref)


def router_kernel(folded_ref, upstream_ref, facts_ref, sign_ref, packed):
    pack_rows(folded_ref, packed)
    rows = packed[...]
    facts = facts_ref[...]
    gate = facts[:, 4:5]
    one, two = slot_hots(facts, folded_ref.shape[0])
    apart = dot(one.astype(LOW), rows) - dot(two.astype(LOW), rows)
    gate_grad = jnp.sum(upstream_ref[...] * apart, axis=1, keepdims=True)
    logit_grad = gate_grad * gate * (1.0 - gate)
    sign_ref[...] = logit_grad * route_signs(facts, folded_ref.shape[0])


def finish_kernel(folded_ref, states_ref, upstream_ref, sign_ref, router_ref, facts_ref, grads_ref, packed):
    pack_rows(folded_ref, packed)
    one, two = slot_hots(facts_ref[...], folded_ref.shape[0])
    back = dot((one + two).astype(LOW), packed[...])
    router_term = jnp.dot(
        sign_ref[...],
        router_ref[...].astype(WIDE),
        precision=lax.Precision.HIGHEST,
        preferred_element_type=WIDE,
    )
    input_total = back + router_term
    grads_ref[...] = upstream_ref[...] + norm_back(states_ref[...].astype(WIDE), input_total)


def local(kernel, out_shape, *operands, scalars=0, scratch=(), late=(), sent=(), held=()):
    single = not isinstance(out_shape, tuple)
    shapes = (out_shape,) if single else out_shape
    count = len(operands)
    total = count + len(shapes)
    moved = [place for place in range(count) if place in late]
    moved += [count + place for place in range(len(shapes)) if place in sent]
    both = list(operands) + list(shapes)

    def body(*refs):
        refs, extra = list(refs[:total]), refs[total:]
        holds, semaphores = extra[: len(moved)], extra[len(moved)] if moved else None
        for number, place in enumerate(moved):
            made = Late if place < count else Sent
            refs[place] = made(refs[place], holds[number], semaphores.at[number])
        kernel(*refs, *extra[len(moved) + (1 if moved else 0) :])
        for place in moved:
            if place >= count:
                refs[place].copy.wait()

    scratches = [pltpu.VMEM(both[place].shape, both[place].dtype) for place in moved]
    if moved:
        scratches.append(pltpu.SemaphoreType.DMA((len(moved),)))
    specs = [SMEM] * scalars + [VMEM] * (total - scalars)
    for place in [*moved, *held]:
        specs[place] = pl.BlockSpec(memory_space=pltpu.HBM)
    cost = sum(x.size * x.dtype.itemsize for x in both)
    operands = [
        pltpu.with_memory_space_constraint(operand, pltpu.HBM) if place in [*late, *held] else operand
        for place, operand in enumerate(operands)
    ]
    shapes = tuple(
        pltpu.HBM(shape.shape, shape.dtype) if place in sent else shape
        for place, shape in enumerate(shapes)
    )
    result = pl.pallas_call(
        body,
        out_shape=shapes,
        in_specs=specs[:count],
        out_specs=tuple(specs[count:]),
        scratch_shapes=scratches + list(scratch),
        compiler_params=PARAMS,
        cost_estimate=pl.CostEstimate(flops=10**9, bytes_accessed=4 * cost, transcendentals=0),
    )(*operands)
    return result[0] if single else result


def shaped(shape, dtype):
    return jax.ShapeDtypeStruct(shape, dtype)


def shift(block, distance):
    count = lax.axis_size("dp")
    return lax.ppermute(block, "dp", [(i, (i + distance) % count) for i in range(count)])


def to_experts(block):
    return lax.all_to_all(block, "expert", split_axis=0, concat_axis=0, tiled=True)


def arrange(dense):
    experts, planes, double, width = dense.shape
    rows = experts * double // 2

    def blocks(count):
        return pl.BlockSpec((count, width), lambda plane: (plane, 0))

    whole, part = shaped((planes * rows, width), LOW), shaped((planes * rows // 2, width), LOW)
    return pl.pallas_call(
        dense_kernel,
        grid=(planes,),
        out_shape=(whole, whole, part, part),
        in_specs=[pl.BlockSpec((experts, 1, double, width), lambda plane: (0, plane, 0, 0))],
        out_specs=(blocks(rows), blocks(rows), blocks(rows // 2), blocks(rows // 2)),
        compiler_params=PARAMS,
        cost_estimate=pl.CostEstimate(flops=10**6, bytes_accessed=20 * 2**20, transcendentals=0),
    )(dense)


def to_holders(folded):
    experts, stack, columns = folded.shape
    rows = shaped((experts * stack // FOLD, columns * FOLD // 2), LOW)
    folded = to_experts(folded)
    token = shaped((8, LANES), WIDE)
    one, _ = local(functools.partial(unfold_kernel, begin=0), (rows, token), folded)
    two, token = local(functools.partial(unfold_kernel, begin=FOLD // 2), (rows, token), folded)
    behind_one, ahead_one = shift(one, 1), shift(one, -1)
    behind_two, ahead_two = shift(two, 1), shift(two, -1)
    far_one, far_two = shift(behind_one, 1), shift(ahead_two, -1)
    return ((one, two), (behind_one, behind_two), (ahead_one, ahead_two), (far_one, far_two)), token


def through_experts(rows, term, block):
    behind, ahead = term(rows[1], 1), term(rows[2], 2)
    sides = (behind[0].astype(LOW), ahead[1].astype(LOW))
    far, sides = lax.optimization_barrier((rows[3], sides))
    far = term(far, 3)
    step_one, step_two = shift(far[0].astype(LOW), 1), shift(far[1].astype(LOW), -1)
    step_one, step_two, sides, own = lax.optimization_barrier((step_one, step_two, sides, rows[0]))
    side_one, side_two = shift(sides[0], -1), shift(sides[1], 1)
    last_one = shift((ahead[0] + step_one.astype(WIDE)).astype(LOW), 1)
    last_two = shift((behind[1] + step_two.astype(WIDE)).astype(LOW), -1)
    own = term(own, 0)
    folded = local(fold_kernel, block, own[0], side_one, last_one, own[1], side_two, last_two)
    return to_experts(folded)


def per_device(
    states, routes, lengths, router, w_in, w_out, w_query, w_key, w_value, w_output, cotangent
):
    section = lax.axis_index("section")
    encoder_side = section == 0
    tokens_here = states[0]
    routes_here = routes[0]
    router_here = router[0].T
    routes_here = routes_here.T
    first_weight = w_in[0, 0]
    second_weight = w_out[0, 0]
    cotangent_here = cotangent[0]
    tokens, columns = tokens_here.shape
    experts = router_here.shape[0]
    capacity = max(2, 5 * TOP * tokens // (4 * experts))
    half = columns // 2
    width = HEADS * HEAD
    slot_count = experts * STRIDE
    block = shaped((experts, FOLD * capacity, columns // FOLD), LOW)
    packed = pltpu.VMEM((slot_count, columns), LOW)

    facts_shape, wide_rows = shaped((tokens, LANES), WIDE), shaped((tokens, columns), WIDE)
    folded, facts = local(
        dispatch_kernel,
        (block, facts_shape),
        tokens_here,
        routes_here,
        router_here,
        late=(0, 2),
        sent=(1,),
    )
    folded, w_query, w_key, w_value, w_output = lax.optimization_barrier(
        (folded, w_query, w_key, w_value, w_output)
    )
    own_a = jnp.where(encoder_side, w_key, w_query)
    output_wide = jnp.concatenate([w_output[:, :width], w_output[:, width:]], axis=0)
    own_b = jnp.where(encoder_side, w_value, output_wide)
    dense = jnp.concatenate([own_a, own_b], axis=0)
    others = shift(dense, 1), shift(dense, -1), shift(dense, 2)
    blocks, token = to_holders(folded)
    dense = local(
        planes_kernel,
        shaped((lax.axis_size("dp"),) + dense.shape, LOW),
        lax.axis_index("dp").reshape(1, 1),
        dense,
        *others,
        token,
        scalars=1,
    )
    dense = lax.all_gather(dense, "expert", axis=0, tiled=True)
    dense = dense.reshape(lax.axis_size("expert"), lax.axis_size("dp"), -1, width)

    actives = [None] * 4

    def forward_term(rows, place):
        pre = dot(rows[0], first_weight[:half]) + dot(rows[1], first_weight[half:])
        active = jnp.maximum(pre, 0.0).astype(LOW)
        actives[place] = active
        return dot(active, second_weight[:, :half]), dot(active, second_weight[:, half:])

    back = through_experts(blocks, forward_term, block)
    full_a, full_value, full_left, full_right = arrange(dense)

    hidden_state, normed_out = local(
        combine_kernel,
        (wide_rows, shaped((tokens, columns), LOW)),
        back,
        tokens_here,
        facts,
        full_a,
        scratch=(packed,),
        late=(1, 2),
        held=(3,),
        sent=(0,),
    )
    own_length = jnp.where(encoder_side, lengths[0, 0], lengths[1, 0])
    live = jnp.arange(LEN, dtype=jnp.int32)[:, None] < own_length
    out_low = jnp.where(live & ~encoder_side, cotangent_here, jnp.zeros((), LOW))
    context_grad = (
        dot_nt(out_low[:, :half], full_left) + dot_nt(out_low[:, half:], full_right)
    ).astype(LOW)

    own_rows = dot(normed_out, full_a).astype(LOW)
    own_values = dot(normed_out, full_value).astype(LOW)
    key_rows = lax.ppermute(own_rows, "section", [(0, 1)])
    value_rows = lax.ppermute(own_values, "section", [(0, 1)])
    low_rows = shaped((tokens, width), LOW)
    value_grad, attention, kept = local(
        attend_kernel,
        (low_rows, shaped((HEADS, LEN, LEN), WIDE), shaped((3, tokens, width), LOW)),
        lengths[0].reshape(1, 1),
        own_rows,
        key_rows,
        context_grad,
        scalars=1,
        sent=(1, 2),
    )
    value_back = lax.ppermute(value_grad, "section", [(1, 0)])
    query_grad, key_grad, context = local(
        attend_back_kernel,
        (low_rows,) * 3,
        value_rows,
        attention,
        kept,
        late=(1, 2),
    )
    key_back = lax.ppermute(key_grad, "section", [(1, 0)])
    attended = jnp.concatenate([dot(context, full_left), dot(context, full_right)], axis=1)
    decoder_out = (hidden_state + attended).astype(LOW)
    forward_out = jnp.where(encoder_side, normed_out, decoder_out)
    projection_back = dot_nt(jnp.where(encoder_side, key_back, query_grad), full_a) + dot_nt(
        value_back, full_value
    )
    flags = jnp.stack([own_length, encoder_side.astype(jnp.int32)])[None]
    upstream, folded = local(
        upstream_kernel,
        (wide_rows, block),
        flags,
        hidden_state,
        projection_back,
        cotangent_here,
        facts,
        scalars=1,
        sent=(0,),
    )
    sign_grad = local(
        router_kernel,
        shaped((tokens, experts), WIDE),
        back,
        upstream,
        facts,
        scratch=(packed,),
        late=(1, 2),
    )

    def backward_term(rows, place):
        slope = dot_nt(rows[0], second_weight[:, :half]) + dot_nt(rows[1], second_weight[:, half:])
        slope = jnp.where(actives[place] > 0, slope, 0.0).astype(LOW)
        return dot_nt(slope, first_weight[:half]), dot_nt(slope, first_weight[half:])

    back = through_experts(to_holders(folded)[0], backward_term, block)
    grads = local(
        finish_kernel,
        wide_rows,
        back,
        tokens_here,
        upstream,
        sign_grad,
        router_here,
        facts,
        scratch=(packed,),
        late=(1, 2, 3, 4, 5),
    )
    return (forward_out[None], grads[None])


def solution(mesh):
    in_specs = (
        P("section", ("dp", "expert"), None),
        P("section", ("dp", "expert"), None),
        P(None, ("dp", "expert")),
        P("section", None, None),
        P("section", "expert", None, "dp"),
        P("section", "expert", "dp", None),
        P(("dp", "expert"), None),
        P(("dp", "expert"), None),
        P(("dp", "expert"), None),
        P(("dp", "expert"), None),
        P("section", ("dp", "expert"), None),
    )
    out_specs = (P("section", ("dp", "expert"), None), P("section", ("dp", "expert"), None))
    return jax.shard_map(
        per_device, mesh=mesh, in_specs=in_specs, out_specs=out_specs, check_vma=False
    )
```

```python
import functools

import jax
import jax.numpy as jnp
from jax import lax
from jax.experimental import pallas as pl
from jax.experimental.pallas import tpu as pltpu
from jax.sharding import PartitionSpec as P

HEADS = 8
HEAD = 128
TOP = 2
LEN = 128
STRIDE = 32
FOLD = 4
LANES = 128


EPS = 1e-05
NEG_FILL = -1e30
LOW = jnp.bfloat16
WIDE = jnp.float32
VMEM = pl.BlockSpec(memory_space=pltpu.VMEM)
SMEM = pl.BlockSpec(memory_space=pltpu.SMEM)
PARAMS = pltpu.CompilerParams(vmem_limit_bytes=20 * 1024 * 1024)


def dot(a, b):
    return jnp.dot(a, b, preferred_element_type=WIDE)


def dot_nt(a, b):
    return lax.dot_general(a, b, (((1,), (1,)), ((), ())), preferred_element_type=WIDE)


def dot_tn(a, b):
    return lax.dot_general(a, b, (((0,), (0,)), ((), ())), preferred_element_type=WIDE)


def normalised(values):
    centred = values - jnp.mean(values, axis=-1, keepdims=True)
    variance = jnp.mean(centred * centred, axis=-1, keepdims=True)
    inverse = lax.rsqrt(variance + EPS)
    return centred * inverse, inverse


def norm_back(values, upstream):
    normed, inverse = normalised(values)
    return inverse * (
        upstream
        - jnp.mean(upstream, axis=-1, keepdims=True)
        - normed * jnp.mean(upstream * normed, axis=-1, keepdims=True)
    )


class Late:
    def __init__(self, source, held, semaphore):
        self.copy = pltpu.make_async_copy(source, held, semaphore)
        self.held, self.shape, self.dtype, self.waiting = held, held.shape, held.dtype, True
        self.copy.start()

    def __getitem__(self, index):
        if self.waiting:
            self.copy.wait()
            self.waiting = False
        return self.held[index]


class Sent:
    def __init__(self, target, held, semaphore):
        self.copy = pltpu.make_async_copy(held, target, semaphore)
        self.held, self.shape, self.dtype = held, held.shape, held.dtype

    def __setitem__(self, index, value):
        self.held[index] = value

    def send(self):
        self.copy.start()


def laned(columns):
    lane = lax.broadcasted_iota(jnp.int32, (columns[0].shape[0], LANES), 1)
    return sum(jnp.where(lane == place, column, 0.0) for place, column in enumerate(columns))


def slot_hots(facts, experts):
    place = lax.broadcasted_iota(jnp.int32, (facts.shape[0], experts * STRIDE), 1)
    return tuple(
        jnp.where(place == (facts[:, at : at + 1] * STRIDE + facts[:, at + 1 : at + 2]).astype(jnp.int32), 1.0, 0.0)
        for at in (0, 2)
    )


def route_signs(facts, experts):
    ids = lax.broadcasted_iota(jnp.int32, (facts.shape[0], experts), 1).astype(WIDE)
    return jnp.where(facts[:, 0:1] == ids, 1.0, 0.0) - jnp.where(facts[:, 2:3] == ids, 1.0, 0.0)


def spread_rows(rows, folded_ref):
    experts, stack, columns = folded_ref.shape
    capacity = stack // FOLD
    for e in range(experts):
        block = rows[e * STRIDE : e * STRIDE + capacity].astype(LOW)
        for place in range(FOLD):
            folded_ref[e, pl.ds(place * capacity, capacity), :] = block[
                :, place * columns : (place + 1) * columns
            ]


def pack_rows(folded_ref, packed):
    experts, stack, columns = folded_ref.shape
    capacity = stack // FOLD
    packed[...] = jnp.zeros_like(packed)
    for e in range(experts):
        for place in range(FOLD):
            packed[pl.ds(e * STRIDE, capacity), pl.ds(place * columns, columns)] = folded_ref[
                e, pl.ds(place * capacity, capacity), :
            ]


def unfold_kernel(folded_ref, rows_ref, token_ref, *, begin):
    token_ref[...] = jnp.zeros_like(token_ref)
    experts, stack, columns = folded_ref.shape
    capacity = stack // FOLD
    for e in range(experts):
        for place in range(FOLD // 2):
            rows_ref[pl.ds(e * capacity, capacity), pl.ds(place * columns, columns)] = folded_ref[
                e, pl.ds((begin + place) * capacity, capacity), :
            ]


def fold_kernel(*refs):
    folded_ref = refs[-1]
    experts, stack, columns = folded_ref.shape
    capacity = stack // FOLD
    for begin in range(2):
        own_ref, side_ref, last_ref = refs[begin * 3 : begin * 3 + 3]
        total = own_ref[...] + side_ref[...].astype(WIDE) + last_ref[...].astype(WIDE)
        total = total.astype(LOW)
        for e in range(experts):
            for place in range(FOLD // 2):
                folded_ref[e, pl.ds((begin * FOLD // 2 + place) * capacity, capacity), :] = total[
                    e * capacity : (e + 1) * capacity, place * columns : (place + 1) * columns
                ]


def planes_kernel(place_ref, own_ref, behind_ref, ahead_ref, far_ref, token_ref, planes_ref):
    count = planes_ref.shape[0]
    for distance, ref in ((0, own_ref), (count - 1, behind_ref), (1, ahead_ref), (2, far_ref)):
        planes_ref[lax.rem(place_ref[0, 0] + distance, count)] = ref[...]


def dense_kernel(dense_ref, first_ref, second_ref, left_ref, right_ref):
    experts, _, double, width = dense_ref.shape
    rows = double // 2
    first_ref[...] = dense_ref[:, 0, :rows].reshape(experts * rows, width)
    second = dense_ref[:, 0, rows:]
    second_ref[...] = second.reshape(experts * rows, width)
    left_ref[...] = second[:, : rows // 2].reshape(experts * rows // 2, width)
    right_ref[...] = second[:, rows // 2 :].reshape(experts * rows // 2, width)


def dispatch_kernel(states_ref, routes_ref, router_ref, folded_ref, facts_ref):
    experts = folded_ref.shape[0]
    tokens = states_ref.shape[0]
    ids = lax.broadcasted_iota(jnp.int32, (experts, tokens), 0)
    row = lax.broadcasted_iota(jnp.int32, (experts, experts), 0)
    column = lax.broadcasted_iota(jnp.int32, (experts, experts), 1)
    same = jnp.where(row == column, 1.0, 0.0).astype(LOW)
    hots = [
        dot_tn(jnp.where(routes_ref[k : k + 1, :] == ids, 1.0, 0.0).astype(LOW), same)
        for k in range(TOP)
    ]
    row = lax.broadcasted_iota(jnp.int32, (tokens, tokens), 0)
    column = lax.broadcasted_iota(jnp.int32, (tokens, tokens), 1)
    earlier = jnp.where(column < row, 1.0, 0.0).astype(LOW)
    rank = dot(earlier, (hots[0] + hots[1]).astype(LOW))
    number = lax.broadcasted_iota(jnp.int32, (tokens, experts), 1).astype(WIDE)
    facts = []
    for hot in hots:
        facts.append(jnp.sum(hot * number, axis=1, keepdims=True))
        facts.append(jnp.sum(hot * rank, axis=1, keepdims=True))
    normed = normalised(states_ref[...].astype(WIDE))[0].astype(LOW)
    logits = dot_nt(normed, router_ref[...])
    spread = jnp.sum(hots[0] * logits - hots[1] * logits, axis=1, keepdims=True)
    facts = laned(facts + [jax.nn.sigmoid(spread)])
    facts_ref[...] = facts
    facts_ref.send()
    one, two = slot_hots(facts, experts)
    spread_rows(dot_tn((one + two).astype(LOW), normed), folded_ref)


def combine_kernel(folded_ref, states_ref, facts_ref, ready_ref, hidden_ref, normed_ref, packed):
    pack_rows(folded_ref, packed)
    rows = packed[...]
    facts = facts_ref[...]
    gate = facts[:, 4:5]
    one, two = slot_hots(facts, folded_ref.shape[0])
    hidden = states_ref[...].astype(WIDE) + (
        gate * dot(one.astype(LOW), rows) + (1.0 - gate) * dot(two.astype(LOW), rows)
    )
    hidden_ref[...] = hidden
    hidden_ref.send()
    normed_ref[...] = normalised(hidden)[0].astype(LOW)


def heads_of(ref, *lead):
    return [ref[(*lead, slice(None), slice(h * HEAD, (h + 1) * HEAD))] for h in range(HEADS)]


def attend_kernel(length_ref, q_ref, k_ref, grad_ref, v_grad_ref, attention_ref, kept_ref):
    kept_ref[0], kept_ref[1], kept_ref[2] = q_ref[...], k_ref[...], grad_ref[...]
    kept_ref.send()
    scale = HEAD ** (-0.5)
    live = lax.broadcasted_iota(jnp.int32, (HEADS * LEN, LEN), 1) < length_ref[0, 0]
    scores = [dot_nt(q, k) for q, k in zip(heads_of(q_ref), heads_of(k_ref))]
    scores = jnp.where(live, jnp.concatenate(scores, axis=0) * scale, NEG_FILL)
    exponent = jnp.exp(scores - jnp.max(scores, axis=-1, keepdims=True))
    attention = exponent / jnp.sum(exponent, axis=-1, keepdims=True)
    attention_ref[...] = attention.reshape(HEADS, LEN, LEN)
    attention_ref.send()
    attention = attention.astype(LOW)
    for head, grad in enumerate(heads_of(grad_ref)):
        at = slice(head * HEAD, (head + 1) * HEAD)
        v_grad_ref[:, at] = dot_tn(attention[head * LEN : (head + 1) * LEN], grad).astype(LOW)


def attend_back_kernel(v_ref, attention_ref, kept_ref, q_grad_ref, k_grad_ref, context_ref):
    scale = HEAD ** (-0.5)
    weight_grad = [dot_nt(grad, v) for grad, v in zip(heads_of(kept_ref, 2), heads_of(v_ref))]
    weight_grad = jnp.concatenate(weight_grad, axis=0)
    attention = attention_ref[...].reshape(HEADS * LEN, LEN)
    score_grad = (
        attention
        * (weight_grad - jnp.sum(attention * weight_grad, axis=-1, keepdims=True))
        * scale
    ).astype(LOW)
    attention = attention.astype(LOW)
    parts = zip(heads_of(kept_ref, 0), heads_of(kept_ref, 1), heads_of(v_ref))
    for head, (q, k, v) in enumerate(parts):
        at = slice(head * HEAD, (head + 1) * HEAD)
        rows = slice(head * LEN, (head + 1) * LEN)
        k_grad_ref[:, at] = dot_tn(score_grad[rows], q).astype(LOW)
        q_grad_ref[:, at] = dot(score_grad[rows], k).astype(LOW)
        context_ref[:, at] = dot(attention[rows], v).astype(LOW)


def upstream_kernel(flags_ref, hidden_ref, back_ref, cotangent_ref, facts_ref, upstream_ref, folded_ref):
    live = lax.broadcasted_iota(jnp.int32, (LEN, 1), 0) < flags_ref[0, 0]
    encoder = flags_ref[0, 1] == 1
    masked = jnp.where(live, cotangent_ref[...].astype(WIDE), 0.0)
    out_grad = jnp.where(encoder, 0.0, masked)
    normed_grad = back_ref[...] + jnp.where(encoder, masked, 0.0)
    upstream = out_grad + norm_back(hidden_ref[...], normed_grad)
    upstream_ref[...] = upstream
    upstream_ref.send()
    facts = facts_ref[...]
    gate = facts[:, 4:5]
    one, two = slot_hots(facts, folded_ref.shape[0])
    rows = dot_tn(one.astype(LOW), (gate * upstream).astype(LOW)) + dot_tn(
        two.astype(LOW), ((1.0 - gate) * upstream).astype(LOW)
    )
    spread_rows(rows, folded_ref)


def router_kernel(folded_ref, upstream_ref, facts_ref, sign_ref, packed):
    pack_rows(folded_ref, packed)
    rows = packed[...]
    facts = facts_ref[...]
    gate = facts[:, 4:5]
    one, two = slot_hots(facts, folded_ref.shape[0])
    apart = dot(one.astype(LOW), rows) - dot(two.astype(LOW), rows)
    gate_grad = jnp.sum(upstream_ref[...] * apart, axis=1, keepdims=True)
    logit_grad = gate_grad * gate * (1.0 - gate)
    sign_ref[...] = logit_grad * route_signs(facts, folded_ref.shape[0])


def finish_kernel(folded_ref, states_ref, upstream_ref, sign_ref, router_ref, facts_ref, grads_ref, packed):
    pack_rows(folded_ref, packed)
    one, two = slot_hots(facts_ref[...], folded_ref.shape[0])
    back = dot((one + two).astype(LOW), packed[...])
    router_term = jnp.dot(
        sign_ref[...],
        router_ref[...].astype(WIDE),
        precision=lax.Precision.HIGHEST,
        preferred_element_type=WIDE,
    )
    input_total = back + router_term
    grads_ref[...] = upstream_ref[...] + norm_back(states_ref[...].astype(WIDE), input_total)


def local(kernel, out_shape, *operands, scalars=0, scratch=(), late=(), sent=(), held=()):
    single = not isinstance(out_shape, tuple)
    shapes = (out_shape,) if single else out_shape
    count = len(operands)
    total = count + len(shapes)
    moved = [place for place in range(count) if place in late]
    moved += [count + place for place in range(len(shapes)) if place in sent]
    both = list(operands) + list(shapes)

    def body(*refs):
        refs, extra = list(refs[:total]), refs[total:]
        holds, semaphores = extra[: len(moved)], extra[len(moved)] if moved else None
        for number, place in enumerate(moved):
            made = Late if place < count else Sent
            refs[place] = made(refs[place], holds[number], semaphores.at[number])
        kernel(*refs, *extra[len(moved) + (1 if moved else 0) :])
        for place in moved:
            if place >= count:
                refs[place].copy.wait()

    scratches = [pltpu.VMEM(both[place].shape, both[place].dtype) for place in moved]
    if moved:
        scratches.append(pltpu.SemaphoreType.DMA((len(moved),)))
    specs = [SMEM] * scalars + [VMEM] * (total - scalars)
    for place in [*moved, *held]:
        specs[place] = pl.BlockSpec(memory_space=pltpu.HBM)
    cost = sum(x.size * x.dtype.itemsize for x in both)
    operands = [
        pltpu.with_memory_space_constraint(operand, pltpu.HBM) if place in [*late, *held] else operand
        for place, operand in enumerate(operands)
    ]
    shapes = tuple(
        pltpu.HBM(shape.shape, shape.dtype) if place in sent else shape
        for place, shape in enumerate(shapes)
    )
    result = pl.pallas_call(
        body,
        out_shape=shapes,
        in_specs=specs[:count],
        out_specs=tuple(specs[count:]),
        scratch_shapes=scratches + list(scratch),
        compiler_params=PARAMS,
        cost_estimate=pl.CostEstimate(flops=10**9, bytes_accessed=4 * cost, transcendentals=0),
    )(*operands)
    return result[0] if single else result


def shaped(shape, dtype):
    return jax.ShapeDtypeStruct(shape, dtype)


def shift(block, distance):
    count = lax.axis_size("dp")
    return lax.ppermute(block, "dp", [(i, (i + distance) % count) for i in range(count)])


def to_experts(block):
    return lax.all_to_all(block, "expert", split_axis=0, concat_axis=0, tiled=True)


def arrange(dense):
    experts, planes, double, width = dense.shape
    rows = experts * double // 2

    def blocks(count):
        return pl.BlockSpec((count, width), lambda plane: (plane, 0))

    whole, part = shaped((planes * rows, width), LOW), shaped((planes * rows // 2, width), LOW)
    return pl.pallas_call(
        dense_kernel,
        grid=(planes,),
        out_shape=(whole, whole, part, part),
        in_specs=[pl.BlockSpec((experts, 1, double, width), lambda plane: (0, plane, 0, 0))],
        out_specs=(blocks(rows), blocks(rows), blocks(rows // 2), blocks(rows // 2)),
        compiler_params=PARAMS,
        cost_estimate=pl.CostEstimate(flops=10**6, bytes_accessed=20 * 2**20, transcendentals=0),
    )(dense)


def to_holders(folded):
    experts, stack, columns = folded.shape
    rows = shaped((experts * stack // FOLD, columns * FOLD // 2), LOW)
    folded = to_experts(folded)
    token = shaped((8, LANES), WIDE)
    one, token = local(functools.partial(unfold_kernel, begin=0), (rows, token), folded)
    two, _ = local(functools.partial(unfold_kernel, begin=FOLD // 2), (rows, token), folded)
    behind_one, ahead_one = shift(one, 1), shift(one, -1)
    behind_two, ahead_two = shift(two, 1), shift(two, -1)
    far_one, far_two = shift(behind_one, 1), shift(ahead_two, -1)
    return ((one, two), (behind_one, behind_two), (ahead_one, ahead_two), (far_one, far_two)), token


def expert_terms(blocks, term):
    terms = [term(block, place) for place, block in enumerate(blocks[:3])]
    sides = (terms[1][0].astype(LOW), terms[2][1].astype(LOW))
    far, sides = lax.optimization_barrier((blocks[3], sides))
    return terms + [term(far, 3), sides]


def to_tokens(own, behind, ahead, far, sides, block):
    step_one, step_two = shift(far[0].astype(LOW), 1), shift(far[1].astype(LOW), -1)
    side_one, side_two = shift(sides[0], -1), shift(sides[1], 1)
    last_one = shift((ahead[0] + step_one.astype(WIDE)).astype(LOW), 1)
    last_two = shift((behind[1] + step_two.astype(WIDE)).astype(LOW), -1)
    folded = local(fold_kernel, block, own[0], side_one, last_one, own[1], side_two, last_two)
    return to_experts(folded)


def per_device(
    states, routes, lengths, router, w_in, w_out, w_query, w_key, w_value, w_output, cotangent
):
    section = lax.axis_index("section")
    encoder_side = section == 0
    tokens_here = states[0]
    routes_here = routes[0]
    router_here = router[0].T
    routes_here = routes_here.T
    first_weight = w_in[0, 0]
    second_weight = w_out[0, 0]
    cotangent_here = cotangent[0]
    tokens, columns = tokens_here.shape
    experts = router_here.shape[0]
    capacity = max(2, 5 * TOP * tokens // (4 * experts))
    half = columns // 2
    width = HEADS * HEAD
    slot_count = experts * STRIDE
    block = shaped((experts, FOLD * capacity, columns // FOLD), LOW)
    packed = pltpu.VMEM((slot_count, columns), LOW)

    facts_shape, wide_rows = shaped((tokens, LANES), WIDE), shaped((tokens, columns), WIDE)
    folded, facts = local(
        dispatch_kernel,
        (block, facts_shape),
        tokens_here,
        routes_here,
        router_here,
        late=(0, 2),
        sent=(1,),
    )
    folded, w_query, w_key, w_value, w_output = lax.optimization_barrier(
        (folded, w_query, w_key, w_value, w_output)
    )
    own_a = jnp.where(encoder_side, w_key, w_query)
    output_wide = jnp.concatenate([w_output[:, :width], w_output[:, width:]], axis=0)
    own_b = jnp.where(encoder_side, w_value, output_wide)
    dense = jnp.concatenate([own_a, own_b], axis=0)
    others = shift(dense, 1), shift(dense, -1), shift(dense, 2)
    blocks, token = to_holders(folded)
    dense = local(
        planes_kernel,
        shaped((lax.axis_size("dp"),) + dense.shape, LOW),
        lax.axis_index("dp").reshape(1, 1),
        dense,
        *others,
        token,
        scalars=1,
    )
    dense = lax.all_gather(dense, "expert", axis=0, tiled=True)
    dense = dense.reshape(lax.axis_size("expert"), lax.axis_size("dp"), -1, width)

    actives = []

    def forward_term(rows, place):
        pre = dot(rows[0], first_weight[:half]) + dot(rows[1], first_weight[half:])
        active = jnp.maximum(pre, 0.0).astype(LOW)
        actives.append(active)
        return dot(active, second_weight[:, :half]), dot(active, second_weight[:, half:])

    terms = expert_terms(blocks, forward_term)
    back = to_tokens(*terms, block)
    full_a, full_value, full_left, full_right = arrange(dense)

    hidden_state, normed_out = local(
        combine_kernel,
        (wide_rows, shaped((tokens, columns), LOW)),
        back,
        tokens_here,
        facts,
        full_a,
        scratch=(packed,),
        late=(1, 2),
        held=(3,),
        sent=(0,),
    )
    own_length = jnp.where(encoder_side, lengths[0, 0], lengths[1, 0])
    live = jnp.arange(LEN, dtype=jnp.int32)[:, None] < own_length
    out_low = jnp.where(live & ~encoder_side, cotangent_here, jnp.zeros((), LOW))
    context_grad = (
        dot_nt(out_low[:, :half], full_left) + dot_nt(out_low[:, half:], full_right)
    ).astype(LOW)

    own_rows = dot(normed_out, full_a).astype(LOW)
    own_values = dot(normed_out, full_value).astype(LOW)
    key_rows = lax.ppermute(own_rows, "section", [(0, 1)])
    value_rows = lax.ppermute(own_values, "section", [(0, 1)])
    low_rows = shaped((tokens, width), LOW)
    value_grad, attention, kept = local(
        attend_kernel,
        (low_rows, shaped((HEADS, LEN, LEN), WIDE), shaped((3, tokens, width), LOW)),
        lengths[0].reshape(1, 1),
        own_rows,
        key_rows,
        context_grad,
        scalars=1,
        sent=(1, 2),
    )
    value_back = lax.ppermute(value_grad, "section", [(1, 0)])
    query_grad, key_grad, context = local(
        attend_back_kernel,
        (low_rows,) * 3,
        value_rows,
        attention,
        kept,
        late=(1, 2),
    )
    key_back = lax.ppermute(key_grad, "section", [(1, 0)])
    attended = jnp.concatenate([dot(context, full_left), dot(context, full_right)], axis=1)
    decoder_out = (hidden_state + attended).astype(LOW)
    forward_out = jnp.where(encoder_side, normed_out, decoder_out)
    projection_back = dot_nt(jnp.where(encoder_side, key_back, query_grad), full_a) + dot_nt(
        value_back, full_value
    )
    flags = jnp.stack([own_length, encoder_side.astype(jnp.int32)])[None]
    upstream, folded = local(
        upstream_kernel,
        (wide_rows, block),
        flags,
        hidden_state,
        projection_back,
        cotangent_here,
        facts,
        scalars=1,
        sent=(0,),
    )
    sign_grad = local(
        router_kernel,
        shaped((tokens, experts), WIDE),
        back,
        upstream,
        facts,
        scratch=(packed,),
        late=(1, 2),
    )

    def backward_term(rows, place):
        slope = dot_nt(rows[0], second_weight[:, :half]) + dot_nt(rows[1], second_weight[:, half:])
        slope = jnp.where(actives[place] > 0, slope, 0.0).astype(LOW)
        return dot_nt(slope, first_weight[:half]), dot_nt(slope, first_weight[half:])

    terms = expert_terms(to_holders(folded)[0], backward_term)
    back = to_tokens(*terms, block)
    grads = local(
        finish_kernel,
        wide_rows,
        back,
        tokens_here,
        upstream,
        sign_grad,
        router_here,
        facts,
        scratch=(packed,),
        late=(1, 2, 3, 4, 5),
    )
    return (forward_out[None], grads[None])


def solution(mesh):
    in_specs = (
        P("section", ("dp", "expert"), None),
        P("section", ("dp", "expert"), None),
        P(None, ("dp", "expert")),
        P("section", None, None),
        P("section", "expert", None, "dp"),
        P("section", "expert", "dp", None),
        P(("dp", "expert"), None),
        P(("dp", "expert"), None),
        P(("dp", "expert"), None),
        P(("dp", "expert"), None),
        P("section", ("dp", "expert"), None),
    )
    out_specs = (P("section", ("dp", "expert"), None), P("section", ("dp", "expert"), None))
    return jax.shard_map(
        per_device, mesh=mesh, in_specs=in_specs, out_specs=out_specs, check_vma=False
    )
```
